128 devices in a mesh: gx: 8 (over x, core), gy: 16 (over z, y).
Axes of the slice: x: 4, y: 4, z: 4, core: 2. Of those that a mesh axis runs over, the one named last changes fastest.
Arguments:
- flow: float32 [5, 128, 512, 128], P(None, 'gx', 'gy'), may hold values from -6 to 6
- near: float32 [5, 16384], P(None, ('gx', 'gy')), may hold values from -6 to 6
- donor_owner: int32 [16384, 1], P(('gx', 'gy')), may hold values from 0 to 127; in each aligned block of 128 rows (0 to 127, 128 to 255, ...) at most 2 rows name the same one
- donor_block: int32 [16384], P(('gx', 'gy')), may hold values from 0 to 127
- recv_offset: int32 [16384], P(('gx', 'gy')), may hold values from 0 to 511
- weights: float32 [3, 8, 16384], P(None, None, ('gx', 'gy')), may hold values from -3 to 3
Outputs:
- flow_out: float32 [5, 128, 512, 128], P(None, 'gx', 'gy')
- near_out: float32 [5, 16384], P(None, ('gx', 'gy'))
The draws below stay inside these ranges and needn't reach their ends.
Inputs may be any that keep to these rules, and one draw needn't show every extreme that they name: `donor_owner`: within the fringe points of one device, no owner is named more than 2 times, a bound that some block reaches.
All inputs are finite; a program needn't handle non-finite values.
Results may differ from the reference program's by a relative error of at most 0.0003.
Values sent between devices are 32-bit elements; how exact they have to be, the bound alone decides.
A program may use at most 128 MiB of HBM per device.

```python
import math
import jax
import jax.numpy as jnp
import numpy as np
from jax import lax

NV = 5
CX = 16
CY = 32
CZ = 128
FR_DEV = 128
STEPS = 2
NX = 128
NY = 512
NZ = 128
BLK_DEV = 128
CAP = 2
FRINGES = 16384
N_GY = 16
DEVICES = 128


def plant(values, own_key, low, top_value):
    index_at = [jax.random.randint(jax.random.fold_in(own_key, axis), (), 0, length) for axis, length in enumerate(values.shape)]
    main_axis = values.shape.index(max(values.shape))
    beside = index_at[:main_axis] + [(index_at[main_axis] + 1) % values.shape[main_axis]] + index_at[main_axis + 1:]
    return values.at[tuple(index_at)].set(low).at[tuple(beside)].set(top_value)


def block_scale(key, shape, split, smallest, largest):
    gain = 1.0
    for axis_at, shards_of in split:
        heights = jax.random.uniform(jax.random.fold_in(jax.random.fold_in(key, 6), axis_at), (shards_of,), jnp.float32, smallest / len(split), largest / len(split))
        gain = gain * jnp.repeat(jnp.exp(heights), shape[axis_at] // shards_of).reshape((-1,) + (1,) * (len(shape) - 1 - axis_at))
    return gain


def deal_out(own_key, own, number, rows, count, top, reach, lean):
    order = jax.random.permutation(own_key, count)
    crowded, common = load_shares(count, rows * top, reach, lean, True), load_shares(count, rows * top, reach, lean, False)
    places = jnp.arange(count)

    def named(sizes, turn):
        used = int((sizes > 0).sum())
        fixed = max(1, used // 4)
        shifted = fixed + (places - fixed + turn * (used - fixed)) % max(1, count - fixed)
        return jnp.zeros((count,), jnp.int32).at[order[jnp.where(places < fixed, places, shifted)]].set(jnp.asarray(sizes, jnp.int32))

    sizes = jnp.where(number % 4 == 0, named(crowded, number // 4), named(common, number - number // 4 - 1))
    mixed = jax.random.permutation(jax.random.fold_in(own, 3), count)
    donor, taker = mixed[0:count // 2 * 2:2], mixed[1:count // 2 * 2:2]
    slack = jnp.minimum(sizes[donor] - 1, reach - sizes[taker]) // 2
    slack = jnp.where((donor == order[0]) | (taker == order[0]) | (sizes[taker] == 0), 0, jnp.maximum(slack, 0))
    shifted = jax.random.randint(jax.random.fold_in(own, 4), (count // 2,), 0, 1 << 20) % (slack + 1)
    sizes = sizes.at[donor].add(-shifted).at[taker].add(shifted)
    labels = jnp.searchsorted(jnp.cumsum(sizes), jnp.arange(rows * top), side="right").astype(jnp.int32)
    grid = labels.reshape(top, rows).T
    grid = grid[jax.random.permutation(jax.random.fold_in(own, 1), rows)]
    turn = jax.random.randint(jax.random.fold_in(own, 2), (rows, 1), 0, top)
    return jnp.take_along_axis(grid, (jnp.arange(top)[None, :] + turn) % top, axis=1)


def load_shares(number_of, total, bound, slope, full):
    weights = [(1 << 20) // math.isqrt(rank ** slope) + 1 for rank in range(1, number_of + 1)]
    largest = bound if full else min(bound, max(-(-total // number_of), total * weights[0] // sum(weights)))
    least = 1 if total - largest >= number_of - 1 else 0
    given, rest = [largest] + [least] * (number_of - 1), total - largest - least * (number_of - 1)
    while rest > 0:
        movable = [i for i in range(1, number_of) if given[i] < largest] or [i for i in range(1, number_of) if given[i] < bound]
        mass, left = sum([weights[i] for i in movable]), rest
        for i in movable:
            more = min(bound - given[i], max(1, left * weights[i] // mass), rest)
            given[i] = given[i] + more
            rest = rest - more
    return np.array(given)


def bell_draw(key, shape, scale, reach, cuts=(), kind=jnp.bfloat16):
    loudness = block_scale(key, shape, cuts, -0.22, 0.18) if cuts else 1.0
    entries = jax.random.normal(key, shape, jnp.float32) * scale * loudness
    return jnp.minimum(jnp.maximum(entries, -reach), reach).astype(kind)


def setup_inputs(seed: int = 0) -> dict:
    seeds = jax.random.split(jax.random.key(seed), 7)
    flow = bell_draw(seeds[0], (NV, NX, NY, NZ), 1.0, 6.0, ((1, 8), (2, 16)), jnp.float32)
    near = bell_draw(seeds[1], (NV, FRINGES), 1.0, 6.0, ((1, 128),), jnp.float32)
    donor_owner_keys = jax.random.split(jax.random.fold_in(seeds[2], 1), FRINGES // FR_DEV)
    donor_owner_turns = jax.random.permutation(jax.random.fold_in(seeds[2], 3), FRINGES // FR_DEV)
    donor_owner = jax.vmap(lambda own, number: deal_out(jax.random.fold_in(seeds[2], 2), own, number, FR_DEV, DEVICES, 1, CAP, 2))(donor_owner_keys, donor_owner_turns).reshape((FRINGES, 1))
    donor_block = plant(jax.random.randint(seeds[3], (FRINGES,), 0, BLK_DEV), jax.random.fold_in(seeds[3], 1), 0, BLK_DEV - 1).astype(jnp.int32)
    recv_offset = plant(jax.random.randint(seeds[4], (FRINGES,), 0, 512), jax.random.fold_in(seeds[4], 1), 0, 511).astype(jnp.int32)
    weights = bell_draw(seeds[5], (3, 8, FRINGES), 0.35, 3.0, ((2, 128),), jnp.float32)
    return {"flow": flow, "near": near, "donor_owner": donor_owner, "donor_block": donor_block, "recv_offset": recv_offset, "weights": weights}


second_taps = (1.0 / 90, -3.0 / 20, 3.0 / 2, -49.0 / 18, 3.0 / 2, -3.0 / 20, 1.0 / 90)
first_taps = (-1.0 / 60, 3.0 / 20, -3.0 / 4, 0.0, 3.0 / 4, -3.0 / 20, 1.0 / 60)
diffusion = 0.05
velocity = (0.6, -0.5, 0.4)
relaxation = 0.6


def advance(padded, flow):
    extent = flow.shape[1:]
    result = flow
    for axis_pos in range(3):
        total = jnp.zeros_like(flow)
        for offset in range(7):
            factor = diffusion * second_taps[offset] - velocity[axis_pos] * first_taps[offset]
            starts = [3, 3, 3]
            starts[axis_pos] = offset
            piece = padded[:, starts[0]:starts[0] + extent[0], starts[1]:starts[1] + extent[1], starts[2]:starts[2] + extent[2]]
            total = total + factor * piece
        result = result + total
    return result


def inject(flow, values, flat_cell):
    shape = flow.shape
    plain = flow.reshape(shape[0], -1)
    accum = jnp.zeros_like(plain).at[:, flat_cell].add(values)
    counts = jnp.zeros((plain.shape[1],), plain.dtype).at[flat_cell].add(jnp.ones_like(values[0]))
    return ((plain + accum) / (1.0 + counts)[None, :]).reshape(shape)


def reference(flow, near, donor_owner, donor_block, recv_offset, weights):
    owner = donor_owner[:, 0]
    blocks_y = CY // 8
    blocks_z = CZ // 8
    base_x = (owner // N_GY) * CX + 8 * (donor_block // (blocks_y * blocks_z))
    base_y = (owner % N_GY) * CY + 8 * ((donor_block // blocks_z) % blocks_y)
    base_z = 8 * (donor_block % blocks_z)
    cell_x = base_x + recv_offset // 64
    cell_y = base_y + (recv_offset // 8) % 8
    cell_z = base_z + recv_offset % 8
    flat_cell = ((cell_x * NY + cell_y) * NZ + cell_z).astype(jnp.int32)
    groups = FRINGES // FR_DEV
    grouped_x = base_x.reshape(groups, FR_DEV).astype(jnp.int32)
    grouped_y = base_y.reshape(groups, FR_DEV).astype(jnp.int32)
    grouped_z = base_z.reshape(groups, FR_DEV).astype(jnp.int32)
    grouped_w = jnp.transpose(weights.reshape(3, 8, groups, FR_DEV), (2, 0, 1, 3))
    zero_index = jnp.zeros((), jnp.int32)
    for step in range(STEPS):
        padded = jnp.pad(flow, ((0, 0), (3, 3), (3, 3), (3, 3)))
        flow = advance(padded, flow)

        def one_group(items):
            first_x, first_y, first_z, factors = items
            cut = jax.vmap(lambda a, b, c: lax.dynamic_slice(flow, (zero_index, a, b, c), (NV, 8, 8, 8)))(first_x, first_y, first_z)
            return jnp.einsum("fvabc,af,bf,cf->vf", cut, factors[0], factors[1], factors[2], precision=lax.Precision.HIGHEST)

        interp = lax.map(one_group, (grouped_x, grouped_y, grouped_z, grouped_w))
        interp = jnp.transpose(interp, (1, 0, 2)).reshape(NV, FRINGES)
        near = near + relaxation * (interp - near)
        flow = inject(flow, near, flat_cell)
    return flow, near
```

```python
import functools

import jax
import jax.numpy as jnp
from jax import lax
from jax.experimental import pallas as pl
from jax.experimental.pallas import tpu as pltpu
from jax.sharding import PartitionSpec as P

STEPS = 2
NV = 5
CX = 16
CY = 32
CZ = 128
FR = 128
GX = 8
GY = 16
DEVICES = GX * GY
SLOTS = 2 * DEVICES
PX = CX + 6
PY = CY + 16
Y0 = 8

second_taps = (1.0 / 90, -3.0 / 20, 3.0 / 2, -49.0 / 18, 3.0 / 2, -3.0 / 20, 1.0 / 90)
first_taps = (-1.0 / 60, 3.0 / 20, -3.0 / 4, 0.0, 3.0 / 4, -3.0 / 20, 1.0 / 60)
diffusion = 0.05
velocity = (0.6, -0.5, 0.4)
relaxation = 0.6

TAPS = [
    [diffusion * second_taps[o] - velocity[d] * first_taps[o] for o in range(7)] for d in range(3)
]
CENTER = 1.0 + sum(TAPS[d][3] for d in range(3))
OFFSETS = (-3, -2, -1, 1, 2, 3)
HIGHEST = lax.Precision.HIGHEST
MESH = pl.DeviceIdType.MESH
BF16 = jnp.bfloat16
F32 = jnp.float32


def tap(dim, j):
    return TAPS[dim][j + 3]


def split(value):
    high = value.astype(BF16)
    low = (value - high.astype(F32)).astype(BF16)
    return high, low


def kernel(
    flow_hbm, near_hbm, owner_hbm, block_hbm, offset_hbm, weights_hbm,
    flow_out, near_out,
    g0, g1, res, hx, hy, sy,
    near_in, owner_in, block_in, offset_in, weights_in, near_res,
    a1, b1, bt, c1, d1, e1, et, fin,
    ohot, wz_rhs, plane, pick, pzt, recip,
    in_sem, small_sem, halo_send, halo_recv, a2a_send, a2a_recv, out_sem, near_sem,
):
    gx = lax.axis_index("gx")
    gy = lax.axis_index("gy")

    small = [
        pltpu.make_async_copy(src, dst, small_sem.at[i])
        for i, (src, dst) in enumerate(
            (
                (owner_hbm, owner_in),
                (block_hbm, block_in),
                (offset_hbm, offset_in),
                (near_hbm, near_in),
                (weights_hbm, weights_in),
            )
        )
    ]
    for copy in small:
        copy.start()

    def flow_in(v):
        return pltpu.make_async_copy(
            flow_hbm.at[v],
            g0.at[pl.ds(v * PX + 3, CX), pl.ds(Y0, CY)],
            in_sem.at[v],
        )

    for v in range(NV):
        flow_in(v).start()

    hx[...] = jnp.zeros_like(hx)
    hy[...] = jnp.zeros_like(hy)

    barrier = pltpu.get_barrier_semaphore()
    for k in range(1, GX):
        pl.semaphore_signal(
            barrier, inc=1, device_id=(lax.rem(gx + k, GX), gy), device_id_type=MESH
        )
    for k in range(1, GY):
        pl.semaphore_signal(
            barrier, inc=1, device_id=(gx, lax.rem(gy + k, GY)), device_id_type=MESH
        )

    def clear(v, carry):
        for g in (g0, g1):
            for x in (0, 1, 2, PX - 3, PX - 2, PX - 1):
                g[v * PX + x, Y0 : Y0 + CY] = jnp.zeros((CY, CZ), F32)
            for x in range(3, PX - 3):
                g[v * PX + x, 0:Y0] = jnp.zeros((Y0, CZ), F32)
                g[v * PX + x, Y0 + CY : PY] = jnp.zeros((PY - Y0 - CY, CZ), F32)
        return carry

    lax.fori_loop(0, NV, clear, 0)

    for copy in small:
        copy.wait()
    owner_row = owner_in[...]
    row = lax.broadcasted_iota(jnp.int32, (FR, FR), 0)
    col = lax.broadcasted_iota(jnp.int32, (FR, FR), 1)
    owner_wide = jnp.broadcast_to(owner_row, (FR, FR))
    owner_tall = jnp.transpose(owner_wide)
    earlier = jnp.where((owner_wide == owner_tall) & (row < col), 1.0, 0.0).astype(F32)
    rank = jnp.sum(earlier, axis=0, keepdims=True)
    mine = owner_wide == row
    ohot[0] = jnp.where(mine & (rank < 0.5), 1.0, 0.0).astype(F32)
    ohot[1] = jnp.where(mine & (rank > 0.5), 1.0, 0.0).astype(F32)
    payload = jnp.concatenate(
        [
            weights_in[...],
            near_in[...],
            block_in[...].astype(F32),
            offset_in[...].astype(F32),
            jnp.ones((1, FR), F32),
        ],
        axis=0,
    )
    nothing = jnp.zeros((32, FR), F32)
    blank = jnp.zeros((64, FR), F32)
    contract_last = (((1,), (1,)), ((), ()))
    rows = lax.dot_general(
        ohot[0], jnp.concatenate([payload, nothing, blank], axis=0), contract_last,
        precision=HIGHEST, preferred_element_type=F32,
    ) + lax.dot_general(
        ohot[1], jnp.concatenate([nothing, payload, blank], axis=0), contract_last,
        precision=HIGHEST, preferred_element_type=F32,
    )
    a1[...] = rows.reshape(GX, GY, 128)

    pl.semaphore_wait(barrier, GX - 1 + GY - 1)

    def exchange_x(src, dst, phase):
        def send(k, carry):
            peer = lax.rem(gx + k, GX)
            pltpu.make_async_remote_copy(
                src_ref=src.at[peer], dst_ref=dst.at[gx],
                send_sem=a2a_send.at[phase], recv_sem=a2a_recv.at[phase],
                device_id=(peer, gy), device_id_type=MESH,
            ).start()
            return carry

        lax.fori_loop(1, GX, send, 0)
        dst[gx] = src[gx]

    def exchange_y(src, dst, phase):
        def send(k, carry):
            peer = lax.rem(gy + k, GY)
            pltpu.make_async_remote_copy(
                src_ref=src.at[peer], dst_ref=dst.at[gy],
                send_sem=a2a_send.at[phase], recv_sem=a2a_recv.at[phase],
                device_id=(gx, peer), device_id_type=MESH,
            ).start()
            return carry

        lax.fori_loop(1, GY, send, 0)
        dst[gy] = src[gy]

    def exchange_wait(buf, count, sem):
        part = buf.at[pl.ds(0, count - 1)]
        pltpu.make_async_copy(part, part, sem).wait()

    exchange_x(a1, b1, 0)

    def face(step, v, side):
        g = (g0, g1)[step]
        if side < 2:
            first = 3 + (CX - 3 if side == 0 else 0)
            src = g.at[pl.ds(v * PX + first, 3), pl.ds(Y0, CY)]
            dst = hx.at[step, v, side]
            target = (gx + (1 if side == 0 else -1), gy)
        else:
            src = sy.at[step, v, side - 2]
            dst = hy.at[step, v, side - 2]
            target = (gx, gy + (1 if side == 2 else -1))
        return pltpu.make_async_remote_copy(
            src_ref=src, dst_ref=dst,
            send_sem=halo_send.at[step, v, side], recv_sem=halo_recv.at[step, v, side],
            device_id=target, device_id_type=MESH,
        )

    sends = (gx < GX - 1, gx > 0, gy < GY - 1, gy > 0)
    takes = (gx > 0, gx < GX - 1, gy > 0, gy < GY - 1)

    def send_faces(step, v):
        flat = (g0, g1)[step].reshape(NV * PX * PY, CZ)
        for side in (0, 1):
            @pl.when(sends[side])
            def _():
                face(step, v, side).start()
        for side, first in ((0, CY - 3), (1, 0)):
            for j in range(3):
                for half in range(2):
                    start = (v * PX + 3 + 8 * half) * PY + Y0 + first + j
                    sy[step, v, side, pl.ds(j * CX + 8 * half, 8)] = flat[pl.ds(start, 8, PY)]
        for side in (2, 3):
            @pl.when(sends[side])
            def _():
                face(step, v, side).start()

    def first_faces(v, carry):
        flow_in(v).wait()
        send_faces(0, v)
        return carry

    lax.fori_loop(0, NV, first_faces, 0)

    lane = lax.broadcasted_iota(jnp.int32, (8, CZ), 1)
    along_z = [
        jnp.where((lane + j >= 0) & (lane + j < CZ), tap(2, j), 0.0).astype(F32) for j in OFFSETS
    ]

    def interior(step, low, high):
        g = (g0, g1)[step]

        def body(i, carry):
            at = (i // CX) * PX + lax.rem(i, CX) + 3
            mid = g[at, Y0 : Y0 + CY]
            total = mid * CENTER
            for j in OFFSETS:
                total = total + g[at + j, Y0 : Y0 + CY] * tap(0, j)
            for j in OFFSETS:
                total = total + g[at, Y0 + j : Y0 + CY + j] * tap(1, j)
            tiles = mid.reshape(CY // 8, 8, CZ)
            for k, j in enumerate(OFFSETS):
                moved = pltpu.roll(mid, (-j) % CZ, axis=1).reshape(CY // 8, 8, CZ)
                total = total + (moved * along_z[k][None]).reshape(CY, CZ)
            res[i] = total
            return carry

        lax.fori_loop(low * CX, high * CX, body, 0)

    interior(0, 0, 2)

    exchange_wait(b1, GX, a2a_recv.at[0])
    b_flat = b1.reshape(GX * GY, 128)
    for h in range(GY):
        bt[h] = b_flat[pl.ds(h, GX, GY)]
    exchange_y(bt, c1, 1)

    interior(0, 2, NV)

    exchange_wait(c1, GY, a2a_recv.at[1])
    table = jnp.transpose(c1[...].reshape(DEVICES, 128))
    asked = jnp.concatenate([table[0:32], table[32:64]], axis=1)
    wx = asked[0:8]
    wy = asked[8:16]
    wz = asked[16:24]
    last = asked[24:32]
    block = last[5:6].astype(jnp.int32)
    offset = last[6:7].astype(jnp.int32)
    live = last[7:8]
    row8 = lax.broadcasted_iota(jnp.int32, (8, SLOTS), 0)
    near = jnp.where(row8 < NV, last, 0.0)
    kx = block // 64
    ky = (block // 16) % 4
    kz = block % 16
    weights_z = jnp.concatenate(
        [jnp.where(kz == b, wz, 0.0) for b in range(CZ // 8)], axis=0
    )
    z_high, z_low = split(weights_z)
    wz_rhs[0:CZ] = z_high
    wz_rhs[CZ : 2 * CZ] = z_high
    wz_rhs[2 * CZ :] = z_low
    weights_x = jnp.concatenate([jnp.where(kx == b, wx, 0.0) for b in range(CX // 8)], axis=0)
    weights_y = jnp.concatenate([jnp.where(ky == b, wy, 0.0) for b in range(CY // 8)], axis=0)
    for x in range(CX):
        plane[x * CY : (x + 1) * CY] = weights_x[x : x + 1] * weights_y
    cell = (8 * kx + offset // 64) * CY + 8 * ky + (offset // 8) % 8
    cell = jnp.where(live > 0.5, cell, -1)
    cell_z = 8 * kz + offset % 8
    places = lax.broadcasted_iota(jnp.int32, (CX * CY, SLOTS), 0)
    pick[...] = jnp.where(places == cell, 1.0, 0.0).astype(F32).astype(BF16)
    places_z = lax.broadcasted_iota(jnp.int32, (CZ, SLOTS), 0)
    hot_z = jnp.where(places_z == cell_z, 1.0, 0.0).astype(F32).astype(BF16)
    pzt[:, 0:SLOTS] = hot_z
    pzt[:, SLOTS:] = hot_z
    counts = lax.dot_general(
        pick[...], hot_z, contract_last, preferred_element_type=F32
    )
    recip[...] = 1.0 / (1.0 + counts)

    flat_res = res.reshape(NV * CX * CY, CZ)

    def add_halo(step, v):
        for r in range(3):
            low = res[v * CX + r]
            high = res[v * CX + CX - 1 - r]
            for j in range(-3, -r):
                low = low + hx[step, v, 0, r + j + 3] * tap(0, j)
                high = high + hx[step, v, 1, -r - 1 - j] * tap(0, -j)
            res[v * CX + r] = low
            res[v * CX + CX - 1 - r] = high
        for r in range(3):
            for half in range(2):
                start = (v * CX + 8 * half) * CY
                at_low = pl.ds(start + r, 8, CY)
                at_high = pl.ds(start + CY - 1 - r, 8, CY)
                low = flat_res[at_low]
                high = flat_res[at_high]
                for j in range(-3, -r):
                    low = low + hy[step, v, 0, pl.ds((r + j + 3) * CX + 8 * half, 8)] * tap(1, j)
                    high = high + hy[step, v, 1, pl.ds((-r - 1 - j) * CX + 8 * half, 8)] * tap(1, -j)
                flat_res[at_low] = low
                flat_res[at_high] = high

    def finish_flow(step, near):
        def body(v, interp):
            for side in range(4):
                @pl.when(takes[side])
                def _():
                    face(step, v, side).wait_recv()
            add_halo(step, v)
            values = flat_res[pl.ds(pl.multiple_of(v * CX * CY, CX * CY), CX * CY)]
            high, low = split(values)
            t = jnp.dot(
                jnp.concatenate([high, low, high], axis=1), wz_rhs[...],
                preferred_element_type=F32,
            )
            here = jnp.sum(t * plane[...], axis=0, keepdims=True)
            return jnp.where(row8 == v, here, interp)

        interp = lax.fori_loop(0, NV, body, jnp.zeros((8, SLOTS), F32))
        return near + relaxation * (interp - near)

    def injected(v, near):
        here = jnp.sum(jnp.where(row8 == v, near, 0.0), axis=0, keepdims=True)
        here = jnp.broadcast_to(here, (16, SLOTS))
        high, low = split(here)
        hot = pick[...].reshape(CX * CY // 16, 16, SLOTS)
        left = jnp.concatenate(
            [
                (hot * high[None]).reshape(CX * CY, SLOTS),
                (hot * low[None]).reshape(CX * CY, SLOTS),
            ],
            axis=1,
        )
        gained = lax.dot_general(left, pzt[...], contract_last, preferred_element_type=F32)
        values = flat_res[pl.ds(pl.multiple_of(v * CX * CY, CX * CY), CX * CY)]
        return ((values + gained) * recip[...]).reshape(CX, CY, CZ)

    near = finish_flow(0, near)

    def second_faces(v, carry):
        g1[pl.ds(v * PX + 3, CX), Y0 : Y0 + CY] = injected(v, near)
        send_faces(1, v)
        return carry

    lax.fori_loop(0, NV, second_faces, 0)
    interior(1, 0, NV)
    near = finish_flow(1, near)

    back = jnp.concatenate(
        [near[:, :DEVICES], near[:, DEVICES:], jnp.zeros((DEVICES - 16, DEVICES), F32)], axis=0
    )
    d1[...] = jnp.transpose(back).reshape(GY, GX, 128)
    exchange_y(d1, e1, 2)

    def flow_back(v):
        return pltpu.make_async_copy(
            res.at[pl.ds(v * CX, CX)], flow_out.at[v], out_sem.at[v]
        )

    def last_injection(v, carry):
        res[pl.ds(v * CX, CX)] = injected(v, near)
        flow_back(v).start()
        return carry

    lax.fori_loop(0, 3, last_injection, 0)
    exchange_wait(e1, GY, a2a_recv.at[2])
    e_flat = e1.reshape(GX * GY, 128)
    for g in range(GX):
        for half in range(2):
            et[g, 8 * half : 8 * half + 8] = e_flat[pl.ds(8 * half * GX + g, 8, GX)]
    exchange_x(et, fin, 3)
    lax.fori_loop(3, NV, last_injection, 0)
    exchange_wait(fin, GX, a2a_recv.at[3])
    returned = jnp.transpose(fin[...].reshape(DEVICES, 128))
    served = jnp.dot(
        returned[0:8], ohot[0], precision=HIGHEST, preferred_element_type=F32
    ) + jnp.dot(returned[8:16], ohot[1], precision=HIGHEST, preferred_element_type=F32)
    near_res[...] = served[0:NV]
    near_copy = pltpu.make_async_copy(near_res, near_out, near_sem)
    near_copy.start()

    exchange_wait(a1, GX, a2a_send.at[0])
    exchange_wait(bt, GY, a2a_send.at[1])
    exchange_wait(d1, GY, a2a_send.at[2])
    exchange_wait(et, GX, a2a_send.at[3])

    def drain(v, carry):
        for step in range(STEPS):
            for side in range(4):
                @pl.when(sends[side])
                def _():
                    face(step, v, side).wait_send()
        flow_back(v).wait()
        return carry

    lax.fori_loop(0, NV, drain, 0)
    near_copy.wait()


def shards(flow, near, donor_owner, donor_block, recv_offset, weights):
    anywhere = pl.BlockSpec(memory_space=pl.ANY)
    vmem = pltpu.VMEM
    dma = pltpu.SemaphoreType.DMA
    return pl.pallas_call(
        kernel,
        out_shape=(
            jax.ShapeDtypeStruct((NV, CX, CY, CZ), F32),
            jax.ShapeDtypeStruct((NV, FR), F32),
        ),
        in_specs=[anywhere] * 6,
        out_specs=(anywhere, anywhere),
        scratch_shapes=[
            vmem((NV * PX, PY, CZ), F32),
            vmem((NV * PX, PY, CZ), F32),
            vmem((NV * CX, CY, CZ), F32),
            vmem((STEPS, NV, 2, 3, CY, CZ), F32),
            vmem((STEPS, NV, 2, 3 * CX, CZ), F32),
            vmem((STEPS, NV, 2, 3 * CX, CZ), F32),
            vmem((NV, FR), F32),
            vmem((1, FR), jnp.int32),
            vmem((1, FR), jnp.int32),
            vmem((1, FR), jnp.int32),
            vmem((24, FR), F32),
            vmem((NV, FR), F32),
            vmem((GX, GY, 128), F32),
            vmem((GX, GY, 128), F32),
            vmem((GY, GX, 128), F32),
            vmem((GY, GX, 128), F32),
            vmem((GY, GX, 128), F32),
            vmem((GY, GX, 128), F32),
            vmem((GX, GY, 128), F32),
            vmem((GX, GY, 128), F32),
            vmem((2, DEVICES, FR), F32),
            vmem((3 * CZ, SLOTS), BF16),
            vmem((CX * CY, SLOTS), F32),
            vmem((CX * CY, SLOTS), BF16),
            vmem((CZ, 2 * SLOTS), BF16),
            vmem((CX * CY, CZ), F32),
            dma((NV,)),
            dma((5,)),
            dma((STEPS, NV, 4)),
            dma((STEPS, NV, 4)),
            dma((4,)),
            dma((4,)),
            dma((NV,)),
            dma,
        ],
        compiler_params=pltpu.CompilerParams(
            collective_id=0, has_side_effects=True, vmem_limit_bytes=48 * 1024 * 1024
        ),
        cost_estimate=pl.CostEstimate(
            flops=2 * STEPS * 20 * NV * CX * CY * CZ,
            bytes_accessed=2 * 4 * NV * CX * CY * CZ,
            transcendentals=0,
        ),
        name="rotor_wake_steps",
    )(
        flow,
        near,
        donor_owner.reshape(1, FR),
        donor_block.reshape(1, FR),
        recv_offset.reshape(1, FR),
        weights.reshape(24, FR),
    )


def solution(mesh):
    in_specs = (
        P(None, "gx", "gy", None),
        P(None, ("gx", "gy")),
        P(("gx", "gy"), None),
        P(("gx", "gy")),
        P(("gx", "gy")),
        P(None, None, ("gx", "gy")),
    )
    out_specs = (P(None, "gx", "gy", None), P(None, ("gx", "gy")))
    return jax.shard_map(shards, mesh=mesh, in_specs=in_specs, out_specs=out_specs, check_vma=False)
```

```python
import functools

import jax
import jax.numpy as jnp
from jax import lax
from jax.experimental import pallas as pl
from jax.experimental.pallas import tpu as pltpu
from jax.sharding import PartitionSpec as P

STEPS = 2
NV = 5
CX = 16
CY = 32
CZ = 128
FR = 128
GX = 8
GY = 16
DEVICES = GX * GY
SLOTS = 2 * DEVICES
PX = CX + 6
PY = CY + 16
Y0 = 8

second_taps = (1.0 / 90, -3.0 / 20, 3.0 / 2, -49.0 / 18, 3.0 / 2, -3.0 / 20, 1.0 / 90)
first_taps = (-1.0 / 60, 3.0 / 20, -3.0 / 4, 0.0, 3.0 / 4, -3.0 / 20, 1.0 / 60)
diffusion = 0.05
velocity = (0.6, -0.5, 0.4)
relaxation = 0.6

TAPS = [
    [diffusion * second_taps[o] - velocity[d] * first_taps[o] for o in range(7)] for d in range(3)
]
CENTER = 1.0 + sum(TAPS[d][3] for d in range(3))
OFFSETS = (-3, -2, -1, 1, 2, 3)
HIGHEST = lax.Precision.HIGHEST
MESH = pl.DeviceIdType.MESH
BF16 = jnp.bfloat16
F32 = jnp.float32


def tap(dim, j):
    return TAPS[dim][j + 3]


def split(value):
    high = value.astype(BF16)
    low = (value - high.astype(F32)).astype(BF16)
    return high, low


def three_term(values, right):
    high, low = split(values)
    return jnp.dot(
        jnp.concatenate([high, low, high], axis=1), right, preferred_element_type=F32
    )


def kernel(
    flow_hbm, near_hbm, owner_hbm, block_hbm, offset_hbm, weights_hbm,
    flow_out, near_out,
    g0, g1, res, hx, hy, sy,
    near_in, owner_in, block_in, offset_in, weights_in, near_res,
    a1, b1, bt, c1, d1, e1, et, fin,
    ohot, along_z, wz_rhs, plane, pick, pzt, recip,
    in_sem, small_sem, halo_send, halo_recv, a2a_send, a2a_recv, out_sem, near_sem,
):
    gx = lax.axis_index("gx")
    gy = lax.axis_index("gy")

    small = [
        pltpu.make_async_copy(src, dst, small_sem.at[i])
        for i, (src, dst) in enumerate(
            (
                (owner_hbm, owner_in),
                (block_hbm, block_in),
                (offset_hbm, offset_in),
                (near_hbm, near_in),
                (weights_hbm, weights_in),
            )
        )
    ]
    for copy in small:
        copy.start()

    def flow_in(v):
        return pltpu.make_async_copy(
            flow_hbm.at[v],
            g0.at[pl.ds(v * PX + 3, CX), pl.ds(Y0, CY)],
            in_sem.at[v],
        )

    for v in range(NV):
        flow_in(v).start()

    hx[...] = jnp.zeros_like(hx)
    hy[...] = jnp.zeros_like(hy)

    barrier = pltpu.get_barrier_semaphore()
    for k in range(1, GX):
        pl.semaphore_signal(
            barrier, inc=1, device_id=(lax.rem(gx + k, GX), gy), device_id_type=MESH
        )
    for k in range(1, GY):
        pl.semaphore_signal(
            barrier, inc=1, device_id=(gx, lax.rem(gy + k, GY)), device_id_type=MESH
        )

    def clear(v, carry):
        for g in (g0, g1):
            for x in (0, 1, 2, PX - 3, PX - 2, PX - 1):
                g[v * PX + x, Y0 : Y0 + CY] = jnp.zeros((CY, CZ), F32)
            for x in range(3, PX - 3):
                g[v * PX + x, 0:Y0] = jnp.zeros((Y0, CZ), F32)
                g[v * PX + x, Y0 + CY : PY] = jnp.zeros((PY - Y0 - CY, CZ), F32)
        return carry

    lax.fori_loop(0, NV, clear, 0)

    z_from = lax.broadcasted_iota(jnp.int32, (CZ, CZ), 0)
    z_to = lax.broadcasted_iota(jnp.int32, (CZ, CZ), 1)
    band = jnp.zeros((CZ, CZ), F32)
    for j in OFFSETS:
        band = jnp.where(z_from - z_to == j, tap(2, j), band)
    band_high, band_low = split(band)
    along_z[0:CZ] = band_high
    along_z[CZ : 2 * CZ] = band_high
    along_z[2 * CZ :] = band_low

    for copy in small:
        copy.wait()
    owner_row = owner_in[...]
    row = lax.broadcasted_iota(jnp.int32, (FR, FR), 0)
    col = lax.broadcasted_iota(jnp.int32, (FR, FR), 1)
    owner_wide = jnp.broadcast_to(owner_row, (FR, FR))
    owner_tall = jnp.transpose(owner_wide)
    earlier = jnp.where((owner_wide == owner_tall) & (row < col), 1.0, 0.0).astype(F32)
    rank = jnp.sum(earlier, axis=0, keepdims=True)
    mine = owner_wide == row
    ohot[0] = jnp.where(mine & (rank < 0.5), 1.0, 0.0).astype(F32)
    ohot[1] = jnp.where(mine & (rank > 0.5), 1.0, 0.0).astype(F32)
    payload = jnp.concatenate(
        [
            weights_in[...],
            near_in[...],
            block_in[...].astype(F32),
            offset_in[...].astype(F32),
            jnp.ones((1, FR), F32),
        ],
        axis=0,
    )
    nothing = jnp.zeros((32, FR), F32)
    blank = jnp.zeros((64, FR), F32)
    contract_last = (((1,), (1,)), ((), ()))
    rows = lax.dot_general(
        ohot[0], jnp.concatenate([payload, nothing, blank], axis=0), contract_last,
        precision=HIGHEST, preferred_element_type=F32,
    ) + lax.dot_general(
        ohot[1], jnp.concatenate([nothing, payload, blank], axis=0), contract_last,
        precision=HIGHEST, preferred_element_type=F32,
    )
    a1[...] = rows.reshape(GX, GY, 128)

    pl.semaphore_wait(barrier, GX - 1 + GY - 1)

    def exchange_x(src, dst, phase):
        def send(k, carry):
            peer = lax.rem(gx + k, GX)
            pltpu.make_async_remote_copy(
                src_ref=src.at[peer], dst_ref=dst.at[gx],
                send_sem=a2a_send.at[phase], recv_sem=a2a_recv.at[phase],
                device_id=(peer, gy), device_id_type=MESH,
            ).start()
            return carry

        lax.fori_loop(1, GX, send, 0)
        dst[gx] = src[gx]

    def exchange_y(src, dst, phase):
        def send(k, carry):
            peer = lax.rem(gy + k, GY)
            pltpu.make_async_remote_copy(
                src_ref=src.at[peer], dst_ref=dst.at[gy],
                send_sem=a2a_send.at[phase], recv_sem=a2a_recv.at[phase],
                device_id=(gx, peer), device_id_type=MESH,
            ).start()
            return carry

        lax.fori_loop(1, GY, send, 0)
        dst[gy] = src[gy]

    def exchange_wait(buf, count, sem):
        part = buf.at[pl.ds(0, count - 1)]
        pltpu.make_async_copy(part, part, sem).wait()

    exchange_x(a1, b1, 0)

    def face(step, v, side):
        g = (g0, g1)[step]
        if side < 2:
            first = 3 + (CX - 3 if side == 0 else 0)
            src = g.at[pl.ds(v * PX + first, 3), pl.ds(Y0, CY)]
            dst = hx.at[step, v, side]
            target = (gx + (1 if side == 0 else -1), gy)
        else:
            src = sy.at[step, v, side - 2]
            dst = hy.at[step, v, side - 2]
            target = (gx, gy + (1 if side == 2 else -1))
        return pltpu.make_async_remote_copy(
            src_ref=src, dst_ref=dst,
            send_sem=halo_send.at[step, v, side], recv_sem=halo_recv.at[step, v, side],
            device_id=target, device_id_type=MESH,
        )

    sends = (gx < GX - 1, gx > 0, gy < GY - 1, gy > 0)
    takes = (gx > 0, gx < GX - 1, gy > 0, gy < GY - 1)

    def send_faces(step, v):
        flat = (g0, g1)[step].reshape(NV * PX * PY, CZ)
        for side in (0, 1):
            @pl.when(sends[side])
            def _():
                face(step, v, side).start()
        for side, first in ((0, CY - 3), (1, 0)):
            for j in range(3):
                for half in range(2):
                    start = (v * PX + 3 + 8 * half) * PY + Y0 + first + j
                    sy[step, v, side, pl.ds(j * CX + 8 * half, 8)] = flat[pl.ds(start, 8, PY)]
        for side in (2, 3):
            @pl.when(sends[side])
            def _():
                face(step, v, side).start()

    def first_faces(v, carry):
        flow_in(v).wait()
        send_faces(0, v)
        return carry

    lax.fori_loop(0, NV, first_faces, 0)

    def interior(step, low, high):
        g = (g0, g1)[step]

        def body(v, carry):
            at = v * PX + 3
            mid = g[pl.ds(at, CX), Y0 : Y0 + CY]
            total = mid * CENTER
            for j in OFFSETS:
                total = total + g[pl.ds(at + j, CX), Y0 : Y0 + CY] * tap(0, j)
            for j in OFFSETS:
                total = total + g[pl.ds(at, CX), Y0 + j : Y0 + CY + j] * tap(1, j)
            z_part = three_term(mid.reshape(CX * CY, CZ), along_z[...])
            res[pl.ds(v * CX, CX)] = total + z_part.reshape(CX, CY, CZ)
            return carry

        lax.fori_loop(low, high, body, 0)

    interior(0, 0, 2)

    exchange_wait(b1, GX, a2a_recv.at[0])
    b_flat = b1.reshape(GX * GY, 128)
    for h in range(GY):
        bt[h] = b_flat[pl.ds(h, GX, GY)]
    exchange_y(bt, c1, 1)

    interior(0, 2, NV)

    exchange_wait(c1, GY, a2a_recv.at[1])
    table = jnp.transpose(c1[...].reshape(DEVICES, 128))
    asked = jnp.concatenate([table[0:32], table[32:64]], axis=1)
    wx = asked[0:8]
    wy = asked[8:16]
    wz = asked[16:24]
    last = asked[24:32]
    block = last[5:6].astype(jnp.int32)
    offset = last[6:7].astype(jnp.int32)
    live = last[7:8]
    row8 = lax.broadcasted_iota(jnp.int32, (8, SLOTS), 0)
    near = jnp.where(row8 < NV, last, 0.0)
    kx = block // 64
    ky = (block // 16) % 4
    kz = block % 16
    weights_z = jnp.concatenate(
        [jnp.where(kz == b, wz, 0.0) for b in range(CZ // 8)], axis=0
    )
    z_high, z_low = split(weights_z)
    wz_rhs[0:CZ] = z_high
    wz_rhs[CZ : 2 * CZ] = z_high
    wz_rhs[2 * CZ :] = z_low
    weights_x = jnp.concatenate([jnp.where(kx == b, wx, 0.0) for b in range(CX // 8)], axis=0)
    weights_y = jnp.concatenate([jnp.where(ky == b, wy, 0.0) for b in range(CY // 8)], axis=0)
    for x in range(CX):
        plane[x * CY : (x + 1) * CY] = weights_x[x : x + 1] * weights_y
    cell = (8 * kx + offset // 64) * CY + 8 * ky + (offset // 8) % 8
    cell = jnp.where(live > 0.5, cell, -1)
    cell_z = 8 * kz + offset % 8
    places = lax.broadcasted_iota(jnp.int32, (CX * CY, SLOTS), 0)
    pick[...] = jnp.where(places == cell, 1.0, 0.0).astype(F32).astype(BF16)
    places_z = lax.broadcasted_iota(jnp.int32, (CZ, SLOTS), 0)
    hot_z = jnp.where(places_z == cell_z, 1.0, 0.0).astype(F32).astype(BF16)
    pzt[:, 0:SLOTS] = hot_z
    pzt[:, SLOTS:] = hot_z
    counts = lax.dot_general(
        pick[...], hot_z, contract_last, preferred_element_type=F32
    )
    recip[...] = 1.0 / (1.0 + counts)

    flat_res = res.reshape(NV * CX * CY, CZ)

    def add_halo(step, v):
        for r in range(3):
            low = res[v * CX + r]
            high = res[v * CX + CX - 1 - r]
            for j in range(-3, -r):
                low = low + hx[step, v, 0, r + j + 3] * tap(0, j)
                high = high + hx[step, v, 1, -r - 1 - j] * tap(0, -j)
            res[v * CX + r] = low
            res[v * CX + CX - 1 - r] = high
        for r in range(3):
            for half in range(2):
                start = (v * CX + 8 * half) * CY
                at_low = pl.ds(start + r, 8, CY)
                at_high = pl.ds(start + CY - 1 - r, 8, CY)
                low = flat_res[at_low]
                high = flat_res[at_high]
                for j in range(-3, -r):
                    low = low + hy[step, v, 0, pl.ds((r + j + 3) * CX + 8 * half, 8)] * tap(1, j)
                    high = high + hy[step, v, 1, pl.ds((-r - 1 - j) * CX + 8 * half, 8)] * tap(1, -j)
                flat_res[at_low] = low
                flat_res[at_high] = high

    def finish_flow(step, near):
        def body(v, interp):
            for side in range(4):
                @pl.when(takes[side])
                def _():
                    face(step, v, side).wait_recv()
            add_halo(step, v)
            values = flat_res[pl.ds(pl.multiple_of(v * CX * CY, CX * CY), CX * CY)]
            t = three_term(values, wz_rhs[...])
            here = jnp.sum(t * plane[...], axis=0, keepdims=True)
            return jnp.where(row8 == v, here, interp)

        interp = lax.fori_loop(0, NV, body, jnp.zeros((8, SLOTS), F32))
        return near + relaxation * (interp - near)

    def injected(v, near):
        here = jnp.sum(jnp.where(row8 == v, near, 0.0), axis=0, keepdims=True)
        here = jnp.broadcast_to(here, (16, SLOTS))
        high, low = split(here)
        hot = pick[...].reshape(CX * CY // 16, 16, SLOTS)
        left = jnp.concatenate(
            [
                (hot * high[None]).reshape(CX * CY, SLOTS),
                (hot * low[None]).reshape(CX * CY, SLOTS),
            ],
            axis=1,
        )
        gained = lax.dot_general(left, pzt[...], contract_last, preferred_element_type=F32)
        values = flat_res[pl.ds(pl.multiple_of(v * CX * CY, CX * CY), CX * CY)]
        return ((values + gained) * recip[...]).reshape(CX, CY, CZ)

    near = finish_flow(0, near)

    def second_faces(v, carry):
        g1[pl.ds(v * PX + 3, CX), Y0 : Y0 + CY] = injected(v, near)
        send_faces(1, v)
        return carry

    lax.fori_loop(0, NV, second_faces, 0)
    interior(1, 0, NV)
    near = finish_flow(1, near)

    back = jnp.concatenate(
        [near[:, :DEVICES], near[:, DEVICES:], jnp.zeros((DEVICES - 16, DEVICES), F32)], axis=0
    )
    d1[...] = jnp.transpose(back).reshape(GY, GX, 128)
    exchange_y(d1, e1, 2)

    def flow_back(v):
        return pltpu.make_async_copy(
            res.at[pl.ds(v * CX, CX)], flow_out.at[v], out_sem.at[v]
        )

    def last_injection(v, carry):
        res[pl.ds(v * CX, CX)] = injected(v, near)
        flow_back(v).start()
        return carry

    lax.fori_loop(0, 3, last_injection, 0)
    exchange_wait(e1, GY, a2a_recv.at[2])
    e_flat = e1.reshape(GX * GY, 128)
    for g in range(GX):
        for half in range(2):
            et[g, 8 * half : 8 * half + 8] = e_flat[pl.ds(8 * half * GX + g, 8, GX)]
    exchange_x(et, fin, 3)
    lax.fori_loop(3, NV, last_injection, 0)
    exchange_wait(fin, GX, a2a_recv.at[3])
    returned = jnp.transpose(fin[...].reshape(DEVICES, 128))
    served = jnp.dot(
        returned[0:8], ohot[0], precision=HIGHEST, preferred_element_type=F32
    ) + jnp.dot(returned[8:16], ohot[1], precision=HIGHEST, preferred_element_type=F32)
    near_res[...] = served[0:NV]
    near_copy = pltpu.make_async_copy(near_res, near_out, near_sem)
    near_copy.start()

    exchange_wait(a1, GX, a2a_send.at[0])
    exchange_wait(bt, GY, a2a_send.at[1])
    exchange_wait(d1, GY, a2a_send.at[2])
    exchange_wait(et, GX, a2a_send.at[3])

    def drain(v, carry):
        for step in range(STEPS):
            for side in range(4):
                @pl.when(sends[side])
                def _():
                    face(step, v, side).wait_send()
        flow_back(v).wait()
        return carry

    lax.fori_loop(0, NV, drain, 0)
    near_copy.wait()


def shards(flow, near, donor_owner, donor_block, recv_offset, weights):
    anywhere = pl.BlockSpec(memory_space=pltpu.HBM)
    vmem = pltpu.VMEM
    dma = pltpu.SemaphoreType.DMA
    return pl.pallas_call(
        kernel,
        out_shape=(
            jax.ShapeDtypeStruct((NV, CX, CY, CZ), F32),
            jax.ShapeDtypeStruct((NV, FR), F32),
        ),
        in_specs=[anywhere] * 6,
        out_specs=(anywhere, anywhere),
        scratch_shapes=[
            vmem((NV * PX, PY, CZ), F32),
            vmem((NV * PX, PY, CZ), F32),
            vmem((NV * CX, CY, CZ), F32),
            vmem((STEPS, NV, 2, 3, CY, CZ), F32),
            vmem((STEPS, NV, 2, 3 * CX, CZ), F32),
            vmem((STEPS, NV, 2, 3 * CX, CZ), F32),
            vmem((NV, FR), F32),
            vmem((1, FR), jnp.int32),
            vmem((1, FR), jnp.int32),
            vmem((1, FR), jnp.int32),
            vmem((24, FR), F32),
            vmem((NV, FR), F32),
            vmem((GX, GY, 128), F32),
            vmem((GX, GY, 128), F32),
            vmem((GY, GX, 128), F32),
            vmem((GY, GX, 128), F32),
            vmem((GY, GX, 128), F32),
            vmem((GY, GX, 128), F32),
            vmem((GX, GY, 128), F32),
            vmem((GX, GY, 128), F32),
            vmem((2, DEVICES, FR), F32),
            vmem((3 * CZ, CZ), BF16),
            vmem((3 * CZ, SLOTS), BF16),
            vmem((CX * CY, SLOTS), F32),
            vmem((CX * CY, SLOTS), BF16),
            vmem((CZ, 2 * SLOTS), BF16),
            vmem((CX * CY, CZ), F32),
            dma((NV,)),
            dma((5,)),
            dma((STEPS, NV, 4)),
            dma((STEPS, NV, 4)),
            dma((4,)),
            dma((4,)),
            dma((NV,)),
            dma,
        ],
        compiler_params=pltpu.CompilerParams(
            collective_id=0, has_side_effects=True, vmem_limit_bytes=60 * 1024 * 1024
        ),
        cost_estimate=pl.CostEstimate(
            flops=2 * STEPS * 20 * NV * CX * CY * CZ,
            bytes_accessed=2 * 4 * NV * CX * CY * CZ,
            transcendentals=0,
        ),
        name="rotor_wake_steps",
    )(
        flow,
        near,
        donor_owner.reshape(1, FR),
        donor_block.reshape(1, FR),
        recv_offset.reshape(1, FR),
        weights.reshape(24, FR),
    )


def solution(mesh):
    in_specs = (
        P(None, "gx", "gy", None),
        P(None, ("gx", "gy")),
        P(("gx", "gy"), None),
        P(("gx", "gy")),
        P(("gx", "gy")),
        P(None, None, ("gx", "gy")),
    )
    out_specs = (P(None, "gx", "gy", None), P(None, ("gx", "gy")))
    return jax.shard_map(shards, mesh=mesh, in_specs=in_specs, out_specs=out_specs, check_vma=False)
```

```python
import itertools

import jax
import jax.numpy as jnp
from jax import lax
from jax.experimental import pallas as pl
from jax.experimental.pallas import tpu as pltpu
from jax.sharding import PartitionSpec as P

STEPS = 2
NV = 5
CX = 16
CY = 32
CZ = 128
FR = 128
GX = 8
GY = 16
DEVICES = GX * GY
SLOTS = 2 * DEVICES
PX = CX + 6
PY = CY + 16
Y0 = 8

second_taps = (1.0 / 90, -3.0 / 20, 3.0 / 2, -49.0 / 18, 3.0 / 2, -3.0 / 20, 1.0 / 90)
first_taps = (-1.0 / 60, 3.0 / 20, -3.0 / 4, 0.0, 3.0 / 4, -3.0 / 20, 1.0 / 60)
diffusion = 0.05
velocity = (0.6, -0.5, 0.4)
relaxation = 0.6

TAPS = [
    [diffusion * second_taps[o] - velocity[d] * first_taps[o] for o in range(7)] for d in range(3)
]
CENTER = 1.0 + sum(TAPS[d][3] for d in range(3))
OFFSETS = (-3, -2, -1, 1, 2, 3)
HIGHEST = lax.Precision.HIGHEST
MESH = pl.DeviceIdType.MESH
BF16 = jnp.bfloat16
F32 = jnp.float32


OTHERS = sorted(
    itertools.product(range(4), range(2), range(4), range(4)),
    key=lambda o: -10 * sum(min(o[i], 4 - o[i]) for i in (0, 2, 3)) - o[1],
)[:-1]


def tap(dim, j):
    return TAPS[dim][j + 3]


def split(value):
    high = value.astype(BF16)
    low = (value - high.astype(F32)).astype(BF16)
    return high, low


def three_term(values, right):
    high, low = split(values)
    return jnp.dot(
        jnp.concatenate([high, low, high], axis=1), right, preferred_element_type=F32
    )


def kernel(
    flow_hbm, near_hbm, owner_hbm, block_hbm, offset_hbm, weights_hbm,
    flow_out, near_out,
    g0, g1, res, hx, hy, sy,
    near_in, owner_in, block_in, offset_in, weights_in,
    a1, c1, d1, fin,
    ohot, along_z, lhs, wz_rhs, plane, pick, pzt, recip,
    in_sem, small_sem, first_send, first_recv, halo_send, halo_recv, a2a_send, a2a_recv,
):
    gx = lax.axis_index("gx")
    gy = lax.axis_index("gy")
    me = gx * GY + gy
    chip_x, core = gx // 2, lax.rem(gx, 2)
    chip_z, chip_y = gy // 4, lax.rem(gy, 4)

    def others():
        for dx, dc, dz, dy in OTHERS:
            yield (
                lax.rem(chip_x + dx, 4) * 2 + lax.rem(core + dc, 2),
                lax.rem(chip_z + dz, 4) * 4 + lax.rem(chip_y + dy, 4),
            )

    small = [
        pltpu.make_async_copy(src, dst, small_sem.at[i])
        for i, (src, dst) in enumerate(
            (
                (owner_hbm, owner_in),
                (block_hbm, block_in),
                (offset_hbm, offset_in),
                (near_hbm, near_in),
                (weights_hbm, weights_in),
            )
        )
    ]
    for copy in small:
        copy.start()

    def flow_in(v):
        return pltpu.make_async_copy(
            flow_hbm.at[v], g0.at[v, pl.ds(3, CX), pl.ds(Y0, CY)], in_sem.at[v]
        )

    for v in range(NV):
        flow_in(v).start()

    hx[...] = jnp.zeros_like(hx)
    hy[...] = jnp.zeros_like(hy)
    barrier = pltpu.get_barrier_semaphore()
    for peer in others():
        pl.semaphore_signal(barrier, inc=1, device_id=peer, device_id_type=MESH)

    def clear(v, carry):
        for g in (g0, g1):
            g[v, 0:3, Y0 : Y0 + CY] = jnp.zeros((3, CY, CZ), F32)
            g[v, PX - 3 : PX, Y0 : Y0 + CY] = jnp.zeros((3, CY, CZ), F32)
            g[v, 3 : PX - 3, 0:Y0] = jnp.zeros((CX, Y0, CZ), F32)
            g[v, 3 : PX - 3, Y0 + CY : PY] = jnp.zeros((CX, PY - Y0 - CY, CZ), F32)
        return carry

    lax.fori_loop(0, NV, clear, 0)

    z_from = lax.broadcasted_iota(jnp.int32, (CZ, CZ), 0)
    z_to = lax.broadcasted_iota(jnp.int32, (CZ, CZ), 1)
    band = jnp.zeros((CZ, CZ), F32)
    for j in OFFSETS:
        band = jnp.where(z_from - z_to == j, tap(2, j), band)
    band_high, band_low = split(band)
    along_z[0:CZ] = band_high
    along_z[CZ : 2 * CZ] = band_high
    along_z[2 * CZ :] = band_low

    for copy in small:
        copy.wait()
    row = lax.broadcasted_iota(jnp.int32, (FR, FR), 0)
    col = lax.broadcasted_iota(jnp.int32, (FR, FR), 1)
    owner_wide = jnp.broadcast_to(owner_in[...], (FR, FR))
    owner_tall = jnp.transpose(owner_wide)
    earlier = jnp.where((owner_wide == owner_tall) & (row < col), 1.0, 0.0).astype(F32)
    rank = jnp.sum(earlier, axis=0, keepdims=True)
    mine = owner_wide == row
    ohot[0] = jnp.where(mine & (rank < 0.5), 1.0, 0.0).astype(F32)
    ohot[1] = jnp.where(mine & (rank > 0.5), 1.0, 0.0).astype(F32)
    payload = jnp.concatenate(
        [
            weights_in[...],
            near_in[...],
            block_in[...].astype(F32),
            offset_in[...].astype(F32),
            jnp.ones((1, FR), F32),
        ],
        axis=0,
    )
    nothing = jnp.zeros((32, FR), F32)
    blank = jnp.zeros((64, FR), F32)
    contract_last = (((1,), (1,)), ((), ()))
    a1[...] = lax.dot_general(
        ohot[0], jnp.concatenate([payload, nothing, blank], axis=0), contract_last,
        precision=HIGHEST, preferred_element_type=F32,
    ) + lax.dot_general(
        ohot[1], jnp.concatenate([nothing, payload, blank], axis=0), contract_last,
        precision=HIGHEST, preferred_element_type=F32,
    )

    targets = ((gx + 1, gy), (gx - 1, gy), (gx, gy + 1), (gx, gy - 1))
    sends = (gx < GX - 1, gx > 0, gy < GY - 1, gy > 0)
    takes = (gx > 0, gx < GX - 1, gy > 0, gy < GY - 1)

    def face(step, side, v=None):
        g = (g0, g1)[step]
        if side < 2:
            layers = pl.ds(CX if side == 0 else 3, 3)
            if v is None:
                src, dst = g.at[:, layers, pl.ds(Y0, CY)], hx.at[step, side]
            else:
                src, dst = g.at[v, layers, pl.ds(Y0, CY)], hx.at[step, side, v]
        elif v is None:
            src, dst = sy.at[step, side - 2], hy.at[step, side - 2]
        else:
            src, dst = sy.at[step, side - 2, v], hy.at[step, side - 2, v]
        return pltpu.make_async_remote_copy(
            src_ref=src, dst_ref=dst,
            send_sem=first_send.at[side] if v is None else halo_send.at[v, side],
            recv_sem=first_recv.at[side] if v is None else halo_recv.at[v, side],
            device_id=targets[side], device_id_type=MESH,
        )

    def pack_faces(step, v):
        flat = (g0, g1)[step].reshape(NV * PX * PY, CZ)
        for side, first in ((0, CY - 3), (1, 0)):
            for j in range(3):
                for half in range(2):
                    start = (v * PX + 3 + 8 * half) * PY + Y0 + first + j
                    sy[step, side, v, pl.ds(j * CX + 8 * half, 8)] = flat[pl.ds(start, 8, PY)]

    def interior(step):
        g = (g0, g1)[step]

        def body(v, carry):
            if step == 0:
                flow_in(v).wait()
                pack_faces(0, v)
            mid = g[v, 3 : 3 + CX, Y0 : Y0 + CY]
            total = mid * CENTER
            for j in OFFSETS:
                total = total + g[v, 3 + j : 3 + j + CX, Y0 : Y0 + CY] * tap(0, j)
            for j in OFFSETS:
                total = total + g[v, 3 : 3 + CX, Y0 + j : Y0 + CY + j] * tap(1, j)
            z_part = three_term(mid.reshape(CX * CY, CZ), along_z[...])
            res[pl.ds(v * CX, CX)] = total + z_part.reshape(CX, CY, CZ)
            return carry

        lax.fori_loop(0, NV, body, 0)

    interior(0)

    def exchange(src, dst, phase):
        for px, py in others():
            pltpu.make_async_remote_copy(
                src_ref=src.at[pl.ds(px * GY + py, 1)], dst_ref=dst.at[pl.ds(me, 1)],
                send_sem=a2a_send.at[phase], recv_sem=a2a_recv.at[phase],
                device_id=(px, py), device_id_type=MESH,
            ).start()
        dst[pl.ds(me, 1)] = src[pl.ds(me, 1)]

    def exchange_wait(buf, sem):
        part = buf.at[pl.ds(0, DEVICES - 1)]
        pltpu.make_async_copy(part, part, sem).wait()

    pl.semaphore_wait(barrier, DEVICES - 1)
    for side in range(4):
        @pl.when(sends[side])
        def _():
            face(0, side).start()
    exchange(a1, c1, 0)

    flat_res = res.reshape(NV * CX * CY, CZ)

    def add_halo(step, v):
        for r in range(3):
            low = res[v * CX + r]
            high = res[v * CX + CX - 1 - r]
            for j in range(-3, -r):
                low = low + hx[step, 0, v, r + j + 3] * tap(0, j)
                high = high + hx[step, 1, v, -r - 1 - j] * tap(0, -j)
            res[v * CX + r] = low
            res[v * CX + CX - 1 - r] = high
        for r in range(3):
            for half in range(2):
                start = (v * CX + 8 * half) * CY
                at_low = pl.ds(start + r, 8, CY)
                at_high = pl.ds(start + CY - 1 - r, 8, CY)
                low = flat_res[at_low]
                high = flat_res[at_high]
                for j in range(-3, -r):
                    low = low + hy[step, 0, v, pl.ds((r + j + 3) * CX + 8 * half, 8)] * tap(1, j)
                    high = high + hy[step, 1, v, pl.ds((-r - 1 - j) * CX + 8 * half, 8)] * tap(1, -j)
                flat_res[at_low] = low
                flat_res[at_high] = high

    def variable(v):
        return pl.ds(pl.multiple_of(v * CX * CY, CX * CY), CX * CY)

    for side in range(4):
        @pl.when(takes[side])
        def _():
            face(0, side).wait_recv()

    def first_lhs(v, carry):
        add_halo(0, v)
        high, low = split(flat_res[variable(v)])
        lhs[variable(v), 0:CZ] = high
        lhs[variable(v), CZ : 2 * CZ] = low
        lhs[variable(v), 2 * CZ :] = high
        return carry

    lax.fori_loop(0, NV, first_lhs, 0)

    exchange_wait(c1, a2a_recv.at[0])
    table = jnp.transpose(c1[...])
    asked = jnp.concatenate([table[0:32], table[32:64]], axis=1)
    wx = asked[0:8]
    wy = asked[8:16]
    wz = asked[16:24]
    last = asked[24:32]
    block = last[5:6].astype(jnp.int32)
    offset = last[6:7].astype(jnp.int32)
    live = last[7:8]
    row8 = lax.broadcasted_iota(jnp.int32, (8, SLOTS), 0)
    near = jnp.where(row8 < NV, last, 0.0)
    kx = block // 64
    ky = (block // 16) % 4
    kz = block % 16
    weights_z = jnp.concatenate(
        [jnp.where(kz == b, wz, 0.0) for b in range(CZ // 8)], axis=0
    )
    z_high, z_low = split(weights_z)
    wz_rhs[0:CZ] = z_high
    wz_rhs[CZ : 2 * CZ] = z_high
    wz_rhs[2 * CZ :] = z_low
    weights_x = jnp.concatenate([jnp.where(kx == b, wx, 0.0) for b in range(CX // 8)], axis=0)
    weights_y = jnp.concatenate([jnp.where(ky == b, wy, 0.0) for b in range(CY // 8)], axis=0)
    for x in range(CX):
        plane[x * CY : (x + 1) * CY] = weights_x[x : x + 1] * weights_y
    cell = (8 * kx + offset // 64) * CY + 8 * ky + (offset // 8) % 8
    cell = jnp.where(live > 0.5, cell, -1)
    cell_z = 8 * kz + offset % 8
    places = lax.broadcasted_iota(jnp.int32, (CX * CY, SLOTS), 0)
    pick[...] = jnp.where(places == cell, 1.0, 0.0).astype(F32).astype(BF16)
    places_z = lax.broadcasted_iota(jnp.int32, (CZ, SLOTS), 0)
    hot_z = jnp.where(places_z == cell_z, 1.0, 0.0).astype(F32).astype(BF16)
    pzt[:, 0:SLOTS] = hot_z
    pzt[:, SLOTS:] = hot_z
    counts = lax.dot_general(
        pick[...], hot_z, contract_last, preferred_element_type=F32
    )
    recip[...] = 1.0 / (1.0 + counts)

    def relaxed(step, near):
        def body(v, interp):
            if step == 0:
                t = jnp.dot(lhs[variable(v)], wz_rhs[...], preferred_element_type=F32)
            else:
                for side in range(4):
                    @pl.when(takes[side])
                    def _():
                        face(1, side, v).wait_recv()
                add_halo(1, v)
                t = three_term(flat_res[variable(v)], wz_rhs[...])
            here = jnp.sum(t * plane[...], axis=0, keepdims=True)
            return jnp.where(row8 == v, here, interp)

        interp = lax.fori_loop(0, NV, body, jnp.zeros((8, SLOTS), F32))
        return near + relaxation * (interp - near)

    def injected(v, near):
        here = jnp.sum(jnp.where(row8 == v, near, 0.0), axis=0, keepdims=True)
        here = jnp.broadcast_to(here, (16, SLOTS))
        high, low = split(here)
        hot = pick[...].reshape(CX * CY // 16, 16, SLOTS)
        left = jnp.concatenate(
            [
                (hot * high[None]).reshape(CX * CY, SLOTS),
                (hot * low[None]).reshape(CX * CY, SLOTS),
            ],
            axis=1,
        )
        gained = lax.dot_general(left, pzt[...], contract_last, preferred_element_type=F32)
        return ((flat_res[variable(v)] + gained) * recip[...]).reshape(CX, CY, CZ)

    near = relaxed(0, near)

    def second_faces(v, carry):
        g1[v, 3 : 3 + CX, Y0 : Y0 + CY] = injected(v, near)
        pack_faces(1, v)
        for side in range(4):
            @pl.when(sends[side])
            def _():
                face(1, side, v).start()
        return carry

    lax.fori_loop(0, NV, second_faces, 0)
    interior(1)
    near = relaxed(1, near)

    back = jnp.concatenate(
        [near[:, :DEVICES], near[:, DEVICES:], jnp.zeros((DEVICES - 16, DEVICES), F32)], axis=0
    )
    d1[...] = jnp.transpose(back)
    exchange(d1, fin, 1)

    def last_injection(v, carry):
        flow_out[v] = injected(v, near)
        return carry

    lax.fori_loop(0, NV, last_injection, 0)

    exchange_wait(a1, a2a_send.at[0])
    for side in range(4):
        @pl.when(sends[side])
        def _():
            face(0, side).wait_send()

    def drain(v, carry):
        for side in range(4):
            @pl.when(sends[side])
            def _():
                face(1, side, v).wait_send()
        return carry

    lax.fori_loop(0, NV, drain, 0)
    exchange_wait(d1, a2a_send.at[1])
    exchange_wait(fin, a2a_recv.at[1])
    returned = jnp.transpose(fin[...])
    served = jnp.dot(
        returned[0:8], ohot[0], precision=HIGHEST, preferred_element_type=F32
    ) + jnp.dot(returned[8:16], ohot[1], precision=HIGHEST, preferred_element_type=F32)
    near_out[...] = served[0:NV]


def hand_over(flow_vmem, near_vmem, flow_out, near_out, sems):
    copies = [
        pltpu.make_async_copy(flow_vmem, flow_out, sems.at[0]),
        pltpu.make_async_copy(near_vmem, near_out, sems.at[1]),
    ]
    for copy in copies:
        copy.start()
    for copy in copies:
        copy.wait()


def shards(flow, near, donor_owner, donor_block, recv_offset, weights):
    hbm = pl.BlockSpec(memory_space=pltpu.HBM)
    whole = pl.BlockSpec(memory_space=pltpu.VMEM)
    vmem = pltpu.VMEM
    dma = pltpu.SemaphoreType.DMA
    operands = (
        flow,
        near,
        donor_owner.reshape(1, FR),
        donor_block.reshape(1, FR),
        recv_offset.reshape(1, FR),
        weights.reshape(24, FR),
    )
    flow, near = pl.pallas_call(
        kernel,
        out_shape=(vmem((NV, CX, CY, CZ), F32), vmem((NV, FR), F32)),
        in_specs=[hbm] * 6,
        out_specs=(whole, whole),
        scratch_shapes=[
            vmem((NV, PX, PY, CZ), F32),
            vmem((NV, PX, PY, CZ), F32),
            vmem((NV * CX, CY, CZ), F32),
            vmem((STEPS, 2, NV, 3, CY, CZ), F32),
            vmem((STEPS, 2, NV, 3 * CX, CZ), F32),
            vmem((STEPS, 2, NV, 3 * CX, CZ), F32),
            vmem((NV, FR), F32),
            vmem((1, FR), jnp.int32),
            vmem((1, FR), jnp.int32),
            vmem((1, FR), jnp.int32),
            vmem((24, FR), F32),
            vmem((DEVICES, 128), F32),
            vmem((DEVICES, 128), F32),
            vmem((DEVICES, 128), F32),
            vmem((DEVICES, 128), F32),
            vmem((2, DEVICES, FR), F32),
            vmem((3 * CZ, CZ), BF16),
            vmem((NV * CX * CY, 3 * CZ), BF16),
            vmem((3 * CZ, SLOTS), BF16),
            vmem((CX * CY, SLOTS), F32),
            vmem((CX * CY, SLOTS), BF16),
            vmem((CZ, 2 * SLOTS), BF16),
            vmem((CX * CY, CZ), F32),
            dma((NV,)),
            dma((5,)),
            dma((4,)),
            dma((4,)),
            dma((NV, 4)),
            dma((NV, 4)),
            dma((2,)),
            dma((2,)),
        ],
        compiler_params=pltpu.CompilerParams(
            collective_id=0, has_side_effects=True, vmem_limit_bytes=40 * 1024 * 1024
        ),
        cost_estimate=pl.CostEstimate(
            flops=2 * STEPS * 20 * NV * CX * CY * CZ,
            bytes_accessed=2 * 4 * NV * CX * CY * CZ,
            transcendentals=0,
        ),
        name="rotor_wake_steps",
    )(*[pltpu.with_memory_space_constraint(operand, pltpu.HBM) for operand in operands])
    return pl.pallas_call(
        hand_over,
        out_shape=(
            jax.ShapeDtypeStruct((NV, CX, CY, CZ), F32),
            jax.ShapeDtypeStruct((NV, FR), F32),
        ),
        in_specs=[whole, whole],
        out_specs=(hbm, hbm),
        scratch_shapes=[dma((2,))],
        name="hand_over",
    )(
        pltpu.with_memory_space_constraint(flow, pltpu.VMEM),
        pltpu.with_memory_space_constraint(near, pltpu.VMEM),
    )


def solution(mesh):
    in_specs = (
        P(None, "gx", "gy", None),
        P(None, ("gx", "gy")),
        P(("gx", "gy"), None),
        P(("gx", "gy")),
        P(("gx", "gy")),
        P(None, None, ("gx", "gy")),
    )
    out_specs = (P(None, "gx", "gy", None), P(None, ("gx", "gy")))
    return jax.shard_map(shards, mesh=mesh, in_specs=in_specs, out_specs=out_specs, check_vma=False)
```

```python
import itertools

import jax
import jax.numpy as jnp
from jax import lax
from jax.experimental import pallas as pl
from jax.experimental.pallas import tpu as pltpu
from jax.sharding import PartitionSpec as P

STEPS = 2
NV = 5
CX = 16
CY = 32
CZ = 128
FR = 128
GX = 8
GY = 16
DEVICES = GX * GY
SLOTS = 2 * DEVICES
PX = CX + 6
PY = CY + 16
Y0 = 8

second_taps = (1.0 / 90, -3.0 / 20, 3.0 / 2, -49.0 / 18, 3.0 / 2, -3.0 / 20, 1.0 / 90)
first_taps = (-1.0 / 60, 3.0 / 20, -3.0 / 4, 0.0, 3.0 / 4, -3.0 / 20, 1.0 / 60)
diffusion = 0.05
velocity = (0.6, -0.5, 0.4)
relaxation = 0.6

TAPS = [
    [diffusion * second_taps[o] - velocity[d] * first_taps[o] for o in range(7)] for d in range(3)
]
CENTER = 1.0 + sum(TAPS[d][3] for d in range(3))
OFFSETS = (-3, -2, -1, 1, 2, 3)
HIGHEST = lax.Precision.HIGHEST
MESH = pl.DeviceIdType.MESH
BF16 = jnp.bfloat16
F32 = jnp.float32


OTHERS = sorted(
    itertools.product(range(4), range(2), range(4), range(4)),
    key=lambda o: -10 * sum(min(o[i], 4 - o[i]) for i in (0, 2, 3)) - o[1],
)[:-1]


def tap(dim, j):
    return TAPS[dim][j + 3]


def split(value):
    high = value.astype(BF16)
    low = (value - high.astype(F32)).astype(BF16)
    return high, low


def three_term(values, right):
    high, low = split(values)
    return jnp.dot(
        jnp.concatenate([high, low, high], axis=1), right, preferred_element_type=F32
    )


def kernel(
    flow_hbm, near_hbm, owner_hbm, block_hbm, offset_hbm, weights_hbm,
    flow_out, near_out,
    g0, g1, res, hx, hy, sy,
    near_in, owner_in, block_in, offset_in, weights_in,
    a1, c1, d1, fin,
    ohot, along_z, lhs, wz_rhs, plane, pick, pzt, recip,
    in_sem, small_sem, first_send, first_recv, halo_send, halo_recv, a2a_send, a2a_recv,
):
    gx = lax.axis_index("gx")
    gy = lax.axis_index("gy")
    me = gx * GY + gy
    chip_x, core = gx // 2, lax.rem(gx, 2)
    chip_z, chip_y = gy // 4, lax.rem(gy, 4)

    def others():
        for dx, dc, dz, dy in OTHERS:
            yield (
                lax.rem(chip_x + dx, 4) * 2 + lax.rem(core + dc, 2),
                lax.rem(chip_z + dz, 4) * 4 + lax.rem(chip_y + dy, 4),
            )

    barrier = pltpu.get_barrier_semaphore()
    peers = list(others())

    for peer in peers:
        pl.semaphore_signal(barrier, inc=1, device_id=peer, device_id_type=MESH)

    small = [
        pltpu.make_async_copy(src, dst, small_sem.at[i])
        for i, (src, dst) in enumerate(
            (
                (owner_hbm, owner_in),
                (block_hbm, block_in),
                (offset_hbm, offset_in),
                (near_hbm, near_in),
                (weights_hbm, weights_in),
            )
        )
    ]
    for copy in small:
        copy.start()

    def flow_in(v):
        return pltpu.make_async_copy(
            flow_hbm.at[v], g0.at[v, pl.ds(3, CX), pl.ds(Y0, CY)], in_sem.at[v]
        )

    for v in range(NV):
        flow_in(v).start()

    def clear(v, carry):
        for g in (g0, g1):
            g[v, 0:3, Y0 : Y0 + CY] = jnp.zeros((3, CY, CZ), F32)
            g[v, PX - 3 : PX, Y0 : Y0 + CY] = jnp.zeros((3, CY, CZ), F32)
            g[v, 3 : PX - 3, 0:Y0] = jnp.zeros((CX, Y0, CZ), F32)
            g[v, 3 : PX - 3, Y0 + CY : PY] = jnp.zeros((CX, PY - Y0 - CY, CZ), F32)
        return carry

    lax.fori_loop(0, NV, clear, 0)

    z_from = lax.broadcasted_iota(jnp.int32, (CZ, CZ), 0)
    z_to = lax.broadcasted_iota(jnp.int32, (CZ, CZ), 1)
    band = jnp.zeros((CZ, CZ), F32)
    for j in OFFSETS:
        band = jnp.where(z_from - z_to == j, tap(2, j), band)
    band_high, band_low = split(band)
    along_z[0:CZ] = band_high
    along_z[CZ : 2 * CZ] = band_high
    along_z[2 * CZ :] = band_low

    for copy in small:
        copy.wait()
    row = lax.broadcasted_iota(jnp.int32, (FR, FR), 0)
    col = lax.broadcasted_iota(jnp.int32, (FR, FR), 1)
    owner_wide = jnp.broadcast_to(owner_in[...], (FR, FR))
    owner_tall = jnp.transpose(owner_wide)
    earlier = jnp.where((owner_wide == owner_tall) & (row < col), 1.0, 0.0).astype(F32)
    rank = jnp.sum(earlier, axis=0, keepdims=True)
    mine = owner_wide == row
    ohot[0] = jnp.where(mine & (rank < 0.5), 1.0, 0.0).astype(F32)
    ohot[1] = jnp.where(mine & (rank > 0.5), 1.0, 0.0).astype(F32)
    payload = jnp.concatenate(
        [
            weights_in[...],
            near_in[...],
            block_in[...].astype(F32),
            offset_in[...].astype(F32),
            jnp.ones((1, FR), F32),
        ],
        axis=0,
    )
    nothing = jnp.zeros((32, FR), F32)
    blank = jnp.zeros((64, FR), F32)
    contract_last = (((1,), (1,)), ((), ()))
    a1[...] = lax.dot_general(
        ohot[0], jnp.concatenate([payload, nothing, blank], axis=0), contract_last,
        precision=HIGHEST, preferred_element_type=F32,
    ) + lax.dot_general(
        ohot[1], jnp.concatenate([nothing, payload, blank], axis=0), contract_last,
        precision=HIGHEST, preferred_element_type=F32,
    )

    targets = ((gx + 1, gy), (gx - 1, gy), (gx, gy + 1), (gx, gy - 1))
    sends = (gx < GX - 1, gx > 0, gy < GY - 1, gy > 0)
    takes = (gx > 0, gx < GX - 1, gy > 0, gy < GY - 1)

    def face(step, side, v=None):
        g = (g0, g1)[step]
        if side < 2:
            layers = pl.ds(CX if side == 0 else 3, 3)
            if v is None:
                src, dst = g.at[:, layers, pl.ds(Y0, CY)], hx.at[step, side]
            else:
                src, dst = g.at[v, layers, pl.ds(Y0, CY)], hx.at[step, side, v]
        elif v is None:
            src, dst = sy.at[step, side - 2], hy.at[step, side - 2]
        else:
            src, dst = sy.at[step, side - 2, v], hy.at[step, side - 2, v]
        return pltpu.make_async_remote_copy(
            src_ref=src, dst_ref=dst,
            send_sem=first_send.at[side] if v is None else halo_send.at[v, side],
            recv_sem=first_recv.at[side] if v is None else halo_recv.at[v, side],
            device_id=targets[side], device_id_type=MESH,
        )

    for side in range(4):
        @pl.when(jnp.logical_not(takes[side]))
        def _():
            halo = (hx, hx, hy, hy)[side]
            for step in range(STEPS):
                halo[step, side % 2] = jnp.zeros(halo.shape[2:], F32)

    def pack_faces(step, v):
        flat = (g0, g1)[step].reshape(NV * PX * PY, CZ)
        for side, first in ((0, CY - 3), (1, 0)):
            for j in range(3):
                for half in range(2):
                    start = (v * PX + 3 + 8 * half) * PY + Y0 + first + j
                    sy[step, side, v, pl.ds(j * CX + 8 * half, 8)] = flat[pl.ds(start, 8, PY)]

    def interior(step):
        g = (g0, g1)[step]

        def body(v, carry):
            mid = g[v, 3 : 3 + CX, Y0 : Y0 + CY]
            total = mid * CENTER
            for j in OFFSETS:
                total = total + g[v, 3 + j : 3 + j + CX, Y0 : Y0 + CY] * tap(0, j)
            for j in OFFSETS:
                total = total + g[v, 3 : 3 + CX, Y0 + j : Y0 + CY + j] * tap(1, j)
            z_part = three_term(mid.reshape(CX * CY, CZ), along_z[...])
            res[pl.ds(v * CX, CX)] = total + z_part.reshape(CX, CY, CZ)
            return carry

        lax.fori_loop(0, NV, body, 0)

    def exchange(src, dst, phase):
        for px, py in peers:
            pltpu.make_async_remote_copy(
                src_ref=src.at[pl.ds(px * GY + py, 1)], dst_ref=dst.at[pl.ds(me, 1)],
                send_sem=a2a_send.at[phase], recv_sem=a2a_recv.at[phase],
                device_id=(px, py), device_id_type=MESH,
            ).start()

    def exchange_wait(buf, sem):
        part = buf.at[pl.ds(0, DEVICES - 1)]
        pltpu.make_async_copy(part, part, sem).wait()

    def first_faces(v, carry):
        flow_in(v).wait()
        pack_faces(0, v)
        return carry

    lax.fori_loop(0, NV, first_faces, 0)
    c1[pl.ds(me, 1)] = a1[pl.ds(me, 1)]
    pl.semaphore_wait(barrier, DEVICES - 1)
    exchange(a1, c1, 0)
    for side in range(4):
        @pl.when(sends[side])
        def _():
            face(0, side).start()
    interior(0)

    flat_res = res.reshape(NV * CX * CY, CZ)

    def add_halo(step, v):
        for r in range(3):
            low = res[v * CX + r]
            high = res[v * CX + CX - 1 - r]
            for j in range(-3, -r):
                low = low + hx[step, 0, v, r + j + 3] * tap(0, j)
                high = high + hx[step, 1, v, -r - 1 - j] * tap(0, -j)
            res[v * CX + r] = low
            res[v * CX + CX - 1 - r] = high
        for r in range(3):
            for half in range(2):
                start = (v * CX + 8 * half) * CY
                at_low = pl.ds(start + r, 8, CY)
                at_high = pl.ds(start + CY - 1 - r, 8, CY)
                low = flat_res[at_low]
                high = flat_res[at_high]
                for j in range(-3, -r):
                    low = low + hy[step, 0, v, pl.ds((r + j + 3) * CX + 8 * half, 8)] * tap(1, j)
                    high = high + hy[step, 1, v, pl.ds((-r - 1 - j) * CX + 8 * half, 8)] * tap(1, -j)
                flat_res[at_low] = low
                flat_res[at_high] = high

    def variable(v):
        return pl.ds(pl.multiple_of(v * CX * CY, CX * CY), CX * CY)

    for side in range(4):
        @pl.when(takes[side])
        def _():
            face(0, side).wait_recv()

    def first_lhs(v, carry):
        add_halo(0, v)
        high, low = split(flat_res[variable(v)])
        lhs[variable(v), 0:CZ] = high
        lhs[variable(v), CZ : 2 * CZ] = low
        lhs[variable(v), 2 * CZ :] = high
        return carry

    lax.fori_loop(0, NV, first_lhs, 0)

    exchange_wait(c1, a2a_recv.at[0])
    table = jnp.transpose(c1[...])
    asked = jnp.concatenate([table[0:32], table[32:64]], axis=1)
    wx = asked[0:8]
    wy = asked[8:16]
    wz = asked[16:24]
    last = asked[24:32]
    block = last[5:6].astype(jnp.int32)
    offset = last[6:7].astype(jnp.int32)
    live = last[7:8]
    row8 = lax.broadcasted_iota(jnp.int32, (8, SLOTS), 0)
    near = jnp.where(row8 < NV, last, 0.0)
    kx = block // 64
    ky = (block // 16) % 4
    kz = block % 16
    weights_z = jnp.concatenate(
        [jnp.where(kz == b, wz, 0.0) for b in range(CZ // 8)], axis=0
    )
    z_high, z_low = split(weights_z)
    wz_rhs[0:CZ] = z_high
    wz_rhs[CZ : 2 * CZ] = z_high
    wz_rhs[2 * CZ :] = z_low
    weights_x = jnp.concatenate([jnp.where(kx == b, wx, 0.0) for b in range(CX // 8)], axis=0)
    weights_y = jnp.concatenate([jnp.where(ky == b, wy, 0.0) for b in range(CY // 8)], axis=0)
    for x in range(CX):
        plane[x * CY : (x + 1) * CY] = weights_x[x : x + 1] * weights_y
    cell = (8 * kx + offset // 64) * CY + 8 * ky + (offset // 8) % 8
    cell = jnp.where(live > 0.5, cell, -1)
    cell_z = 8 * kz + offset % 8
    places = lax.broadcasted_iota(jnp.int32, (CX * CY, SLOTS), 0)
    pick[...] = jnp.where(places == cell, 1.0, 0.0).astype(F32).astype(BF16)
    places_z = lax.broadcasted_iota(jnp.int32, (CZ, SLOTS), 0)
    hot_z = jnp.where(places_z == cell_z, 1.0, 0.0).astype(F32).astype(BF16)
    pzt[:, 0:SLOTS] = hot_z
    pzt[:, SLOTS:] = hot_z
    counts = lax.dot_general(
        pick[...], hot_z, contract_last, preferred_element_type=F32
    )
    recip[...] = 1.0 / (1.0 + counts)

    def relaxed(step, near):
        def body(v, interp):
            if step == 0:
                t = jnp.dot(lhs[variable(v)], wz_rhs[...], preferred_element_type=F32)
            else:
                for side in range(4):
                    @pl.when(takes[side])
                    def _():
                        face(1, side, v).wait_recv()
                add_halo(1, v)
                t = three_term(flat_res[variable(v)], wz_rhs[...])
            here = jnp.sum(t * plane[...], axis=0, keepdims=True)
            return jnp.where(row8 == v, here, interp)

        interp = lax.fori_loop(0, NV, body, jnp.zeros((8, SLOTS), F32), unroll=True)
        return near + relaxation * (interp - near)

    def injected(v, near):
        here = jnp.sum(jnp.where(row8 == v, near, 0.0), axis=0, keepdims=True)
        here = jnp.broadcast_to(here, (16, SLOTS))
        high, low = split(here)
        hot = pick[...].reshape(CX * CY // 16, 16, SLOTS)
        left = jnp.concatenate(
            [
                (hot * high[None]).reshape(CX * CY, SLOTS),
                (hot * low[None]).reshape(CX * CY, SLOTS),
            ],
            axis=1,
        )
        gained = lax.dot_general(left, pzt[...], contract_last, preferred_element_type=F32)
        return ((flat_res[variable(v)] + gained) * recip[...]).reshape(CX, CY, CZ)

    near = relaxed(0, near)

    def second_faces(v, carry):
        g1[v, 3 : 3 + CX, Y0 : Y0 + CY] = injected(v, near)
        pack_faces(1, v)
        for side in range(4):
            @pl.when(sends[side])
            def _():
                face(1, side, v).start()
        return carry

    lax.fori_loop(0, NV, second_faces, 0, unroll=True)
    interior(1)
    near = relaxed(1, near)

    back = jnp.concatenate(
        [near[:, :DEVICES], near[:, DEVICES:], jnp.zeros((DEVICES - 16, DEVICES), F32)], axis=0
    )
    d1[...] = jnp.transpose(back)
    exchange(d1, fin, 1)
    fin[pl.ds(me, 1)] = d1[pl.ds(me, 1)]

    def last_injection(v, carry):
        flow_out[v] = injected(v, near)
        return carry

    lax.fori_loop(0, NV, last_injection, 0, unroll=True)

    exchange_wait(a1, a2a_send.at[0])
    for side in range(4):
        @pl.when(sends[side])
        def _():
            face(0, side).wait_send()

    def drain(v, carry):
        for side in range(4):
            @pl.when(sends[side])
            def _():
                face(1, side, v).wait_send()
        return carry

    lax.fori_loop(0, NV, drain, 0)
    exchange_wait(d1, a2a_send.at[1])
    exchange_wait(fin, a2a_recv.at[1])
    returned = jnp.transpose(fin[...])
    served = jnp.dot(
        returned[0:8], ohot[0], precision=HIGHEST, preferred_element_type=F32
    ) + jnp.dot(returned[8:16], ohot[1], precision=HIGHEST, preferred_element_type=F32)
    near_out[...] = served[0:NV]


def hand_over(flow_vmem, near_vmem, flow_out, near_out, sems):
    copies = [
        pltpu.make_async_copy(flow_vmem, flow_out, sems.at[0]),
        pltpu.make_async_copy(near_vmem, near_out, sems.at[1]),
    ]
    for copy in copies:
        copy.start()
    for copy in copies:
        copy.wait()


def shards(flow, near, donor_owner, donor_block, recv_offset, weights):
    hbm = pl.BlockSpec(memory_space=pltpu.HBM)
    whole = pl.BlockSpec(memory_space=pltpu.VMEM)
    vmem = pltpu.VMEM
    dma = pltpu.SemaphoreType.DMA
    operands = (
        flow,
        near,
        donor_owner.reshape(1, FR),
        donor_block.reshape(1, FR),
        recv_offset.reshape(1, FR),
        weights.reshape(24, FR),
    )
    flow, near = pl.pallas_call(
        kernel,
        out_shape=(vmem((NV, CX, CY, CZ), F32), vmem((NV, FR), F32)),
        in_specs=[hbm] * 6,
        out_specs=(whole, whole),
        scratch_shapes=[
            vmem((NV, PX, PY, CZ), F32),
            vmem((NV, PX, PY, CZ), F32),
            vmem((NV * CX, CY, CZ), F32),
            vmem((STEPS, 2, NV, 3, CY, CZ), F32),
            vmem((STEPS, 2, NV, 3 * CX, CZ), F32),
            vmem((STEPS, 2, NV, 3 * CX, CZ), F32),
            vmem((NV, FR), F32),
            vmem((1, FR), jnp.int32),
            vmem((1, FR), jnp.int32),
            vmem((1, FR), jnp.int32),
            vmem((24, FR), F32),
            vmem((DEVICES, 128), F32),
            vmem((DEVICES, 128), F32),
            vmem((DEVICES, 128), F32),
            vmem((DEVICES, 128), F32),
            vmem((2, DEVICES, FR), F32),
            vmem((3 * CZ, CZ), BF16),
            vmem((NV * CX * CY, 3 * CZ), BF16),
            vmem((3 * CZ, SLOTS), BF16),
            vmem((CX * CY, SLOTS), F32),
            vmem((CX * CY, SLOTS), BF16),
            vmem((CZ, 2 * SLOTS), BF16),
            vmem((CX * CY, CZ), F32),
            dma((NV,)),
            dma((5,)),
            dma((4,)),
            dma((4,)),
            dma((NV, 4)),
            dma((NV, 4)),
            dma((2,)),
            dma((2,)),
        ],
        compiler_params=pltpu.CompilerParams(
            collective_id=0, has_side_effects=True, vmem_limit_bytes=40 * 1024 * 1024
        ),
        cost_estimate=pl.CostEstimate(
            flops=2 * STEPS * 20 * NV * CX * CY * CZ,
            bytes_accessed=2 * 4 * NV * CX * CY * CZ,
            transcendentals=0,
        ),
        name="rotor_wake_steps",
    )(*[pltpu.with_memory_space_constraint(operand, pltpu.HBM) for operand in operands])
    return pl.pallas_call(
        hand_over,
        out_shape=(
            jax.ShapeDtypeStruct((NV, CX, CY, CZ), F32),
            jax.ShapeDtypeStruct((NV, FR), F32),
        ),
        in_specs=[whole, whole],
        out_specs=(hbm, hbm),
        scratch_shapes=[dma((2,))],
        name="hand_over",
    )(
        pltpu.with_memory_space_constraint(flow, pltpu.VMEM),
        pltpu.with_memory_space_constraint(near, pltpu.VMEM),
    )


def solution(mesh):
    in_specs = (
        P(None, "gx", "gy", None),
        P(None, ("gx", "gy")),
        P(("gx", "gy"), None),
        P(("gx", "gy")),
        P(("gx", "gy")),
        P(None, None, ("gx", "gy")),
    )
    out_specs = (P(None, "gx", "gy", None), P(None, ("gx", "gy")))
    return jax.shard_map(shards, mesh=mesh, in_specs=in_specs, out_specs=out_specs, check_vma=False)
```

```python
import itertools

import jax
import jax.numpy as jnp
from jax import lax
from jax.experimental import pallas as pl
from jax.experimental.pallas import tpu as pltpu
from jax.sharding import PartitionSpec as P

STEPS = 2
NV = 5
CX = 16
CY = 32
CZ = 128
FR = 128
GX = 8
GY = 16
DEVICES = GX * GY
SLOTS = 2 * DEVICES
PX = CX + 6
PY = CY + 16
Y0 = 8

second_taps = (1.0 / 90, -3.0 / 20, 3.0 / 2, -49.0 / 18, 3.0 / 2, -3.0 / 20, 1.0 / 90)
first_taps = (-1.0 / 60, 3.0 / 20, -3.0 / 4, 0.0, 3.0 / 4, -3.0 / 20, 1.0 / 60)
diffusion = 0.05
velocity = (0.6, -0.5, 0.4)
relaxation = 0.6

TAPS = [
    [diffusion * second_taps[o] - velocity[d] * first_taps[o] for o in range(7)] for d in range(3)
]
CENTER = 1.0 + sum(TAPS[d][3] for d in range(3))
OFFSETS = (-3, -2, -1, 1, 2, 3)
HIGHEST = lax.Precision.HIGHEST
MESH = pl.DeviceIdType.MESH
BF16 = jnp.bfloat16
F32 = jnp.float32


OTHERS = sorted(
    itertools.product(range(4), range(2), range(4), range(4)),
    key=lambda o: -10 * sum(min(o[i], 4 - o[i]) for i in (0, 2, 3)) - o[1],
)[:-1]


def tap(dim, j):
    return TAPS[dim][j + 3]


def split(value):
    high = value.astype(BF16)
    low = (value - high.astype(F32)).astype(BF16)
    return high, low


def three_term(values, right):
    high, low = split(values)
    return jnp.dot(
        jnp.concatenate([high, low, high], axis=1), right, preferred_element_type=F32
    )


def kernel(
    flow_hbm, near_hbm, owner_hbm, block_hbm, offset_hbm, weights_hbm,
    flow_out, near_out,
    g0, g1, res, hx, hy, sy,
    near_in, owner_in, block_in, offset_in, weights_in,
    a1, b1, bt, c1, d1, fin,
    ohot, band_z, lhs, wz_rhs, plane, pick, pzt, recip,
    in_sem, small_sem, first_send, first_recv, halo_send, halo_recv, row_send, row_recv, vouched,
):
    gx = lax.axis_index("gx")
    gy = lax.axis_index("gy")
    me = gx * GY + gy
    chip_x, core = gx // 2, lax.rem(gx, 2)
    chip_z, chip_y = gy // 4, lax.rem(gy, 4)

    def others():
        for dx, dc, dz, dy in OTHERS:
            yield (
                lax.rem(chip_x + dx, 4) * 2 + lax.rem(core + dc, 2),
                lax.rem(chip_z + dz, 4) * 4 + lax.rem(chip_y + dy, 4),
            )

    along_x = [(lax.rem(gx + k, GX), gy) for k in range(1, GX)]
    along_y = [(gx, chip_z * 4 + lax.rem(chip_y + k, 4)) for k in range(1, 4)]
    along_z = [(gx, lax.rem(gy + 4 * k, GY)) for k in range(1, 4)]
    plane_yz = [(gx, lax.rem(gy + k, GY)) for k in range(1, GY)]
    barrier = pltpu.get_barrier_semaphore()
    for peer in along_y + along_z + along_x:
        pl.semaphore_signal(barrier, inc=1, device_id=peer, device_id_type=MESH)
    after = (chip_y == 3) & (gy < GY - 1)
    before = (chip_y == 0) & (gy > 0)

    @pl.when(after)
    def _():
        pl.semaphore_signal(barrier, inc=1, device_id=(gx, gy + 1), device_id_type=MESH)

    @pl.when(before)
    def _():
        pl.semaphore_signal(barrier, inc=1, device_id=(gx, gy - 1), device_id_type=MESH)

    greeted = GX + 5 + after.astype(jnp.int32) + before.astype(jnp.int32)

    small = [
        pltpu.make_async_copy(src, dst, small_sem.at[i])
        for i, (src, dst) in enumerate(
            (
                (owner_hbm, owner_in),
                (block_hbm, block_in),
                (offset_hbm, offset_in),
                (near_hbm, near_in),
                (weights_hbm, weights_in),
            )
        )
    ]
    for copy in small:
        copy.start()

    def flow_in(v):
        return pltpu.make_async_copy(
            flow_hbm.at[v], g0.at[v, pl.ds(3, CX), pl.ds(Y0, CY)], in_sem.at[v]
        )

    for v in range(NV):
        flow_in(v).start()

    def clear(v, carry):
        for g in (g0, g1):
            g[v, 0:3, Y0 : Y0 + CY] = jnp.zeros((3, CY, CZ), F32)
            g[v, PX - 3 : PX, Y0 : Y0 + CY] = jnp.zeros((3, CY, CZ), F32)
            g[v, 3 : PX - 3, 0:Y0] = jnp.zeros((CX, Y0, CZ), F32)
            g[v, 3 : PX - 3, Y0 + CY : PY] = jnp.zeros((CX, PY - Y0 - CY, CZ), F32)
        return carry

    lax.fori_loop(0, NV, clear, 0)

    z_from = lax.broadcasted_iota(jnp.int32, (CZ, CZ), 0)
    z_to = lax.broadcasted_iota(jnp.int32, (CZ, CZ), 1)
    band = jnp.zeros((CZ, CZ), F32)
    for j in OFFSETS:
        band = jnp.where(z_from - z_to == j, tap(2, j), band)
    band_high, band_low = split(band)
    band_z[0:CZ] = band_high
    band_z[CZ : 2 * CZ] = band_high
    band_z[2 * CZ :] = band_low

    for copy in small:
        copy.wait()
    row = lax.broadcasted_iota(jnp.int32, (FR, FR), 0)
    col = lax.broadcasted_iota(jnp.int32, (FR, FR), 1)
    owner_wide = jnp.broadcast_to(owner_in[...], (FR, FR))
    owner_tall = jnp.transpose(owner_wide)
    earlier = jnp.where((owner_wide == owner_tall) & (row < col), 1.0, 0.0).astype(F32)
    rank = jnp.sum(earlier, axis=0, keepdims=True)
    mine = owner_wide == row
    ohot[0] = jnp.where(mine & (rank < 0.5), 1.0, 0.0).astype(F32)
    ohot[1] = jnp.where(mine & (rank > 0.5), 1.0, 0.0).astype(F32)
    payload = jnp.concatenate(
        [
            weights_in[...],
            near_in[...],
            block_in[...].astype(F32),
            offset_in[...].astype(F32),
            jnp.ones((1, FR), F32),
        ],
        axis=0,
    )
    nothing = jnp.zeros((32, FR), F32)
    blank = jnp.zeros((64, FR), F32)
    contract_last = (((1,), (1,)), ((), ()))
    a1[...] = lax.dot_general(
        ohot[0], jnp.concatenate([payload, nothing, blank], axis=0), contract_last,
        precision=HIGHEST, preferred_element_type=F32,
    ) + lax.dot_general(
        ohot[1], jnp.concatenate([nothing, payload, blank], axis=0), contract_last,
        precision=HIGHEST, preferred_element_type=F32,
    )

    targets = ((gx + 1, gy), (gx - 1, gy), (gx, gy + 1), (gx, gy - 1))
    sends = (gx < GX - 1, gx > 0, gy < GY - 1, gy > 0)
    takes = (gx > 0, gx < GX - 1, gy > 0, gy < GY - 1)

    def face(step, side, v=None):
        g = (g0, g1)[step]
        if side < 2:
            layers = pl.ds(CX if side == 0 else 3, 3)
            if v is None:
                src, dst = g.at[:, layers, pl.ds(Y0, CY)], hx.at[step, side]
            else:
                src, dst = g.at[v, layers, pl.ds(Y0, CY)], hx.at[step, side, v]
        elif v is None:
            src, dst = sy.at[step, side - 2], hy.at[step, side - 2]
        else:
            src, dst = sy.at[step, side - 2, v], hy.at[step, side - 2, v]
        return pltpu.make_async_remote_copy(
            src_ref=src, dst_ref=dst,
            send_sem=first_send.at[side] if v is None else halo_send.at[v, side],
            recv_sem=first_recv.at[side] if v is None else halo_recv.at[v, side],
            device_id=targets[side], device_id_type=MESH,
        )

    for side in range(4):
        @pl.when(jnp.logical_not(takes[side]))
        def _():
            halo = (hx, hx, hy, hy)[side]
            for step in range(STEPS):
                halo[step, side % 2] = jnp.zeros(halo.shape[2:], F32)

    def pack_faces(step, v):
        flat = (g0, g1)[step].reshape(NV * PX * PY, CZ)
        for side, first in ((0, CY - 3), (1, 0)):
            for j in range(3):
                for half in range(2):
                    start = (v * PX + 3 + 8 * half) * PY + Y0 + first + j
                    sy[step, side, v, pl.ds(j * CX + 8 * half, 8)] = flat[pl.ds(start, 8, PY)]

    def interior(step):
        g = (g0, g1)[step]

        def body(v, carry):
            mid = g[v, 3 : 3 + CX, Y0 : Y0 + CY]
            total = mid * CENTER
            for j in OFFSETS:
                total = total + g[v, 3 + j : 3 + j + CX, Y0 : Y0 + CY] * tap(0, j)
            for j in OFFSETS:
                total = total + g[v, 3 : 3 + CX, Y0 + j : Y0 + CY + j] * tap(1, j)
            z_part = three_term(mid.reshape(CX * CY, CZ), band_z[...])
            res[pl.ds(v * CX, CX)] = total + z_part.reshape(CX, CY, CZ)
            return carry

        lax.fori_loop(0, NV, body, 0)

    def rows_to(src, source, count, dst, target, phase, peer):
        pltpu.make_async_remote_copy(
            src_ref=src.at[pl.ds(source, count)], dst_ref=dst.at[pl.ds(target, count)],
            send_sem=row_send.at[phase], recv_sem=row_recv.at[phase],
            device_id=peer, device_id_type=MESH,
        ).start()

    def rows_wait(buf, count, sem):
        part = buf.at[pl.ds(0, count)]
        pltpu.make_async_copy(part, part, sem).wait()

    def first_faces(v, carry):
        flow_in(v).wait()
        pack_faces(0, v)
        return carry

    lax.fori_loop(0, NV, first_faces, 0)
    x_rows = pl.ds(pl.multiple_of(gx * GY, GY), GY)
    b1[x_rows] = a1[x_rows]
    pl.semaphore_wait(barrier, greeted)
    for peer in along_x:
        rows_to(a1, pl.multiple_of(peer[0] * GY, GY), GY, b1, pl.multiple_of(gx * GY, GY), 0, peer)
    for peer in along_y:
        pl.semaphore_signal(vouched, inc=1, device_id=peer, device_id_type=MESH)
    for side in range(4):
        @pl.when(sends[side])
        def _():
            face(0, side).start()
    interior(0)
    rows_wait(b1, DEVICES - GY, row_recv.at[0])
    for h in range(GY):
        bt[h * GX : (h + 1) * GX] = b1[pl.ds(h, GX, GY)]
    y_rows = pl.ds(pl.multiple_of(gy * GX, GX), GX)
    c1[y_rows] = bt[y_rows]
    pl.semaphore_wait(vouched, 3)
    for peer in plane_yz:
        rows_to(bt, pl.multiple_of(peer[1] * GX, GX), GX, c1, pl.multiple_of(gy * GX, GX), 1, peer)

    flat_res = res.reshape(NV * CX * CY, CZ)

    def add_halo(step, v):
        for r in range(3):
            low = res[v * CX + r]
            high = res[v * CX + CX - 1 - r]
            for j in range(-3, -r):
                low = low + hx[step, 0, v, r + j + 3] * tap(0, j)
                high = high + hx[step, 1, v, -r - 1 - j] * tap(0, -j)
            res[v * CX + r] = low
            res[v * CX + CX - 1 - r] = high
        for r in range(3):
            for half in range(2):
                start = (v * CX + 8 * half) * CY
                at_low = pl.ds(start + r, 8, CY)
                at_high = pl.ds(start + CY - 1 - r, 8, CY)
                low = flat_res[at_low]
                high = flat_res[at_high]
                for j in range(-3, -r):
                    low = low + hy[step, 0, v, pl.ds((r + j + 3) * CX + 8 * half, 8)] * tap(1, j)
                    high = high + hy[step, 1, v, pl.ds((-r - 1 - j) * CX + 8 * half, 8)] * tap(1, -j)
                flat_res[at_low] = low
                flat_res[at_high] = high

    def variable(v):
        return pl.ds(pl.multiple_of(v * CX * CY, CX * CY), CX * CY)

    for side in range(4):
        @pl.when(takes[side])
        def _():
            face(0, side).wait_recv()

    def first_lhs(v, carry):
        add_halo(0, v)
        high, low = split(flat_res[variable(v)])
        lhs[variable(v), 0:CZ] = high
        lhs[variable(v), CZ : 2 * CZ] = low
        lhs[variable(v), 2 * CZ :] = high
        return carry

    lax.fori_loop(0, NV, first_lhs, 0)

    rows_wait(c1, DEVICES - GX, row_recv.at[1])
    table = jnp.transpose(c1[...])
    asked = jnp.concatenate([table[0:32], table[32:64]], axis=1)
    wx = asked[0:8]
    wy = asked[8:16]
    wz = asked[16:24]
    last = asked[24:32]
    block = last[5:6].astype(jnp.int32)
    offset = last[6:7].astype(jnp.int32)
    live = last[7:8]
    row8 = lax.broadcasted_iota(jnp.int32, (8, SLOTS), 0)
    near = jnp.where(row8 < NV, last, 0.0)
    kx = block // 64
    ky = (block // 16) % 4
    kz = block % 16
    weights_z = jnp.concatenate(
        [jnp.where(kz == b, wz, 0.0) for b in range(CZ // 8)], axis=0
    )
    z_high, z_low = split(weights_z)
    wz_rhs[0:CZ] = z_high
    wz_rhs[CZ : 2 * CZ] = z_high
    wz_rhs[2 * CZ :] = z_low
    weights_x = jnp.concatenate([jnp.where(kx == b, wx, 0.0) for b in range(CX // 8)], axis=0)
    weights_y = jnp.concatenate([jnp.where(ky == b, wy, 0.0) for b in range(CY // 8)], axis=0)
    for x in range(CX):
        plane[x * CY : (x + 1) * CY] = weights_x[x : x + 1] * weights_y
    cell = (8 * kx + offset // 64) * CY + 8 * ky + (offset // 8) % 8
    cell = jnp.where(live > 0.5, cell, -1)
    cell_z = 8 * kz + offset % 8
    places = lax.broadcasted_iota(jnp.int32, (CX * CY, SLOTS), 0)
    pick[...] = jnp.where(places == cell, 1.0, 0.0).astype(F32).astype(BF16)
    places_z = lax.broadcasted_iota(jnp.int32, (CZ, SLOTS), 0)
    hot_z = jnp.where(places_z == cell_z, 1.0, 0.0).astype(F32).astype(BF16)
    pzt[:, 0:SLOTS] = hot_z
    pzt[:, SLOTS:] = hot_z
    counts = lax.dot_general(
        pick[...], hot_z, contract_last, preferred_element_type=F32
    )
    recip[...] = 1.0 / (1.0 + counts)

    def relaxed(step, near):
        def body(v, interp):
            if step == 0:
                t = jnp.dot(lhs[variable(v)], wz_rhs[...], preferred_element_type=F32)
            else:
                for side in range(4):
                    @pl.when(takes[side])
                    def _():
                        face(1, side, v).wait_recv()
                add_halo(1, v)
                t = three_term(flat_res[variable(v)], wz_rhs[...])
            here = jnp.sum(t * plane[...], axis=0, keepdims=True)
            return jnp.where(row8 == v, here, interp)

        interp = lax.fori_loop(0, NV, body, jnp.zeros((8, SLOTS), F32), unroll=True)
        return near + relaxation * (interp - near)

    def injected(v, near):
        here = jnp.sum(jnp.where(row8 == v, near, 0.0), axis=0, keepdims=True)
        here = jnp.broadcast_to(here, (16, SLOTS))
        high, low = split(here)
        hot = pick[...].reshape(CX * CY // 16, 16, SLOTS)
        left = jnp.concatenate(
            [
                (hot * high[None]).reshape(CX * CY, SLOTS),
                (hot * low[None]).reshape(CX * CY, SLOTS),
            ],
            axis=1,
        )
        gained = lax.dot_general(left, pzt[...], contract_last, preferred_element_type=F32)
        return ((flat_res[variable(v)] + gained) * recip[...]).reshape(CX, CY, CZ)

    near = relaxed(0, near)

    def second_faces(v, carry):
        g1[v, 3 : 3 + CX, Y0 : Y0 + CY] = injected(v, near)
        pack_faces(1, v)
        for side in range(4):
            @pl.when(sends[side])
            def _():
                face(1, side, v).start()
        return carry

    lax.fori_loop(0, NV, second_faces, 0, unroll=True)
    interior(1)
    near = relaxed(1, near)

    back = jnp.concatenate(
        [near[:, :DEVICES], near[:, DEVICES:], jnp.zeros((DEVICES - 16, DEVICES), F32)], axis=0
    )
    d1[...] = jnp.transpose(back)
    for px, py in others():
        rows_to(d1, py * GX + px, 1, fin, me, 2, (px, py))
    fin[pl.ds(me, 1)] = d1[pl.ds(gy * GX + gx, 1)]

    def last_injection(v, carry):
        flow_out[v] = injected(v, near)
        return carry

    lax.fori_loop(0, NV, last_injection, 0, unroll=True)

    rows_wait(a1, DEVICES - GY, row_send.at[0])
    rows_wait(bt, DEVICES - GX, row_send.at[1])
    for side in range(4):
        @pl.when(sends[side])
        def _():
            face(0, side).wait_send()

    def drain(v, carry):
        for side in range(4):
            @pl.when(sends[side])
            def _():
                face(1, side, v).wait_send()
        return carry

    lax.fori_loop(0, NV, drain, 0)
    rows_wait(d1, DEVICES - 1, row_send.at[2])
    rows_wait(fin, DEVICES - 1, row_recv.at[2])
    returned = jnp.transpose(fin[...])
    served = jnp.dot(
        returned[0:8], ohot[0], precision=HIGHEST, preferred_element_type=F32
    ) + jnp.dot(returned[8:16], ohot[1], precision=HIGHEST, preferred_element_type=F32)
    near_out[...] = served[0:NV]


def hand_over(flow_vmem, near_vmem, flow_out, near_out, sems):
    copies = [
        pltpu.make_async_copy(flow_vmem, flow_out, sems.at[0]),
        pltpu.make_async_copy(near_vmem, near_out, sems.at[1]),
    ]
    for copy in copies:
        copy.start()
    for copy in copies:
        copy.wait()


def shards(flow, near, donor_owner, donor_block, recv_offset, weights):
    hbm = pl.BlockSpec(memory_space=pltpu.HBM)
    whole = pl.BlockSpec(memory_space=pltpu.VMEM)
    vmem = pltpu.VMEM
    dma = pltpu.SemaphoreType.DMA
    operands = (
        flow,
        near,
        donor_owner.reshape(1, FR),
        donor_block.reshape(1, FR),
        recv_offset.reshape(1, FR),
        weights.reshape(24, FR),
    )
    flow, near = pl.pallas_call(
        kernel,
        out_shape=(vmem((NV, CX, CY, CZ), F32), vmem((NV, FR), F32)),
        in_specs=[hbm] * 6,
        out_specs=(whole, whole),
        scratch_shapes=[
            vmem((NV, PX, PY, CZ), F32),
            vmem((NV, PX, PY, CZ), F32),
            vmem((NV * CX, CY, CZ), F32),
            vmem((STEPS, 2, NV, 3, CY, CZ), F32),
            vmem((STEPS, 2, NV, 3 * CX, CZ), F32),
            vmem((STEPS, 2, NV, 3 * CX, CZ), F32),
            vmem((NV, FR), F32),
            vmem((1, FR), jnp.int32),
            vmem((1, FR), jnp.int32),
            vmem((1, FR), jnp.int32),
            vmem((24, FR), F32),
            vmem((DEVICES, 128), F32),
            vmem((DEVICES, 128), F32),
            vmem((DEVICES, 128), F32),
            vmem((DEVICES, 128), F32),
            vmem((DEVICES, 128), F32),
            vmem((DEVICES, 128), F32),
            vmem((2, DEVICES, FR), F32),
            vmem((3 * CZ, CZ), BF16),
            vmem((NV * CX * CY, 3 * CZ), BF16),
            vmem((3 * CZ, SLOTS), BF16),
            vmem((CX * CY, SLOTS), F32),
            vmem((CX * CY, SLOTS), BF16),
            vmem((CZ, 2 * SLOTS), BF16),
            vmem((CX * CY, CZ), F32),
            dma((NV,)),
            dma((5,)),
            dma((4,)),
            dma((4,)),
            dma((NV, 4)),
            dma((NV, 4)),
            dma((3,)),
            dma((3,)),
            pltpu.SemaphoreType.REGULAR,
        ],
        compiler_params=pltpu.CompilerParams(
            collective_id=0, has_side_effects=True, vmem_limit_bytes=40 * 1024 * 1024
        ),
        cost_estimate=pl.CostEstimate(
            flops=2 * STEPS * 20 * NV * CX * CY * CZ,
            bytes_accessed=2 * 4 * NV * CX * CY * CZ,
            transcendentals=0,
        ),
        name="rotor_wake_steps",
    )(*[pltpu.with_memory_space_constraint(operand, pltpu.HBM) for operand in operands])
    return pl.pallas_call(
        hand_over,
        out_shape=(
            jax.ShapeDtypeStruct((NV, CX, CY, CZ), F32),
            jax.ShapeDtypeStruct((NV, FR), F32),
        ),
        in_specs=[whole, whole],
        out_specs=(hbm, hbm),
        scratch_shapes=[dma((2,))],
        name="hand_over",
    )(
        pltpu.with_memory_space_constraint(flow, pltpu.VMEM),
        pltpu.with_memory_space_constraint(near, pltpu.VMEM),
    )


def solution(mesh):
    in_specs = (
        P(None, "gx", "gy", None),
        P(None, ("gx", "gy")),
        P(("gx", "gy"), None),
        P(("gx", "gy")),
        P(("gx", "gy")),
        P(None, None, ("gx", "gy")),
    )
    out_specs = (P(None, "gx", "gy", None), P(None, ("gx", "gy")))
    return jax.shard_map(shards, mesh=mesh, in_specs=in_specs, out_specs=out_specs, check_vma=False)
```

```python
import itertools

import jax
import jax.numpy as jnp
from jax import lax
from jax.experimental import pallas as pl
from jax.experimental.pallas import tpu as pltpu
from jax.sharding import PartitionSpec as P

STEPS = 2
NV = 5
CX = 16
CY = 32
CZ = 128
FR = 128
GX = 8
GY = 16
DEVICES = GX * GY
SLOTS = 2 * DEVICES
PX = CX + 6
PY = CY + 16
Y0 = 8

second_taps = (1.0 / 90, -3.0 / 20, 3.0 / 2, -49.0 / 18, 3.0 / 2, -3.0 / 20, 1.0 / 90)
first_taps = (-1.0 / 60, 3.0 / 20, -3.0 / 4, 0.0, 3.0 / 4, -3.0 / 20, 1.0 / 60)
diffusion = 0.05
velocity = (0.6, -0.5, 0.4)
relaxation = 0.6

TAPS = [
    [diffusion * second_taps[o] - velocity[d] * first_taps[o] for o in range(7)] for d in range(3)
]
CENTER = 1.0 + sum(TAPS[d][3] for d in range(3))
OFFSETS = (-3, -2, -1, 1, 2, 3)
HIGHEST = lax.Precision.HIGHEST
MESH = pl.DeviceIdType.MESH
BF16 = jnp.bfloat16
F32 = jnp.float32


OTHERS = sorted(
    itertools.product(range(4), range(2), range(4), range(4)),
    key=lambda o: -10 * sum(min(o[i], 4 - o[i]) for i in (0, 2, 3)) - o[1],
)[:-1]


def tap(dim, j):
    return TAPS[dim][j + 3]


def split(value):
    high = value.astype(BF16)
    low = (value - high.astype(F32)).astype(BF16)
    return high, low


def three_term(values, right):
    high, low = split(values)
    return jnp.dot(
        jnp.concatenate([high, low, high], axis=1), right, preferred_element_type=F32
    )


def kernel(
    flow_hbm, near_hbm, owner_hbm, block_hbm, offset_hbm, weights_hbm,
    flow_out, near_out,
    g0, g1, res, hx, hy, sy,
    near_in, owner_in, block_in, offset_in, weights_in,
    a1, b1, bt, c1, d1, fin, table, tables,
    ohot, band_z, lhs, wz_rhs, near_rhs, plane, plane_z, pad_x, pad_y, pad_z, pick, pzt, recip,
    in_sem, small_sem, first_send, first_recv, halo_send, halo_recv, row_send, row_recv, vouched,
    table_send, table_recv,
):
    gx = lax.axis_index("gx")
    gy = lax.axis_index("gy")
    me = gx * GY + gy
    chip_x, core = gx // 2, lax.rem(gx, 2)
    chip_z, chip_y = gy // 4, lax.rem(gy, 4)

    def others():
        for dx, dc, dz, dy in OTHERS:
            yield (
                lax.rem(chip_x + dx, 4) * 2 + lax.rem(core + dc, 2),
                lax.rem(chip_z + dz, 4) * 4 + lax.rem(chip_y + dy, 4),
            )

    along_x = [(lax.rem(gx + k, GX), gy) for k in range(1, GX)]
    along_y = [(gx, chip_z * 4 + lax.rem(chip_y + k, 4)) for k in range(1, 4)]
    along_z = [(gx, lax.rem(gy + 4 * k, GY)) for k in range(1, 4)]
    plane_yz = [(gx, lax.rem(gy + k, GY)) for k in range(1, GY)]
    barrier = pltpu.get_barrier_semaphore()
    for peer in along_y + along_z + along_x:
        pl.semaphore_signal(barrier, inc=1, device_id=peer, device_id_type=MESH)
    after = (chip_y == 3) & (gy < GY - 1)
    before = (chip_y == 0) & (gy > 0)

    @pl.when(after)
    def _():
        pl.semaphore_signal(barrier, inc=1, device_id=(gx, gy + 1), device_id_type=MESH)

    @pl.when(before)
    def _():
        pl.semaphore_signal(barrier, inc=1, device_id=(gx, gy - 1), device_id_type=MESH)

    greeted = GX + 5 + after.astype(jnp.int32) + before.astype(jnp.int32)

    small = [
        pltpu.make_async_copy(src, dst, small_sem.at[i])
        for i, (src, dst) in enumerate(
            (
                (owner_hbm, owner_in),
                (block_hbm, block_in),
                (offset_hbm, offset_in),
                (near_hbm, near_in),
                (weights_hbm, weights_in),
            )
        )
    ]
    for copy in small:
        copy.start()

    def flow_in(v):
        return pltpu.make_async_copy(
            flow_hbm.at[v], g0.at[v, pl.ds(3, CX), pl.ds(Y0, CY)], in_sem.at[v]
        )

    for v in range(NV):
        flow_in(v).start()

    def clear(v, carry):
        for g in (g0, g1):
            g[v, 0:3, Y0 : Y0 + CY] = jnp.zeros((3, CY, CZ), F32)
            g[v, PX - 3 : PX, Y0 : Y0 + CY] = jnp.zeros((3, CY, CZ), F32)
            g[v, 3 : PX - 3, 0:Y0] = jnp.zeros((CX, Y0, CZ), F32)
            g[v, 3 : PX - 3, Y0 + CY : PY] = jnp.zeros((CX, PY - Y0 - CY, CZ), F32)
        return carry

    lax.fori_loop(0, NV, clear, 0)
    for pad in (pad_x, pad_y, pad_z):
        size = pad.shape[0]
        pad[0:8] = jnp.zeros((8, SLOTS), F32)
        pad[size - 8 : size] = jnp.zeros((8, SLOTS), F32)

    z_from = lax.broadcasted_iota(jnp.int32, (CZ, CZ), 0)
    z_to = lax.broadcasted_iota(jnp.int32, (CZ, CZ), 1)
    band = jnp.zeros((CZ, CZ), F32)
    for j in OFFSETS:
        band = jnp.where(z_from - z_to == j, tap(2, j), band)
    band_high, band_low = split(band)
    band_z[0:CZ] = band_high
    band_z[CZ : 2 * CZ] = band_high
    band_z[2 * CZ :] = band_low

    for copy in small:
        copy.wait()
    row = lax.broadcasted_iota(jnp.int32, (FR, FR), 0)
    col = lax.broadcasted_iota(jnp.int32, (FR, FR), 1)
    owner_wide = jnp.broadcast_to(owner_in[...], (FR, FR))
    owner_tall = jnp.transpose(owner_wide)
    earlier = jnp.where((owner_wide == owner_tall) & (row < col), 1.0, 0.0).astype(F32)
    rank = jnp.sum(earlier, axis=0, keepdims=True)
    mine = owner_wide == row
    ohot[0] = jnp.where(mine & (rank < 0.5), 1.0, 0.0).astype(F32)
    ohot[1] = jnp.where(mine & (rank > 0.5), 1.0, 0.0).astype(F32)
    payload = jnp.concatenate(
        [
            weights_in[...],
            near_in[...],
            block_in[...].astype(F32),
            offset_in[...].astype(F32),
            jnp.ones((1, FR), F32),
        ],
        axis=0,
    )
    nothing = jnp.zeros((32, FR), F32)
    blank = jnp.zeros((64, FR), F32)
    contract_last = (((1,), (1,)), ((), ()))
    a1[...] = lax.dot_general(
        ohot[0], jnp.concatenate([payload, nothing, blank], axis=0), contract_last,
        precision=HIGHEST, preferred_element_type=F32,
    ) + lax.dot_general(
        ohot[1], jnp.concatenate([nothing, payload, blank], axis=0), contract_last,
        precision=HIGHEST, preferred_element_type=F32,
    )

    targets = ((gx + 1, gy), (gx - 1, gy), (gx, gy + 1), (gx, gy - 1))
    sends = (gx < GX - 1, gx > 0, gy < GY - 1, gy > 0)
    takes = (gx > 0, gx < GX - 1, gy > 0, gy < GY - 1)

    def face(step, side, v=None):
        g = (g0, g1)[step]
        if side < 2:
            layers = pl.ds(CX if side == 0 else 3, 3)
            if v is None:
                src, dst = g.at[:, layers, pl.ds(Y0, CY)], hx.at[step, side]
            else:
                src, dst = g.at[v, layers, pl.ds(Y0, CY)], hx.at[step, side, v]
        elif v is None:
            src, dst = sy.at[step, side - 2], hy.at[step, side - 2]
        else:
            src, dst = sy.at[step, side - 2, v], hy.at[step, side - 2, v]
        return pltpu.make_async_remote_copy(
            src_ref=src, dst_ref=dst,
            send_sem=first_send.at[side] if v is None else halo_send.at[v, side],
            recv_sem=first_recv.at[side] if v is None else halo_recv.at[v, side],
            device_id=targets[side], device_id_type=MESH,
        )

    for side in range(4):
        @pl.when(jnp.logical_not(takes[side]))
        def _():
            halo = (hx, hx, hy, hy)[side]
            for step in range(STEPS):
                halo[step, side % 2] = jnp.zeros(halo.shape[2:], F32)
            tables[side] = jnp.zeros((32, SLOTS), F32)

    def pack_faces(step, v):
        flat = (g0, g1)[step].reshape(NV * PX * PY, CZ)
        for side, first in ((0, CY - 3), (1, 0)):
            for j in range(3):
                for half in range(2):
                    start = (v * PX + 3 + 8 * half) * PY + Y0 + first + j
                    sy[step, side, v, pl.ds(j * CX + 8 * half, 8)] = flat[pl.ds(start, 8, PY)]

    def interior(step):
        g = (g0, g1)[step]

        def body(v, carry):
            mid = g[v, 3 : 3 + CX, Y0 : Y0 + CY]
            total = mid * CENTER
            for j in OFFSETS:
                total = total + g[v, 3 + j : 3 + j + CX, Y0 : Y0 + CY] * tap(0, j)
            for j in OFFSETS:
                total = total + g[v, 3 : 3 + CX, Y0 + j : Y0 + CY + j] * tap(1, j)
            z_part = three_term(mid.reshape(CX * CY, CZ), band_z[...])
            res[pl.ds(v * CX, CX)] = total + z_part.reshape(CX, CY, CZ)
            return carry

        lax.fori_loop(0, NV, body, 0)

    def rows_to(src, source, count, dst, target, phase, peer):
        pltpu.make_async_remote_copy(
            src_ref=src.at[pl.ds(source, count)], dst_ref=dst.at[pl.ds(target, count)],
            send_sem=row_send.at[phase], recv_sem=row_recv.at[phase],
            device_id=peer, device_id_type=MESH,
        ).start()

    def rows_wait(buf, count, sem):
        part = buf.at[pl.ds(0, count)]
        pltpu.make_async_copy(part, part, sem).wait()

    def first_faces(v, carry):
        flow_in(v).wait()
        pack_faces(0, v)
        return carry

    lax.fori_loop(0, NV, first_faces, 0)
    x_rows = pl.ds(pl.multiple_of(gx * GY, GY), GY)
    b1[x_rows] = a1[x_rows]
    pl.semaphore_wait(barrier, greeted)
    for peer in along_x:
        rows_to(a1, pl.multiple_of(peer[0] * GY, GY), GY, b1, pl.multiple_of(gx * GY, GY), 0, peer)
    for peer in along_y:
        pl.semaphore_signal(vouched, inc=1, device_id=peer, device_id_type=MESH)
    for side in range(4):
        @pl.when(sends[side])
        def _():
            face(0, side).start()
    interior(0)
    rows_wait(b1, DEVICES - GY, row_recv.at[0])
    for h in range(GY):
        bt[h * GX : (h + 1) * GX] = b1[pl.ds(h, GX, GY)]
    y_rows = pl.ds(pl.multiple_of(gy * GX, GX), GX)
    c1[y_rows] = bt[y_rows]
    pl.semaphore_wait(vouched, 3)
    for peer in plane_yz:
        rows_to(bt, pl.multiple_of(peer[1] * GX, GX), GX, c1, pl.multiple_of(gy * GX, GX), 1, peer)

    flat_res = res.reshape(NV * CX * CY, CZ)

    def add_halo(step, v):
        for r in range(3):
            low = res[v * CX + r]
            high = res[v * CX + CX - 1 - r]
            for j in range(-3, -r):
                low = low + hx[step, 0, v, r + j + 3] * tap(0, j)
                high = high + hx[step, 1, v, -r - 1 - j] * tap(0, -j)
            res[v * CX + r] = low
            res[v * CX + CX - 1 - r] = high
        for r in range(3):
            for half in range(2):
                start = (v * CX + 8 * half) * CY
                at_low = pl.ds(start + r, 8, CY)
                at_high = pl.ds(start + CY - 1 - r, 8, CY)
                low = flat_res[at_low]
                high = flat_res[at_high]
                for j in range(-3, -r):
                    low = low + hy[step, 0, v, pl.ds((r + j + 3) * CX + 8 * half, 8)] * tap(1, j)
                    high = high + hy[step, 1, v, pl.ds((-r - 1 - j) * CX + 8 * half, 8)] * tap(1, -j)
                flat_res[at_low] = low
                flat_res[at_high] = high

    def variable(v):
        return pl.ds(pl.multiple_of(v * CX * CY, CX * CY), CX * CY)

    for side in range(4):
        @pl.when(takes[side])
        def _():
            face(0, side).wait_recv()

    def first_lhs(v, carry):
        add_halo(0, v)
        high, low = split(flat_res[variable(v)])
        lhs[variable(v), 0:CZ] = high
        lhs[variable(v), CZ : 2 * CZ] = low
        lhs[variable(v), 2 * CZ :] = high
        return carry

    lax.fori_loop(0, NV, first_lhs, 0)

    rows_wait(c1, DEVICES - GX, row_recv.at[1])
    turned = jnp.transpose(c1[...])
    table[:, 0:DEVICES] = turned[0:32]
    table[:, DEVICES:] = turned[32:64]

    def table_copy(side):
        return pltpu.make_async_remote_copy(
            src_ref=table, dst_ref=tables.at[side],
            send_sem=table_send.at[side], recv_sem=table_recv.at[side],
            device_id=targets[side], device_id_type=MESH,
        )

    for side in range(4):
        @pl.when(sends[side])
        def _():
            table_copy(side).start()

    row8 = lax.broadcasted_iota(jnp.int32, (8, SLOTS), 0)

    def weights_of(asked):
        block = asked[29:30].astype(jnp.int32)
        places = (block // 64, (block // 16) % 4, block % 16)
        spread = [
            jnp.concatenate(
                [jnp.where(place == b, asked[8 * d : 8 * d + 8], 0.0) for b in range(size // 8)],
                axis=0,
            )
            for d, (place, size) in enumerate(zip(places, (CX, CY, CZ)))
        ]
        return places, spread

    def put_three(ref, at, values):
        high, low = split(values)
        ref[0:CZ, at] = high
        ref[CZ : 2 * CZ, at] = high
        ref[2 * CZ :, at] = low

    asked = table[...]
    (kx, ky, kz), (weights_x, weights_y, weights_z) = weights_of(asked)
    last = asked[24:32]
    offset = last[6:7].astype(jnp.int32)
    live = last[7:8]
    near = jnp.where(row8 < NV, last, 0.0)
    put_three(wz_rhs, slice(0, SLOTS), weights_z)
    for x in range(CX):
        plane[x * CY : (x + 1) * CY] = weights_x[x : x + 1] * weights_y
    cell = (8 * kx + offset // 64) * CY + 8 * ky + (offset // 8) % 8
    cell = jnp.where(live > 0.5, cell, -1)
    cell_z = 8 * kz + offset % 8
    places = lax.broadcasted_iota(jnp.int32, (CX * CY, SLOTS), 0)
    pick[...] = jnp.where(places == cell, 1.0, 0.0).astype(F32).astype(BF16)
    places_z = lax.broadcasted_iota(jnp.int32, (CZ, SLOTS), 0)
    hot_z = jnp.where(places_z == cell_z, 1.0, 0.0).astype(F32).astype(BF16)
    pzt[:, 0:SLOTS] = hot_z
    pzt[:, SLOTS:] = hot_z
    counts = lax.dot_general(
        pick[...], hot_z, contract_last, preferred_element_type=F32
    )
    recip[...] = 1.0 / (1.0 + counts)

    def moved(pad, values, dim):
        size = values.shape[0]
        pad[8 : 8 + size] = values
        total = jnp.zeros_like(values)
        for j in OFFSETS:
            total = total + pad[8 - j : 8 - j + size] * tap(dim, j)
        return total

    moved_x = weights_x * CENTER + moved(pad_x, weights_x, 0)
    moved_y = moved(pad_y, weights_y, 1)
    put_three(wz_rhs, slice(SLOTS, 2 * SLOTS), moved(pad_z, weights_z, 2))
    for x in range(CX):
        plane_z[x * CY : (x + 1) * CY] = (
            moved_x[x : x + 1] * weights_y + weights_x[x : x + 1] * moved_y
        )

    def relaxed(step, near):
        def body(v, interp):
            if step == 0:
                t = jnp.dot(lhs[variable(v)], wz_rhs[:, 0:SLOTS], preferred_element_type=F32)
            else:
                for side in range(4):
                    @pl.when(takes[side])
                    def _():
                        face(1, side, v).wait_recv()
                add_halo(1, v)
                t = three_term(flat_res[variable(v)], wz_rhs[:, 0:SLOTS])
            here = jnp.sum(t * plane[...], axis=0, keepdims=True)
            return jnp.where(row8 == v, here, interp)

        interp = lax.fori_loop(0, NV, body, jnp.zeros((8, SLOTS), F32), unroll=True)
        return near + relaxation * (interp - near)

    def injected(v, near):
        here = jnp.sum(jnp.where(row8 == v, near, 0.0), axis=0, keepdims=True)
        here = jnp.broadcast_to(here, (16, SLOTS))
        high, low = split(here)
        hot = pick[...].reshape(CX * CY // 16, 16, SLOTS)
        left = jnp.concatenate(
            [
                (hot * high[None]).reshape(CX * CY, SLOTS),
                (hot * low[None]).reshape(CX * CY, SLOTS),
            ],
            axis=1,
        )
        gained = lax.dot_general(left, pzt[...], contract_last, preferred_element_type=F32)
        return ((flat_res[variable(v)] + gained) * recip[...]).reshape(CX, CY, CZ)

    near = relaxed(0, near)

    def second_faces(v, carry):
        values = injected(v, near)
        g1[v, 3 : 3 + CX, Y0 : Y0 + CY] = values
        pack_faces(1, v)
        for side in range(4):
            @pl.when(sends[side])
            def _():
                face(1, side, v).start()
        high, low = split(values.reshape(CX * CY, CZ))
        lhs[variable(v), 0:CZ] = high
        lhs[variable(v), CZ : 2 * CZ] = low
        lhs[variable(v), 2 * CZ :] = high
        return carry

    lax.fori_loop(0, NV, second_faces, 0, unroll=True)

    def own_part(v, own):
        t = jnp.dot(lhs[variable(v)], wz_rhs[...], preferred_element_type=F32)
        both = t[:, 0:SLOTS] * plane_z[...] + t[:, SLOTS:] * plane[...]
        return jnp.where(row8 == v, jnp.sum(both, axis=0, keepdims=True), own)

    own = lax.fori_loop(0, NV, own_part, jnp.zeros((8, SLOTS), F32), unroll=True)
    parts = [near + relaxation * (own - near)]
    for side in range(4):
        @pl.when(takes[side])
        def _():
            table_copy(side).wait_recv()
        _, spread = weights_of(tables[side])
        put_three(near_rhs.at[side], slice(0, SLOTS), spread[2])
        dim = side // 2
        across, beside = spread[dim], spread[1 - dim]
        size = across.shape[0]
        reach = []
        for i in range(3):
            total = jnp.zeros((1, SLOTS), F32)
            for j in range(1, 4):
                if side % 2 == 0 and j > i:
                    total = total + across[size + i - j : size + i - j + 1] * tap(dim, j)
                if side % 2 == 1 and j >= 3 - i:
                    total = total + across[i - 3 + j : i - 2 + j] * tap(dim, -j)
            reach.append(total * beside)
        reach = jnp.concatenate(reach, axis=0)
        if dim == 0:
            first = 0 if side == 0 else (CX - 3) * CY
            left = jnp.concatenate(
                [lhs[v * CX * CY + first : v * CX * CY + first + 3 * CY] for v in range(NV)], axis=0
            )
            t = jnp.dot(left, near_rhs[side], preferred_element_type=F32)
        else:
            t = three_term(sy[1, 3 - side].reshape(NV * 3 * CX, CZ), near_rhs[side])
        rows = reach.shape[0]
        added = jnp.zeros((8, SLOTS), F32)
        for v in range(NV):
            here = jnp.sum(t[v * rows : (v + 1) * rows] * reach, axis=0, keepdims=True)
            added = jnp.where(row8 == v, here, added)
        parts.append(relaxation * added)

    back = jnp.concatenate(
        [part[:, half : half + DEVICES] for part in parts for half in (0, DEVICES)]
        + [jnp.zeros((DEVICES - 80, DEVICES), F32)],
        axis=0,
    )
    d1[...] = jnp.transpose(back)
    for px, py in others():
        rows_to(d1, py * GX + px, 1, fin, me, 2, (px, py))
    fin[pl.ds(me, 1)] = d1[pl.ds(gy * GX + gx, 1)]

    interior(1)
    near = relaxed(1, near)

    def last_injection(v, carry):
        flow_out[v] = injected(v, near)
        return carry

    lax.fori_loop(0, NV, last_injection, 0, unroll=True)

    rows_wait(a1, DEVICES - GY, row_send.at[0])
    rows_wait(bt, DEVICES - GX, row_send.at[1])
    for side in range(4):
        @pl.when(sends[side])
        def _():
            face(0, side).wait_send()
            table_copy(side).wait_send()

    def drain(v, carry):
        for side in range(4):
            @pl.when(sends[side])
            def _():
                face(1, side, v).wait_send()
        return carry

    lax.fori_loop(0, NV, drain, 0)
    rows_wait(d1, DEVICES - 1, row_send.at[2])
    rows_wait(fin, DEVICES - 1, row_recv.at[2])
    returned = jnp.transpose(fin[...])
    total = returned[0:16]
    for side, shift in enumerate((DEVICES - GY, GY, DEVICES - 1, 1)):
        total = total + pltpu.roll(returned[16 + 16 * side : 32 + 16 * side], shift, axis=1)
    served = jnp.dot(
        total[0:8], ohot[0], precision=HIGHEST, preferred_element_type=F32
    ) + jnp.dot(total[8:16], ohot[1], precision=HIGHEST, preferred_element_type=F32)
    near_out[...] = served[0:NV]


def hand_over(flow_vmem, near_vmem, flow_out, near_out, sems):
    copies = [
        pltpu.make_async_copy(flow_vmem, flow_out, sems.at[0]),
        pltpu.make_async_copy(near_vmem, near_out, sems.at[1]),
    ]
    for copy in copies:
        copy.start()
    for copy in copies:
        copy.wait()


def shards(flow, near, donor_owner, donor_block, recv_offset, weights):
    hbm = pl.BlockSpec(memory_space=pltpu.HBM)
    whole = pl.BlockSpec(memory_space=pltpu.VMEM)
    vmem = pltpu.VMEM
    dma = pltpu.SemaphoreType.DMA
    operands = (
        flow,
        near,
        donor_owner.reshape(1, FR),
        donor_block.reshape(1, FR),
        recv_offset.reshape(1, FR),
        weights.reshape(24, FR),
    )
    flow, near = pl.pallas_call(
        kernel,
        out_shape=(vmem((NV, CX, CY, CZ), F32), vmem((NV, FR), F32)),
        in_specs=[hbm] * 6,
        out_specs=(whole, whole),
        scratch_shapes=[
            vmem((NV, PX, PY, CZ), F32),
            vmem((NV, PX, PY, CZ), F32),
            vmem((NV * CX, CY, CZ), F32),
            vmem((STEPS, 2, NV, 3, CY, CZ), F32),
            vmem((STEPS, 2, NV, 3 * CX, CZ), F32),
            vmem((STEPS, 2, NV, 3 * CX, CZ), F32),
            vmem((NV, FR), F32),
            vmem((1, FR), jnp.int32),
            vmem((1, FR), jnp.int32),
            vmem((1, FR), jnp.int32),
            vmem((24, FR), F32),
            vmem((DEVICES, 128), F32),
            vmem((DEVICES, 128), F32),
            vmem((DEVICES, 128), F32),
            vmem((DEVICES, 128), F32),
            vmem((DEVICES, 128), F32),
            vmem((DEVICES, 128), F32),
            vmem((32, SLOTS), F32),
            vmem((4, 32, SLOTS), F32),
            vmem((2, DEVICES, FR), F32),
            vmem((3 * CZ, CZ), BF16),
            vmem((NV * CX * CY, 3 * CZ), BF16),
            vmem((3 * CZ, 2 * SLOTS), BF16),
            vmem((4, 3 * CZ, SLOTS), BF16),
            vmem((CX * CY, SLOTS), F32),
            vmem((CX * CY, SLOTS), F32),
            vmem((CX + 16, SLOTS), F32),
            vmem((CY + 16, SLOTS), F32),
            vmem((CZ + 16, SLOTS), F32),
            vmem((CX * CY, SLOTS), BF16),
            vmem((CZ, 2 * SLOTS), BF16),
            vmem((CX * CY, CZ), F32),
            dma((NV,)),
            dma((5,)),
            dma((4,)),
            dma((4,)),
            dma((NV, 4)),
            dma((NV, 4)),
            dma((3,)),
            dma((3,)),
            pltpu.SemaphoreType.REGULAR,
            dma((4,)),
            dma((4,)),
        ],
        compiler_params=pltpu.CompilerParams(
            collective_id=0, has_side_effects=True, vmem_limit_bytes=40 * 1024 * 1024
        ),
        cost_estimate=pl.CostEstimate(
            flops=2 * STEPS * 20 * NV * CX * CY * CZ,
            bytes_accessed=2 * 4 * NV * CX * CY * CZ,
            transcendentals=0,
        ),
        name="rotor_wake_steps",
    )(*[pltpu.with_memory_space_constraint(operand, pltpu.HBM) for operand in operands])
    return pl.pallas_call(
        hand_over,
        out_shape=(
            jax.ShapeDtypeStruct((NV, CX, CY, CZ), F32),
            jax.ShapeDtypeStruct((NV, FR), F32),
        ),
        in_specs=[whole, whole],
        out_specs=(hbm, hbm),
        scratch_shapes=[dma((2,))],
        name="hand_over",
    )(
        pltpu.with_memory_space_constraint(flow, pltpu.VMEM),
        pltpu.with_memory_space_constraint(near, pltpu.VMEM),
    )


def solution(mesh):
    in_specs = (
        P(None, "gx", "gy", None),
        P(None, ("gx", "gy")),
        P(("gx", "gy"), None),
        P(("gx", "gy")),
        P(("gx", "gy")),
        P(None, None, ("gx", "gy")),
    )
    out_specs = (P(None, "gx", "gy", None), P(None, ("gx", "gy")))
    return jax.shard_map(shards, mesh=mesh, in_specs=in_specs, out_specs=out_specs, check_vma=False)
```

```python
import itertools

import jax
import jax.numpy as jnp
from jax import lax
from jax.experimental import pallas as pl
from jax.experimental.pallas import tpu as pltpu
from jax.sharding import PartitionSpec as P

STEPS = 2
NV = 5
CX = 16
CY = 32
CZ = 128
FR = 128
GX = 8
GY = 16
DEVICES = GX * GY
SLOTS = 2 * DEVICES
PX = CX + 6
PY = CY + 16
Y0 = 8

second_taps = (1.0 / 90, -3.0 / 20, 3.0 / 2, -49.0 / 18, 3.0 / 2, -3.0 / 20, 1.0 / 90)
first_taps = (-1.0 / 60, 3.0 / 20, -3.0 / 4, 0.0, 3.0 / 4, -3.0 / 20, 1.0 / 60)
diffusion = 0.05
velocity = (0.6, -0.5, 0.4)
relaxation = 0.6

TAPS = [
    [diffusion * second_taps[o] - velocity[d] * first_taps[o] for o in range(7)] for d in range(3)
]
CENTER = 1.0 + sum(TAPS[d][3] for d in range(3))
OFFSETS = (-3, -2, -1, 1, 2, 3)
HIGHEST = lax.Precision.HIGHEST
MESH = pl.DeviceIdType.MESH
BF16 = jnp.bfloat16
F32 = jnp.float32


OTHERS = sorted(
    itertools.product(range(4), range(2), range(4), range(4)),
    key=lambda o: -10 * sum(min(o[i], 4 - o[i]) for i in (0, 2, 3)) - o[1],
)[:-1]


def tap(dim, j):
    return TAPS[dim][j + 3]


def split(value):
    high = value.astype(BF16)
    low = (value - high.astype(F32)).astype(BF16)
    return high, low


def three_term(values, right):
    high, low = split(values)
    return jnp.dot(
        jnp.concatenate([high, low, high], axis=1), right, preferred_element_type=F32
    )


def kernel(
    flow_hbm, near_hbm, owner_hbm, block_hbm, offset_hbm, weights_hbm,
    flow_out, near_out,
    g0, g1, res, hx, hy, sy,
    near_in, owner_in, block_in, offset_in, weights_in,
    a1, b1, bt, c1, d1, fin, table, tables,
    ohot, band_z, lhs, wz_rhs, near_rhs, plane, plane_z, pad_x, pad_y, pad_z, pick, recip,
    in_sem, small_sem, first_send, first_recv, halo_send, halo_recv, row_send, row_recv, vouched,
    table_send, table_recv,
):
    gx = lax.axis_index("gx")
    gy = lax.axis_index("gy")
    me = gx * GY + gy
    chip_x, core = gx // 2, lax.rem(gx, 2)
    chip_z, chip_y = gy // 4, lax.rem(gy, 4)

    def others():
        for dx, dc, dz, dy in OTHERS:
            yield (
                lax.rem(chip_x + dx, 4) * 2 + lax.rem(core + dc, 2),
                lax.rem(chip_z + dz, 4) * 4 + lax.rem(chip_y + dy, 4),
            )

    along_x = [(lax.rem(gx + k, GX), gy) for k in range(1, GX)]
    along_y = [(gx, chip_z * 4 + lax.rem(chip_y + k, 4)) for k in range(1, 4)]
    along_z = [(gx, lax.rem(gy + 4 * k, GY)) for k in range(1, 4)]
    plane_yz = [(gx, lax.rem(gy + k, GY)) for k in range(1, GY)]
    barrier = pltpu.get_barrier_semaphore()
    for peer in along_y + along_z + along_x:
        pl.semaphore_signal(barrier, inc=1, device_id=peer, device_id_type=MESH)
    after = (chip_y == 3) & (gy < GY - 1)
    before = (chip_y == 0) & (gy > 0)

    @pl.when(after)
    def _():
        pl.semaphore_signal(barrier, inc=1, device_id=(gx, gy + 1), device_id_type=MESH)

    @pl.when(before)
    def _():
        pl.semaphore_signal(barrier, inc=1, device_id=(gx, gy - 1), device_id_type=MESH)

    greeted = GX + 5 + after.astype(jnp.int32) + before.astype(jnp.int32)

    small = [
        pltpu.make_async_copy(src, dst, small_sem.at[i])
        for i, (src, dst) in enumerate(
            (
                (owner_hbm, owner_in),
                (block_hbm, block_in),
                (offset_hbm, offset_in),
                (near_hbm, near_in),
                (weights_hbm, weights_in),
            )
        )
    ]
    for copy in small:
        copy.start()

    def flow_in(v):
        return pltpu.make_async_copy(
            flow_hbm.at[v], g0.at[v, pl.ds(3, CX), pl.ds(Y0, CY)], in_sem.at[v]
        )

    for v in range(NV):
        flow_in(v).start()

    def clear(v, carry):
        for g in (g0, g1):
            g[v, 0:3, Y0 : Y0 + CY] = jnp.zeros((3, CY, CZ), F32)
            g[v, PX - 3 : PX, Y0 : Y0 + CY] = jnp.zeros((3, CY, CZ), F32)
            g[v, 3 : PX - 3, 0:Y0] = jnp.zeros((CX, Y0, CZ), F32)
            g[v, 3 : PX - 3, Y0 + CY : PY] = jnp.zeros((CX, PY - Y0 - CY, CZ), F32)
        return carry

    lax.fori_loop(0, NV, clear, 0)
    for pad in (pad_x, pad_y, pad_z):
        size = pad.shape[0]
        pad[0:8] = jnp.zeros((8, SLOTS), F32)
        pad[size - 8 : size] = jnp.zeros((8, SLOTS), F32)

    z_from = lax.broadcasted_iota(jnp.int32, (CZ, CZ), 0)
    z_to = lax.broadcasted_iota(jnp.int32, (CZ, CZ), 1)
    band = jnp.zeros((CZ, CZ), F32)
    for j in OFFSETS:
        band = jnp.where(z_from - z_to == j, tap(2, j), band)
    band_high, band_low = split(band)
    band_z[0:CZ] = band_high
    band_z[CZ : 2 * CZ] = band_high
    band_z[2 * CZ :] = band_low

    for copy in small:
        copy.wait()
    row = lax.broadcasted_iota(jnp.int32, (FR, FR), 0)
    col = lax.broadcasted_iota(jnp.int32, (FR, FR), 1)
    owner_wide = jnp.broadcast_to(owner_in[...], (FR, FR))
    owner_tall = jnp.transpose(owner_wide)
    earlier = jnp.where((owner_wide == owner_tall) & (row < col), 1.0, 0.0).astype(F32)
    rank = jnp.sum(earlier, axis=0, keepdims=True)
    mine = owner_wide == row
    ohot[0] = jnp.where(mine & (rank < 0.5), 1.0, 0.0).astype(F32)
    ohot[1] = jnp.where(mine & (rank > 0.5), 1.0, 0.0).astype(F32)
    payload = jnp.concatenate(
        [
            weights_in[...],
            near_in[...],
            block_in[...].astype(F32),
            offset_in[...].astype(F32),
            jnp.ones((1, FR), F32),
        ],
        axis=0,
    )
    nothing = jnp.zeros((32, FR), F32)
    blank = jnp.zeros((64, FR), F32)
    contract_last = (((1,), (1,)), ((), ()))
    a1[...] = lax.dot_general(
        ohot[0], jnp.concatenate([payload, nothing, blank], axis=0), contract_last,
        precision=HIGHEST, preferred_element_type=F32,
    ) + lax.dot_general(
        ohot[1], jnp.concatenate([nothing, payload, blank], axis=0), contract_last,
        precision=HIGHEST, preferred_element_type=F32,
    )

    targets = ((gx + 1, gy), (gx - 1, gy), (gx, gy + 1), (gx, gy - 1))
    sends = (gx < GX - 1, gx > 0, gy < GY - 1, gy > 0)
    takes = (gx > 0, gx < GX - 1, gy > 0, gy < GY - 1)

    def face(step, side, v=None):
        g = (g0, g1)[step]
        if side < 2:
            layers = pl.ds(CX if side == 0 else 3, 3)
            if v is None:
                src, dst = g.at[:, layers, pl.ds(Y0, CY)], hx.at[step, side]
            else:
                src, dst = g.at[v, layers, pl.ds(Y0, CY)], hx.at[step, side, v]
        elif v is None:
            src, dst = sy.at[step, side - 2], hy.at[step, side - 2]
        else:
            src, dst = sy.at[step, side - 2, v], hy.at[step, side - 2, v]
        return pltpu.make_async_remote_copy(
            src_ref=src, dst_ref=dst,
            send_sem=first_send.at[side] if v is None else halo_send.at[v, side],
            recv_sem=first_recv.at[side] if v is None else halo_recv.at[v, side],
            device_id=targets[side], device_id_type=MESH,
        )

    for side in range(4):
        @pl.when(jnp.logical_not(takes[side]))
        def _():
            halo = (hx, hx, hy, hy)[side]
            for step in range(STEPS):
                halo[step, side % 2] = jnp.zeros(halo.shape[2:], F32)
            tables[side] = jnp.zeros((32, SLOTS), F32)

    def pack_faces(step, v):
        flat = (g0, g1)[step].reshape(NV * PX * PY, CZ)
        for side, first in ((0, CY - 3), (1, 0)):
            for j in range(3):
                for half in range(2):
                    start = (v * PX + 3 + 8 * half) * PY + Y0 + first + j
                    sy[step, side, v, pl.ds(j * CX + 8 * half, 8)] = flat[pl.ds(start, 8, PY)]

    def interior(step):
        g = (g0, g1)[step]

        def body(v, carry):
            mid = g[v, 3 : 3 + CX, Y0 : Y0 + CY]
            total = mid * CENTER
            for j in OFFSETS:
                total = total + g[v, 3 + j : 3 + j + CX, Y0 : Y0 + CY] * tap(0, j)
            for j in OFFSETS:
                total = total + g[v, 3 : 3 + CX, Y0 + j : Y0 + CY + j] * tap(1, j)
            z_part = three_term(mid.reshape(CX * CY, CZ), band_z[...])
            res[pl.ds(v * CX, CX)] = total + z_part.reshape(CX, CY, CZ)
            return carry

        lax.fori_loop(0, NV, body, 0)

    def rows_to(src, source, count, dst, target, phase, peer):
        pltpu.make_async_remote_copy(
            src_ref=src.at[pl.ds(source, count)], dst_ref=dst.at[pl.ds(target, count)],
            send_sem=row_send.at[phase], recv_sem=row_recv.at[phase],
            device_id=peer, device_id_type=MESH,
        ).start()

    def rows_wait(buf, count, sem):
        part = buf.at[pl.ds(0, count)]
        pltpu.make_async_copy(part, part, sem).wait()

    def first_faces(v, carry):
        flow_in(v).wait()
        pack_faces(0, v)
        return carry

    lax.fori_loop(0, NV, first_faces, 0)
    x_rows = pl.ds(pl.multiple_of(gx * GY, GY), GY)
    b1[x_rows] = a1[x_rows]
    pl.semaphore_wait(barrier, greeted)
    for peer in along_x:
        rows_to(a1, pl.multiple_of(peer[0] * GY, GY), GY, b1, pl.multiple_of(gx * GY, GY), 0, peer)
    for peer in along_y:
        pl.semaphore_signal(vouched, inc=1, device_id=peer, device_id_type=MESH)
    for side in range(4):
        @pl.when(sends[side])
        def _():
            face(0, side).start()
    interior(0)
    rows_wait(b1, DEVICES - GY, row_recv.at[0])
    for h in range(GY):
        bt[h * GX : (h + 1) * GX] = b1[pl.ds(h, GX, GY)]
    y_rows = pl.ds(pl.multiple_of(gy * GX, GX), GX)
    c1[y_rows] = bt[y_rows]
    pl.semaphore_wait(vouched, 3)
    for peer in plane_yz:
        rows_to(bt, pl.multiple_of(peer[1] * GX, GX), GX, c1, pl.multiple_of(gy * GX, GX), 1, peer)

    flat_res = res.reshape(NV * CX * CY, CZ)

    def add_halo(step, v):
        for r in range(3):
            low = res[v * CX + r]
            high = res[v * CX + CX - 1 - r]
            for j in range(-3, -r):
                low = low + hx[step, 0, v, r + j + 3] * tap(0, j)
                high = high + hx[step, 1, v, -r - 1 - j] * tap(0, -j)
            res[v * CX + r] = low
            res[v * CX + CX - 1 - r] = high
        for r in range(3):
            for half in range(2):
                start = (v * CX + 8 * half) * CY
                at_low = pl.ds(start + r, 8, CY)
                at_high = pl.ds(start + CY - 1 - r, 8, CY)
                low = flat_res[at_low]
                high = flat_res[at_high]
                for j in range(-3, -r):
                    low = low + hy[step, 0, v, pl.ds((r + j + 3) * CX + 8 * half, 8)] * tap(1, j)
                    high = high + hy[step, 1, v, pl.ds((-r - 1 - j) * CX + 8 * half, 8)] * tap(1, -j)
                flat_res[at_low] = low
                flat_res[at_high] = high

    def variable(v):
        start = v * CX * CY
        return pl.ds(start if isinstance(v, int) else pl.multiple_of(start, CX * CY), CX * CY)

    for side in range(4):
        @pl.when(takes[side])
        def _():
            face(0, side).wait_recv()

    def first_lhs(v, carry):
        add_halo(0, v)
        high, low = split(flat_res[variable(v)])
        lhs[variable(v), 0:CZ] = high
        lhs[variable(v), CZ : 2 * CZ] = low
        lhs[variable(v), 2 * CZ :] = high
        return carry

    lax.fori_loop(0, NV, first_lhs, 0)

    rows_wait(c1, DEVICES - GX, row_recv.at[1])
    turned = jnp.transpose(c1[...])
    table[:, 0:DEVICES] = turned[0:32]
    table[:, DEVICES:] = turned[32:64]

    def table_copy(side):
        return pltpu.make_async_remote_copy(
            src_ref=table, dst_ref=tables.at[side],
            send_sem=table_send.at[side], recv_sem=table_recv.at[side],
            device_id=targets[side], device_id_type=MESH,
        )

    for side in range(4):
        @pl.when(sends[side])
        def _():
            table_copy(side).start()

    row8 = lax.broadcasted_iota(jnp.int32, (8, SLOTS), 0)

    def weights_of(asked):
        block = asked[29:30].astype(jnp.int32)
        places = (block // 64, (block // 16) % 4, block % 16)
        spread = [
            jnp.concatenate(
                [jnp.where(place == b, asked[8 * d : 8 * d + 8], 0.0) for b in range(size // 8)],
                axis=0,
            )
            for d, (place, size) in enumerate(zip(places, (CX, CY, CZ)))
        ]
        return places, spread

    def put_three(ref, at, values):
        high, low = split(values)
        ref[0:CZ, at] = high
        ref[CZ : 2 * CZ, at] = high
        ref[2 * CZ :, at] = low

    asked = table[...]
    (kx, ky, kz), (weights_x, weights_y, weights_z) = weights_of(asked)
    last = asked[24:32]
    offset = last[6:7].astype(jnp.int32)
    live = last[7:8]
    near = jnp.where(row8 < NV, last, 0.0)
    put_three(wz_rhs, slice(0, SLOTS), weights_z)
    for x in range(CX):
        plane[x * CY : (x + 1) * CY] = weights_x[x : x + 1] * weights_y
    cell = (8 * kx + offset // 64) * CY + 8 * ky + (offset // 8) % 8
    cell = jnp.where(live > 0.5, cell, -1)
    cell_z = 8 * kz + offset % 8
    places = lax.broadcasted_iota(jnp.int32, (CX * CY, SLOTS), 0)
    picked = jnp.where(places == cell, 1.0, 0.0).astype(F32).astype(BF16)
    pick[:, 0:SLOTS] = picked
    pick[:, SLOTS:] = picked
    places_z = lax.broadcasted_iota(jnp.int32, (CZ, SLOTS), 0)
    hot_z = jnp.where(places_z == cell_z, 1.0, 0.0).astype(F32).astype(BF16)
    counts = lax.dot_general(
        picked, hot_z, contract_last, preferred_element_type=F32
    )
    recip[...] = 1.0 / (1.0 + counts)

    def moved(pad, values, dim):
        size = values.shape[0]
        pad[8 : 8 + size] = values
        total = jnp.zeros_like(values)
        for j in OFFSETS:
            total = total + pad[8 - j : 8 - j + size] * tap(dim, j)
        return total

    moved_x = weights_x * CENTER + moved(pad_x, weights_x, 0)
    moved_y = moved(pad_y, weights_y, 1)
    put_three(wz_rhs, slice(SLOTS, 2 * SLOTS), moved(pad_z, weights_z, 2))
    for x in range(CX):
        plane_z[x * CY : (x + 1) * CY] = (
            moved_x[x : x + 1] * weights_y + weights_x[x : x + 1] * moved_y
        )

    def relaxed(step, near):
        def body(v, interp):
            if step == 0:
                t = jnp.dot(lhs[variable(v)], wz_rhs[:, 0:SLOTS], preferred_element_type=F32)
            else:
                for side in range(4):
                    @pl.when(takes[side])
                    def _():
                        face(1, side, v).wait_recv()
                add_halo(1, v)
                t = three_term(flat_res[variable(v)], wz_rhs[:, 0:SLOTS])
            here = jnp.sum(t * plane[...], axis=0, keepdims=True)
            return jnp.where(row8 == v, here, interp)

        interp = lax.fori_loop(0, NV, body, jnp.zeros((8, SLOTS), F32), unroll=True)
        return near + relaxation * (interp - near)

    def injected(near):
        right = []
        for v in range(NV):
            high, low = split(jnp.broadcast_to(near[v : v + 1], (16, SLOTS)))
            hot = hot_z.reshape(CZ // 16, 16, SLOTS)
            right.append(
                jnp.concatenate(
                    [
                        (hot * high[None]).reshape(CZ, SLOTS),
                        (hot * low[None]).reshape(CZ, SLOTS),
                    ],
                    axis=1,
                )
            )
        gained = lax.dot_general(
            pick[...], jnp.concatenate(right, axis=0), contract_last, preferred_element_type=F32
        )
        for v in range(NV):
            part = gained[:, v * CZ : (v + 1) * CZ]
            yield v, ((flat_res[variable(v)] + part) * recip[...]).reshape(CX, CY, CZ)

    near = relaxed(0, near)

    for v, values in injected(near):
        g1[v, 3 : 3 + CX, Y0 : Y0 + CY] = values
        pack_faces(1, v)
        for side in range(4):
            @pl.when(sends[side])
            def _():
                face(1, side, v).start()
        high, low = split(values.reshape(CX * CY, CZ))
        lhs[variable(v), 0:CZ] = high
        lhs[variable(v), CZ : 2 * CZ] = low
        lhs[variable(v), 2 * CZ :] = high

    def own_part(v, own):
        t = jnp.dot(lhs[variable(v)], wz_rhs[...], preferred_element_type=F32)
        both = t[:, 0:SLOTS] * plane_z[...] + t[:, SLOTS:] * plane[...]
        return jnp.where(row8 == v, jnp.sum(both, axis=0, keepdims=True), own)

    own = lax.fori_loop(0, NV, own_part, jnp.zeros((8, SLOTS), F32), unroll=True)
    parts = [near + relaxation * (own - near)]
    for side in range(4):
        @pl.when(takes[side])
        def _():
            table_copy(side).wait_recv()
        _, spread = weights_of(tables[side])
        put_three(near_rhs.at[side], slice(0, SLOTS), spread[2])
        dim = side // 2
        across, beside = spread[dim], spread[1 - dim]
        size = across.shape[0]
        reach = []
        for i in range(3):
            total = jnp.zeros((1, SLOTS), F32)
            for j in range(1, 4):
                if side % 2 == 0 and j > i:
                    total = total + across[size + i - j : size + i - j + 1] * tap(dim, j)
                if side % 2 == 1 and j >= 3 - i:
                    total = total + across[i - 3 + j : i - 2 + j] * tap(dim, -j)
            reach.append(total * beside)
        reach = jnp.concatenate(reach, axis=0)
        if dim == 0:
            first = 0 if side == 0 else (CX - 3) * CY
            left = jnp.concatenate(
                [lhs[v * CX * CY + first : v * CX * CY + first + 3 * CY] for v in range(NV)], axis=0
            )
            t = jnp.dot(left, near_rhs[side], preferred_element_type=F32)
        else:
            t = three_term(sy[1, 3 - side].reshape(NV * 3 * CX, CZ), near_rhs[side])
        rows = reach.shape[0]
        added = jnp.zeros((8, SLOTS), F32)
        for v in range(NV):
            here = jnp.sum(t[v * rows : (v + 1) * rows] * reach, axis=0, keepdims=True)
            added = jnp.where(row8 == v, here, added)
        parts.append(relaxation * added)

    back = jnp.concatenate(
        [part[:, half : half + DEVICES] for part in parts for half in (0, DEVICES)]
        + [jnp.zeros((DEVICES - 80, DEVICES), F32)],
        axis=0,
    )
    d1[...] = jnp.transpose(back)
    for px, py in others():
        rows_to(d1, py * GX + px, 1, fin, me, 2, (px, py))
    fin[pl.ds(me, 1)] = d1[pl.ds(gy * GX + gx, 1)]

    interior(1)
    near = relaxed(1, near)

    for v, values in injected(near):
        flow_out[v] = values

    rows_wait(a1, DEVICES - GY, row_send.at[0])
    rows_wait(bt, DEVICES - GX, row_send.at[1])
    for side in range(4):
        @pl.when(sends[side])
        def _():
            face(0, side).wait_send()
            table_copy(side).wait_send()

    def drain(v, carry):
        for side in range(4):
            @pl.when(sends[side])
            def _():
                face(1, side, v).wait_send()
        return carry

    lax.fori_loop(0, NV, drain, 0)
    rows_wait(d1, DEVICES - 1, row_send.at[2])
    rows_wait(fin, DEVICES - 1, row_recv.at[2])
    returned = jnp.transpose(fin[...])
    total = returned[0:16]
    for side, shift in enumerate((DEVICES - GY, GY, DEVICES - 1, 1)):
        total = total + pltpu.roll(returned[16 + 16 * side : 32 + 16 * side], shift, axis=1)
    served = jnp.dot(
        jnp.concatenate([total[0:8], total[8:16]], axis=1), ohot[...].reshape(2 * DEVICES, FR),
        precision=HIGHEST, preferred_element_type=F32,
    )
    near_out[...] = served[0:NV]


def hand_over(flow_vmem, near_vmem, flow_out, near_out, sems):
    copies = [
        pltpu.make_async_copy(flow_vmem, flow_out, sems.at[0]),
        pltpu.make_async_copy(near_vmem, near_out, sems.at[1]),
    ]
    for copy in copies:
        copy.start()
    for copy in copies:
        copy.wait()


def shards(flow, near, donor_owner, donor_block, recv_offset, weights):
    hbm = pl.BlockSpec(memory_space=pltpu.HBM)
    whole = pl.BlockSpec(memory_space=pltpu.VMEM)
    vmem = pltpu.VMEM
    dma = pltpu.SemaphoreType.DMA
    operands = (
        flow,
        near,
        donor_owner.reshape(1, FR),
        donor_block.reshape(1, FR),
        recv_offset.reshape(1, FR),
        weights.reshape(24, FR),
    )
    flow, near = pl.pallas_call(
        kernel,
        out_shape=(vmem((NV, CX, CY, CZ), F32), vmem((NV, FR), F32)),
        in_specs=[hbm] * 6,
        out_specs=(whole, whole),
        scratch_shapes=[
            vmem((NV, PX, PY, CZ), F32),
            vmem((NV, PX, PY, CZ), F32),
            vmem((NV * CX, CY, CZ), F32),
            vmem((STEPS, 2, NV, 3, CY, CZ), F32),
            vmem((STEPS, 2, NV, 3 * CX, CZ), F32),
            vmem((STEPS, 2, NV, 3 * CX, CZ), F32),
            vmem((NV, FR), F32),
            vmem((1, FR), jnp.int32),
            vmem((1, FR), jnp.int32),
            vmem((1, FR), jnp.int32),
            vmem((24, FR), F32),
            vmem((DEVICES, 128), F32),
            vmem((DEVICES, 128), F32),
            vmem((DEVICES, 128), F32),
            vmem((DEVICES, 128), F32),
            vmem((DEVICES, 128), F32),
            vmem((DEVICES, 128), F32),
            vmem((32, SLOTS), F32),
            vmem((4, 32, SLOTS), F32),
            vmem((2, DEVICES, FR), F32),
            vmem((3 * CZ, CZ), BF16),
            vmem((NV * CX * CY, 3 * CZ), BF16),
            vmem((3 * CZ, 2 * SLOTS), BF16),
            vmem((4, 3 * CZ, SLOTS), BF16),
            vmem((CX * CY, SLOTS), F32),
            vmem((CX * CY, SLOTS), F32),
            vmem((CX + 16, SLOTS), F32),
            vmem((CY + 16, SLOTS), F32),
            vmem((CZ + 16, SLOTS), F32),
            vmem((CX * CY, 2 * SLOTS), BF16),
            vmem((CX * CY, CZ), F32),
            dma((NV,)),
            dma((5,)),
            dma((4,)),
            dma((4,)),
            dma((NV, 4)),
            dma((NV, 4)),
            dma((3,)),
            dma((3,)),
            pltpu.SemaphoreType.REGULAR,
            dma((4,)),
            dma((4,)),
        ],
        compiler_params=pltpu.CompilerParams(
            collective_id=0, has_side_effects=True, vmem_limit_bytes=40 * 1024 * 1024
        ),
        cost_estimate=pl.CostEstimate(
            flops=2 * STEPS * 20 * NV * CX * CY * CZ,
            bytes_accessed=2 * 4 * NV * CX * CY * CZ,
            transcendentals=0,
        ),
        name="rotor_wake_steps",
    )(*[pltpu.with_memory_space_constraint(operand, pltpu.HBM) for operand in operands])
    return pl.pallas_call(
        hand_over,
        out_shape=(
            jax.ShapeDtypeStruct((NV, CX, CY, CZ), F32),
            jax.ShapeDtypeStruct((NV, FR), F32),
        ),
        in_specs=[whole, whole],
        out_specs=(hbm, hbm),
        scratch_shapes=[dma((2,))],
        name="hand_over",
    )(
        pltpu.with_memory_space_constraint(flow, pltpu.VMEM),
        pltpu.with_memory_space_constraint(near, pltpu.VMEM),
    )


def solution(mesh):
    in_specs = (
        P(None, "gx", "gy", None),
        P(None, ("gx", "gy")),
        P(("gx", "gy"), None),
        P(("gx", "gy")),
        P(("gx", "gy")),
        P(None, None, ("gx", "gy")),
    )
    out_specs = (P(None, "gx", "gy", None), P(None, ("gx", "gy")))
    return jax.shard_map(shards, mesh=mesh, in_specs=in_specs, out_specs=out_specs, check_vma=False)
```

```python
import itertools

import jax
import jax.numpy as jnp
from jax import lax
from jax.experimental import pallas as pl
from jax.experimental.pallas import tpu as pltpu
from jax.sharding import PartitionSpec as P

STEPS = 2
NV = 5
CX = 16
CY = 32
CZ = 128
FR = 128
GX = 8
GY = 16
DEVICES = GX * GY
SLOTS = 2 * DEVICES
PX = CX + 6
PY = CY + 16
Y0 = 8

second_taps = (1.0 / 90, -3.0 / 20, 3.0 / 2, -49.0 / 18, 3.0 / 2, -3.0 / 20, 1.0 / 90)
first_taps = (-1.0 / 60, 3.0 / 20, -3.0 / 4, 0.0, 3.0 / 4, -3.0 / 20, 1.0 / 60)
diffusion = 0.05
velocity = (0.6, -0.5, 0.4)
relaxation = 0.6

TAPS = [
    [diffusion * second_taps[o] - velocity[d] * first_taps[o] for o in range(7)] for d in range(3)
]
CENTER = 1.0 + sum(TAPS[d][3] for d in range(3))
OFFSETS = (-3, -2, -1, 1, 2, 3)
HIGHEST = lax.Precision.HIGHEST
MESH = pl.DeviceIdType.MESH
BF16 = jnp.bfloat16
F32 = jnp.float32


OTHERS = sorted(
    itertools.product(range(4), range(2), range(4), range(4)),
    key=lambda o: -10 * sum(min(o[i], 4 - o[i]) for i in (0, 2, 3)) - o[1],
)[:-1]


def tap(dim, j):
    return TAPS[dim][j + 3]


def split(value):
    high = value.astype(BF16)
    low = (value - high.astype(F32)).astype(BF16)
    return high, low


def three_term(values, right):
    high, low = split(values)
    return jnp.dot(
        jnp.concatenate([high, low, high], axis=1), right, preferred_element_type=F32
    )


def kernel(
    flow_hbm, near_hbm, owner_hbm, block_hbm, offset_hbm, weights_hbm,
    flow_out, near_out,
    g0, g1, res, hx, hy, sy,
    near_in, owner_in, block_in, offset_in, weights_in,
    a1, b1, bt, c1, d1, fin, table, tables,
    ohot, ohot_low, band_z, lhs, wz_rhs, near_rhs, plane, plane_z, pad_x, pad_y, pad_z, pick, recip,
    in_sem, small_sem, halo_send, halo_recv, row_send, row_recv, vouched,
    table_send, table_recv,
):
    gx = lax.axis_index("gx")
    gy = lax.axis_index("gy")
    me = gx * GY + gy
    chip_x, core = gx // 2, lax.rem(gx, 2)
    chip_z, chip_y = gy // 4, lax.rem(gy, 4)

    placed = [
        (
            (dx, dc, dz, dy),
            (
                lax.rem(chip_x + dx, 4) * 2 + lax.rem(core + dc, 2),
                lax.rem(chip_z + dz, 4) * 4 + lax.rem(chip_y + dy, 4),
            ),
        )
        for dx, dc, dz, dy in OTHERS
    ]

    along_x = [(px, py) for o, (px, py) in placed if o[2] == o[3] == 0]
    along_y = [(gx, py) for o, (px, py) in placed if o[0] == o[1] == o[2] == 0]
    along_z = [(gx, py) for o, (px, py) in placed if o[0] == o[1] == o[3] == 0]
    plane_yz = [(gx, py) for o, (px, py) in placed if o[0] == o[1] == 0]
    barrier = pltpu.get_barrier_semaphore()
    for peer in along_y + along_z + along_x:
        pl.semaphore_signal(barrier, inc=1, device_id=peer, device_id_type=MESH)
    after = (chip_y == 3) & (gy < GY - 1)
    before = (chip_y == 0) & (gy > 0)

    @pl.when(after)
    def _():
        pl.semaphore_signal(barrier, inc=1, device_id=(gx, gy + 1), device_id_type=MESH)

    @pl.when(before)
    def _():
        pl.semaphore_signal(barrier, inc=1, device_id=(gx, gy - 1), device_id_type=MESH)

    greeted = GX + 5 + after.astype(jnp.int32) + before.astype(jnp.int32)

    small = [
        pltpu.make_async_copy(src, dst, small_sem.at[i])
        for i, (src, dst) in enumerate(
            (
                (owner_hbm, owner_in),
                (block_hbm, block_in),
                (offset_hbm, offset_in),
                (near_hbm, near_in),
                (weights_hbm, weights_in),
            )
        )
    ]
    for copy in small:
        copy.start()

    def flow_in(v):
        return pltpu.make_async_copy(
            flow_hbm.at[v], g0.at[v, pl.ds(3, CX), pl.ds(Y0, CY)], in_sem.at[v]
        )

    for v in range(NV):
        flow_in(v).start()

    def clear(v, carry):
        for g in (g0, g1):
            g[v, 0:3, Y0 : Y0 + CY] = jnp.zeros((3, CY, CZ), F32)
            g[v, PX - 3 : PX, Y0 : Y0 + CY] = jnp.zeros((3, CY, CZ), F32)
            g[v, 3 : PX - 3, 0:Y0] = jnp.zeros((CX, Y0, CZ), F32)
            g[v, 3 : PX - 3, Y0 + CY : PY] = jnp.zeros((CX, PY - Y0 - CY, CZ), F32)
        return carry

    lax.fori_loop(0, NV, clear, 0)
    for pad in (pad_x, pad_y, pad_z):
        size = pad.shape[0]
        pad[0:8] = jnp.zeros((8, SLOTS), F32)
        pad[size - 8 : size] = jnp.zeros((8, SLOTS), F32)

    z_from = lax.broadcasted_iota(jnp.int32, (CZ, CZ), 0)
    z_to = lax.broadcasted_iota(jnp.int32, (CZ, CZ), 1)
    band = jnp.zeros((CZ, CZ), F32)
    for j in OFFSETS:
        band = jnp.where(z_from - z_to == j, tap(2, j), band)
    band_high, band_low = split(band)
    band_z[0:CZ] = band_high
    band_z[CZ : 2 * CZ] = band_high
    band_z[2 * CZ :] = band_low

    for copy in small:
        copy.wait()
    row = lax.broadcasted_iota(jnp.int32, (FR, FR), 0)
    col = lax.broadcasted_iota(jnp.int32, (FR, FR), 1)
    owner_wide = jnp.broadcast_to(owner_in[...], (FR, FR))
    owner_tall = jnp.transpose(owner_wide)
    earlier = jnp.where((owner_wide == owner_tall) & (row < col), 1.0, 0.0).astype(F32)
    rank = jnp.sum(earlier, axis=0, keepdims=True)
    mine = owner_wide == row
    ohot[0] = jnp.where(mine & (rank < 0.5), 1.0, 0.0).astype(F32)
    ohot[1] = jnp.where(mine & (rank > 0.5), 1.0, 0.0).astype(F32)
    ohot_low[...] = ohot[...].reshape(2 * DEVICES, FR).astype(BF16)
    payload = jnp.concatenate(
        [
            weights_in[...],
            near_in[...],
            block_in[...].astype(F32),
            offset_in[...].astype(F32),
            jnp.ones((1, FR), F32),
        ],
        axis=0,
    )
    nothing = jnp.zeros((32, FR), F32)
    blank = jnp.zeros((64, FR), F32)
    contract_last = (((1,), (1,)), ((), ()))
    a1[...] = lax.dot_general(
        ohot[0], jnp.concatenate([payload, nothing, blank], axis=0), contract_last,
        precision=HIGHEST, preferred_element_type=F32,
    ) + lax.dot_general(
        ohot[1], jnp.concatenate([nothing, payload, blank], axis=0), contract_last,
        precision=HIGHEST, preferred_element_type=F32,
    )

    targets = ((gx + 1, gy), (gx - 1, gy), (gx, gy + 1), (gx, gy - 1))
    sends = (gx < GX - 1, gx > 0, gy < GY - 1, gy > 0)
    takes = (gx > 0, gx < GX - 1, gy > 0, gy < GY - 1)

    def face(step, side):
        if side < 2:
            layers = pl.ds(CX if side == 0 else 3, 3)
            src, dst = (g0, g1)[step].at[:, layers, pl.ds(Y0, CY)], hx.at[step, side]
        else:
            src, dst = sy.at[step, side - 2], hy.at[step, side - 2]
        return pltpu.make_async_remote_copy(
            src_ref=src, dst_ref=dst,
            send_sem=halo_send.at[step, side], recv_sem=halo_recv.at[step, side],
            device_id=targets[side], device_id_type=MESH,
        )

    for side in range(4):
        @pl.when(jnp.logical_not(takes[side]))
        def _():
            halo = (hx, hx, hy, hy)[side]
            for step in range(STEPS):
                halo[step, side % 2] = jnp.zeros(halo.shape[2:], F32)
            tables[side] = jnp.zeros((32, SLOTS), F32)

    def pack_faces(step, v):
        flat = (g0, g1)[step].reshape(NV * PX * PY, CZ)
        for side, first in ((0, CY - 3), (1, 0)):
            for j in range(3):
                for half in range(2):
                    start = (v * PX + 3 + 8 * half) * PY + Y0 + first + j
                    sy[step, side, v, pl.ds(j * CX + 8 * half, 8)] = flat[pl.ds(start, 8, PY)]

    def interior(step):
        g = (g0, g1)[step]

        def body(v, carry):
            mid = g[v, 3 : 3 + CX, Y0 : Y0 + CY]
            total = mid * CENTER
            for j in OFFSETS:
                total = total + g[v, 3 + j : 3 + j + CX, Y0 : Y0 + CY] * tap(0, j)
            for j in OFFSETS:
                total = total + g[v, 3 : 3 + CX, Y0 + j : Y0 + CY + j] * tap(1, j)
            z_part = three_term(mid.reshape(CX * CY, CZ), band_z[...])
            res[pl.ds(v * CX, CX)] = total + z_part.reshape(CX, CY, CZ)
            return carry

        lax.fori_loop(0, NV, body, 0)

    def rows_to(src, source, count, dst, target, phase, peer):
        pltpu.make_async_remote_copy(
            src_ref=src.at[pl.ds(source, count)], dst_ref=dst.at[pl.ds(target, count)],
            send_sem=row_send.at[phase], recv_sem=row_recv.at[phase],
            device_id=peer, device_id_type=MESH,
        ).start()

    def rows_wait(buf, count, sem):
        part = buf.at[pl.ds(0, count)]
        pltpu.make_async_copy(part, part, sem).wait()

    def first_faces(v, carry):
        flow_in(v).wait()
        pack_faces(0, v)
        return carry

    lax.fori_loop(0, NV, first_faces, 0)
    x_rows = pl.ds(pl.multiple_of(gx * GY, GY), GY)
    b1[x_rows] = a1[x_rows]
    pl.semaphore_wait(barrier, greeted)
    for peer in along_y:
        pl.semaphore_signal(vouched, inc=1, device_id=peer, device_id_type=MESH)
    for peer in along_x:
        rows_to(a1, pl.multiple_of(peer[0] * GY, GY), GY, b1, pl.multiple_of(gx * GY, GY), 0, peer)
    for side in range(4):
        @pl.when(sends[side])
        def _():
            face(0, side).start()
    interior(0)
    rows_wait(b1, DEVICES - GY, row_recv.at[0])
    for h in range(GY):
        bt[h * GX : (h + 1) * GX] = b1[pl.ds(h, GX, GY)]
    y_rows = pl.ds(pl.multiple_of(gy * GX, GX), GX)
    c1[y_rows] = bt[y_rows]
    pl.semaphore_wait(vouched, 3)
    for peer in plane_yz:
        rows_to(bt, pl.multiple_of(peer[1] * GX, GX), GX, c1, pl.multiple_of(gy * GX, GX), 1, peer)

    flat_res = res.reshape(NV * CX * CY, CZ)

    def add_halo(step, v):
        for r in range(3):
            low = res[v * CX + r]
            high = res[v * CX + CX - 1 - r]
            for j in range(-3, -r):
                low = low + hx[step, 0, v, r + j + 3] * tap(0, j)
                high = high + hx[step, 1, v, -r - 1 - j] * tap(0, -j)
            res[v * CX + r] = low
            res[v * CX + CX - 1 - r] = high
        for r in range(3):
            for half in range(2):
                start = (v * CX + 8 * half) * CY
                at_low = pl.ds(start + r, 8, CY)
                at_high = pl.ds(start + CY - 1 - r, 8, CY)
                low = flat_res[at_low]
                high = flat_res[at_high]
                for j in range(-3, -r):
                    low = low + hy[step, 0, v, pl.ds((r + j + 3) * CX + 8 * half, 8)] * tap(1, j)
                    high = high + hy[step, 1, v, pl.ds((-r - 1 - j) * CX + 8 * half, 8)] * tap(1, -j)
                flat_res[at_low] = low
                flat_res[at_high] = high

    def variable(v):
        start = v * CX * CY
        return pl.ds(start if isinstance(v, int) else pl.multiple_of(start, CX * CY), CX * CY)

    for side in range(4):
        @pl.when(takes[side])
        def _():
            face(0, side).wait_recv()

    def first_lhs(v, carry):
        add_halo(0, v)
        high, low = split(flat_res[variable(v)])
        lhs[variable(v), 0:CZ] = high
        lhs[variable(v), CZ : 2 * CZ] = low
        lhs[variable(v), 2 * CZ :] = high
        return carry

    lax.fori_loop(0, NV, first_lhs, 0)

    rows_wait(c1, DEVICES - GX, row_recv.at[1])
    turned = jnp.transpose(c1[...])
    table[:, 0:DEVICES] = turned[0:32]
    table[:, DEVICES:] = turned[32:64]

    def table_copy(side):
        return pltpu.make_async_remote_copy(
            src_ref=table, dst_ref=tables.at[side],
            send_sem=table_send.at[side], recv_sem=table_recv.at[side],
            device_id=targets[side], device_id_type=MESH,
        )

    for side in range(4):
        @pl.when(sends[side])
        def _():
            table_copy(side).start()

    row8 = lax.broadcasted_iota(jnp.int32, (8, SLOTS), 0)

    def weights_of(asked):
        block = asked[29:30].astype(jnp.int32)
        places = (block // 64, (block // 16) % 4, block % 16)
        spread = [
            jnp.concatenate(
                [jnp.where(place == b, asked[8 * d : 8 * d + 8], 0.0) for b in range(size // 8)],
                axis=0,
            )
            for d, (place, size) in enumerate(zip(places, (CX, CY, CZ)))
        ]
        return places, spread

    def put_three(ref, at, values):
        high, low = split(values)
        ref[0:CZ, at] = high
        ref[CZ : 2 * CZ, at] = high
        ref[2 * CZ :, at] = low

    asked = table[...]
    (kx, ky, kz), (weights_x, weights_y, weights_z) = weights_of(asked)
    last = asked[24:32]
    offset = last[6:7].astype(jnp.int32)
    live = last[7:8]
    near = jnp.where(row8 < NV, last, 0.0)
    put_three(wz_rhs, slice(0, SLOTS), weights_z)
    for x in range(CX):
        plane[x * CY : (x + 1) * CY] = weights_x[x : x + 1] * weights_y
    cell = (8 * kx + offset // 64) * CY + 8 * ky + (offset // 8) % 8
    cell = jnp.where(live > 0.5, cell, -1)
    cell_z = 8 * kz + offset % 8
    places = lax.broadcasted_iota(jnp.int32, (CX * CY, SLOTS), 0)
    picked = jnp.where(places == cell, 1.0, 0.0).astype(F32).astype(BF16)
    pick[:, 0:SLOTS] = picked
    pick[:, SLOTS:] = picked
    places_z = lax.broadcasted_iota(jnp.int32, (CZ, SLOTS), 0)
    hot_z = jnp.where(places_z == cell_z, 1.0, 0.0).astype(F32).astype(BF16)
    counts = lax.dot_general(
        picked, hot_z, contract_last, preferred_element_type=F32
    )
    recip[...] = 1.0 / (1.0 + counts)

    def moved(pad, values, dim):
        size = values.shape[0]
        pad[8 : 8 + size] = values
        total = jnp.zeros_like(values)
        for j in OFFSETS:
            total = total + pad[8 - j : 8 - j + size] * tap(dim, j)
        return total

    moved_x = weights_x * CENTER + moved(pad_x, weights_x, 0)
    moved_y = moved(pad_y, weights_y, 1)
    put_three(wz_rhs, slice(SLOTS, 2 * SLOTS), moved(pad_z, weights_z, 2))
    for x in range(CX):
        plane_z[x * CY : (x + 1) * CY] = (
            moved_x[x : x + 1] * weights_y + weights_x[x : x + 1] * moved_y
        )

    def relaxed(step, near):
        def body(v, interp):
            if step == 0:
                t = jnp.dot(lhs[variable(v)], wz_rhs[:, 0:SLOTS], preferred_element_type=F32)
            else:
                add_halo(1, v)
                t = three_term(flat_res[variable(v)], wz_rhs[:, 0:SLOTS])
            here = jnp.sum(t * plane[...], axis=0, keepdims=True)
            return jnp.where(row8 == v, here, interp)

        if step == 1:
            for side in range(4):
                @pl.when(takes[side])
                def _():
                    face(1, side).wait_recv()
        interp = lax.fori_loop(0, NV, body, jnp.zeros((8, SLOTS), F32), unroll=True)
        return near + relaxation * (interp - near)

    def injected(near):
        right = []
        for v in range(NV):
            high, low = split(jnp.broadcast_to(near[v : v + 1], (16, SLOTS)))
            hot = hot_z.reshape(CZ // 16, 16, SLOTS)
            right.append(
                jnp.concatenate(
                    [
                        (hot * high[None]).reshape(CZ, SLOTS),
                        (hot * low[None]).reshape(CZ, SLOTS),
                    ],
                    axis=1,
                )
            )
        gained = lax.dot_general(
            pick[...], jnp.concatenate(right, axis=0), contract_last, preferred_element_type=F32
        )
        for v in range(NV):
            part = gained[:, v * CZ : (v + 1) * CZ]
            yield v, ((flat_res[variable(v)] + part) * recip[...]).reshape(CX, CY, CZ)

    near = relaxed(0, near)

    for v, values in injected(near):
        g1[v, 3 : 3 + CX, Y0 : Y0 + CY] = values
        pack_faces(1, v)
        high, low = split(values.reshape(CX * CY, CZ))
        lhs[variable(v), 0:CZ] = high
        lhs[variable(v), CZ : 2 * CZ] = low
        lhs[variable(v), 2 * CZ :] = high
    for side in range(4):
        @pl.when(sends[side])
        def _():
            face(1, side).start()

    def own_part(v, own):
        t = jnp.dot(lhs[variable(v)], wz_rhs[...], preferred_element_type=F32)
        both = t[:, 0:SLOTS] * plane_z[...] + t[:, SLOTS:] * plane[...]
        return jnp.where(row8 == v, jnp.sum(both, axis=0, keepdims=True), own)

    own = lax.fori_loop(0, NV, own_part, jnp.zeros((8, SLOTS), F32), unroll=True)
    parts = [near + relaxation * (own - near)]
    for side in range(4):
        @pl.when(takes[side])
        def _():
            table_copy(side).wait_recv()
    for side in range(4):
        _, spread = weights_of(tables[side])
        put_three(near_rhs.at[side], slice(0, SLOTS), spread[2])
        dim = side // 2
        across, beside = spread[dim], spread[1 - dim]
        size = across.shape[0]
        reach = []
        for i in range(3):
            total = jnp.zeros((1, SLOTS), F32)
            for j in range(1, 4):
                if side % 2 == 0 and j > i:
                    total = total + across[size + i - j : size + i - j + 1] * tap(dim, j)
                if side % 2 == 1 and j >= 3 - i:
                    total = total + across[i - 3 + j : i - 2 + j] * tap(dim, -j)
            reach.append(total * beside)
        reach = jnp.concatenate(reach, axis=0)
        if dim == 0:
            first = 0 if side == 0 else (CX - 3) * CY
            left = jnp.concatenate(
                [lhs[v * CX * CY + first : v * CX * CY + first + 3 * CY] for v in range(NV)], axis=0
            )
            t = jnp.dot(left, near_rhs[side], preferred_element_type=F32)
        else:
            t = three_term(sy[1, 3 - side].reshape(NV * 3 * CX, CZ), near_rhs[side])
        rows = reach.shape[0]
        added = jnp.zeros((8, SLOTS), F32)
        for v in range(NV):
            here = jnp.sum(t[v * rows : (v + 1) * rows] * reach, axis=0, keepdims=True)
            added = jnp.where(row8 == v, here, added)
        parts.append(relaxation * added)

    back = jnp.concatenate(
        [part[:, half : half + DEVICES] for part in parts for half in (0, DEVICES)]
        + [jnp.zeros((DEVICES - 80, DEVICES), F32)],
        axis=0,
    )
    d1[...] = jnp.transpose(back)
    for _, (px, py) in placed:
        rows_to(d1, py * GX + px, 1, fin, me, 2, (px, py))
    fin[pl.ds(me, 1)] = d1[pl.ds(gy * GX + gx, 1)]

    interior(1)
    near = relaxed(1, near)

    for v, values in injected(near):
        flow_out[v] = values

    rows_wait(a1, DEVICES - GY, row_send.at[0])
    rows_wait(bt, DEVICES - GX, row_send.at[1])
    for side in range(4):
        @pl.when(sends[side])
        def _():
            face(0, side).wait_send()
            face(1, side).wait_send()
            table_copy(side).wait_send()

    rows_wait(d1, DEVICES - 1, row_send.at[2])
    rows_wait(fin, DEVICES - 1, row_recv.at[2])
    returned = jnp.transpose(fin[...])
    total = returned[0:16]
    for side, shift in enumerate((DEVICES - GY, GY, DEVICES - 1, 1)):
        total = total + pltpu.roll(returned[16 + 16 * side : 32 + 16 * side], shift, axis=1)
    total = jnp.concatenate([total[0:8], total[8:16]], axis=1)
    high, low = split(total)
    rest = total - high.astype(F32) - low.astype(F32)
    served = jnp.dot(
        jnp.concatenate([high.astype(F32), low.astype(F32), rest], axis=0).astype(BF16),
        ohot_low[...], preferred_element_type=F32,
    )
    near_out[...] = (served[0:8] + served[8:16] + served[16:24])[0:NV]


def hand_over(flow_vmem, near_vmem, flow_out, near_out, sems):
    copies = [
        pltpu.make_async_copy(flow_vmem, flow_out, sems.at[0]),
        pltpu.make_async_copy(near_vmem, near_out, sems.at[1]),
    ]
    for copy in copies:
        copy.start()
    for copy in copies:
        copy.wait()


def shards(flow, near, donor_owner, donor_block, recv_offset, weights):
    hbm = pl.BlockSpec(memory_space=pltpu.HBM)
    whole = pl.BlockSpec(memory_space=pltpu.VMEM)
    vmem = pltpu.VMEM
    dma = pltpu.SemaphoreType.DMA
    operands = (
        flow,
        near,
        donor_owner.reshape(1, FR),
        donor_block.reshape(1, FR),
        recv_offset.reshape(1, FR),
        weights.reshape(24, FR),
    )
    flow, near = pl.pallas_call(
        kernel,
        out_shape=(vmem((NV, CX, CY, CZ), F32), vmem((NV, FR), F32)),
        in_specs=[hbm] * 6,
        out_specs=(whole, whole),
        scratch_shapes=[
            vmem((NV, PX, PY, CZ), F32),
            vmem((NV, PX, PY, CZ), F32),
            vmem((NV * CX, CY, CZ), F32),
            vmem((STEPS, 2, NV, 3, CY, CZ), F32),
            vmem((STEPS, 2, NV, 3 * CX, CZ), F32),
            vmem((STEPS, 2, NV, 3 * CX, CZ), F32),
            vmem((NV, FR), F32),
            vmem((1, FR), jnp.int32),
            vmem((1, FR), jnp.int32),
            vmem((1, FR), jnp.int32),
            vmem((24, FR), F32),
            vmem((DEVICES, 128), F32),
            vmem((DEVICES, 128), F32),
            vmem((DEVICES, 128), F32),
            vmem((DEVICES, 128), F32),
            vmem((DEVICES, 128), F32),
            vmem((DEVICES, 128), F32),
            vmem((32, SLOTS), F32),
            vmem((4, 32, SLOTS), F32),
            vmem((2, DEVICES, FR), F32),
            vmem((2 * DEVICES, FR), BF16),
            vmem((3 * CZ, CZ), BF16),
            vmem((NV * CX * CY, 3 * CZ), BF16),
            vmem((3 * CZ, 2 * SLOTS), BF16),
            vmem((4, 3 * CZ, SLOTS), BF16),
            vmem((CX * CY, SLOTS), F32),
            vmem((CX * CY, SLOTS), F32),
            vmem((CX + 16, SLOTS), F32),
            vmem((CY + 16, SLOTS), F32),
            vmem((CZ + 16, SLOTS), F32),
            vmem((CX * CY, 2 * SLOTS), BF16),
            vmem((CX * CY, CZ), F32),
            dma((NV,)),
            dma((5,)),
            dma((STEPS, 4)),
            dma((STEPS, 4)),
            dma((3,)),
            dma((3,)),
            pltpu.SemaphoreType.REGULAR,
            dma((4,)),
            dma((4,)),
        ],
        compiler_params=pltpu.CompilerParams(
            collective_id=0, has_side_effects=True, vmem_limit_bytes=40 * 1024 * 1024
        ),
        cost_estimate=pl.CostEstimate(
            flops=2 * STEPS * 20 * NV * CX * CY * CZ,
            bytes_accessed=2 * 4 * NV * CX * CY * CZ,
            transcendentals=0,
        ),
        name="rotor_wake_steps",
    )(*[pltpu.with_memory_space_constraint(operand, pltpu.HBM) for operand in operands])
    return pl.pallas_call(
        hand_over,
        out_shape=(
            jax.ShapeDtypeStruct((NV, CX, CY, CZ), F32),
            jax.ShapeDtypeStruct((NV, FR), F32),
        ),
        in_specs=[whole, whole],
        out_specs=(hbm, hbm),
        scratch_shapes=[dma((2,))],
        name="hand_over",
    )(
        pltpu.with_memory_space_constraint(flow, pltpu.VMEM),
        pltpu.with_memory_space_constraint(near, pltpu.VMEM),
    )


def solution(mesh):
    in_specs = (
        P(None, "gx", "gy", None),
        P(None, ("gx", "gy")),
        P(("gx", "gy"), None),
        P(("gx", "gy")),
        P(("gx", "gy")),
        P(None, None, ("gx", "gy")),
    )
    out_specs = (P(None, "gx", "gy", None), P(None, ("gx", "gy")))
    return jax.shard_map(shards, mesh=mesh, in_specs=in_specs, out_specs=out_specs, check_vma=False)
```

```python
import itertools

import jax
import jax.numpy as jnp
from jax import lax
from jax.experimental import pallas as pl
from jax.experimental.pallas import tpu as pltpu
from jax.sharding import PartitionSpec as P

STEPS = 2
NV = 5
CX = 16
CY = 32
CZ = 128
FR = 128
GX = 8
GY = 16
DEVICES = GX * GY
SLOTS = 2 * DEVICES
PX = CX + 6
PY = CY + 16
Y0 = 8

second_taps = (1.0 / 90, -3.0 / 20, 3.0 / 2, -49.0 / 18, 3.0 / 2, -3.0 / 20, 1.0 / 90)
first_taps = (-1.0 / 60, 3.0 / 20, -3.0 / 4, 0.0, 3.0 / 4, -3.0 / 20, 1.0 / 60)
diffusion = 0.05
velocity = (0.6, -0.5, 0.4)
relaxation = 0.6

TAPS = [
    [diffusion * second_taps[o] - velocity[d] * first_taps[o] for o in range(7)] for d in range(3)
]
CENTER = 1.0 + sum(TAPS[d][3] for d in range(3))
OFFSETS = (-3, -2, -1, 1, 2, 3)
HIGHEST = lax.Precision.HIGHEST
MESH = pl.DeviceIdType.MESH
BF16 = jnp.bfloat16
F32 = jnp.float32


OTHERS = sorted(
    itertools.product(range(4), range(2), range(4), range(4)),
    key=lambda o: -10 * sum(min(o[i], 4 - o[i]) for i in (0, 2, 3)) - o[1],
)[:-1]


def tap(dim, j):
    return TAPS[dim][j + 3]


def split(value):
    high = value.astype(BF16)
    low = (value - high.astype(F32)).astype(BF16)
    return high, low


def three_term(values, right):
    high, low = split(values)
    return jnp.dot(
        jnp.concatenate([high, low, high], axis=1), right, preferred_element_type=F32
    )


def kernel(
    flow_hbm, near_hbm, owner_hbm, block_hbm, offset_hbm, weights_hbm,
    flow_out, near_out,
    g0, g1, res, hx, hy, sy,
    near_in, owner_in, block_in, offset_in, weights_in,
    a1, b1, bt, c1, d1, fin, table, tables,
    ohot, ohot_low, band_z, lhs, wz_rhs, near_rhs, plane, plane_z, pad_x, pad_y, pad_z, pick, recip,
    in_sem, small_sem, halo_send, halo_recv, row_send, row_recv, vouched,
    table_send, table_recv,
):
    gx = lax.axis_index("gx")
    gy = lax.axis_index("gy")
    me = gx * GY + gy
    chip_x, core = gx // 2, lax.rem(gx, 2)
    chip_z, chip_y = gy // 4, lax.rem(gy, 4)

    placed = [
        (
            (dx, dc, dz, dy),
            (
                lax.rem(chip_x + dx, 4) * 2 + lax.rem(core + dc, 2),
                lax.rem(chip_z + dz, 4) * 4 + lax.rem(chip_y + dy, 4),
            ),
        )
        for dx, dc, dz, dy in OTHERS
    ]

    along_x = [(px, py) for o, (px, py) in placed if o[2] == o[3] == 0]
    along_y = [(gx, py) for o, (px, py) in placed if o[0] == o[1] == o[2] == 0]
    along_z = [(gx, py) for o, (px, py) in placed if o[0] == o[1] == o[3] == 0]
    plane_yz = [(gx, py) for o, (px, py) in placed if o[0] == o[1] == 0]
    barrier = pltpu.get_barrier_semaphore()
    for peer in along_y + along_z + along_x:
        pl.semaphore_signal(barrier, inc=1, device_id=peer, device_id_type=MESH)
    after = (chip_y == 3) & (gy < GY - 1)
    before = (chip_y == 0) & (gy > 0)

    @pl.when(after)
    def _():
        pl.semaphore_signal(barrier, inc=1, device_id=(gx, gy + 1), device_id_type=MESH)

    @pl.when(before)
    def _():
        pl.semaphore_signal(barrier, inc=1, device_id=(gx, gy - 1), device_id_type=MESH)

    greeted = GX + 5 + after.astype(jnp.int32) + before.astype(jnp.int32)

    small = [
        pltpu.make_async_copy(src, dst, small_sem.at[i])
        for i, (src, dst) in enumerate(
            (
                (owner_hbm, owner_in),
                (block_hbm, block_in),
                (offset_hbm, offset_in),
                (near_hbm, near_in),
                (weights_hbm, weights_in),
            )
        )
    ]
    for copy in small:
        copy.start()

    def flow_in(v):
        return pltpu.make_async_copy(
            flow_hbm.at[v], g0.at[v, pl.ds(3, CX), pl.ds(Y0, CY)], in_sem.at[v]
        )

    for v in range(NV):
        flow_in(v).start()

    for copy in small:
        copy.wait()
    row = lax.broadcasted_iota(jnp.int32, (FR, FR), 0)
    col = lax.broadcasted_iota(jnp.int32, (FR, FR), 1)
    owner_wide = jnp.broadcast_to(owner_in[...], (FR, FR))
    owner_tall = jnp.transpose(owner_wide)
    earlier = jnp.where((owner_wide == owner_tall) & (row < col), 1.0, 0.0).astype(F32)
    rank = jnp.sum(earlier, axis=0, keepdims=True)
    mine = owner_wide == row
    ohot[0] = jnp.where(mine & (rank < 0.5), 1.0, 0.0).astype(F32)
    ohot[1] = jnp.where(mine & (rank > 0.5), 1.0, 0.0).astype(F32)
    ohot_low[...] = ohot[...].reshape(2 * DEVICES, FR).astype(BF16)
    payload = jnp.concatenate(
        [
            weights_in[...],
            near_in[...],
            block_in[...].astype(F32),
            offset_in[...].astype(F32),
            jnp.ones((1, FR), F32),
        ],
        axis=0,
    )
    nothing = jnp.zeros((32, FR), F32)
    blank = jnp.zeros((64, FR), F32)
    contract_last = (((1,), (1,)), ((), ()))
    a1[...] = lax.dot_general(
        ohot[0], jnp.concatenate([payload, nothing, blank], axis=0), contract_last,
        precision=HIGHEST, preferred_element_type=F32,
    ) + lax.dot_general(
        ohot[1], jnp.concatenate([nothing, payload, blank], axis=0), contract_last,
        precision=HIGHEST, preferred_element_type=F32,
    )

    targets = ((gx + 1, gy), (gx - 1, gy), (gx, gy + 1), (gx, gy - 1))
    sends = (gx < GX - 1, gx > 0, gy < GY - 1, gy > 0)
    takes = (gx > 0, gx < GX - 1, gy > 0, gy < GY - 1)

    def face(step, side):
        if side < 2:
            layers = pl.ds(CX if side == 0 else 3, 3)
            src, dst = (g0, g1)[step].at[:, layers, pl.ds(Y0, CY)], hx.at[step, side]
        else:
            src, dst = sy.at[step, side - 2], hy.at[step, side - 2]
        return pltpu.make_async_remote_copy(
            src_ref=src, dst_ref=dst,
            send_sem=halo_send.at[step, side], recv_sem=halo_recv.at[step, side],
            device_id=targets[side], device_id_type=MESH,
        )

    def pack_faces(step, v):
        flat = (g0, g1)[step].reshape(NV * PX * PY, CZ)
        for side, first in ((0, CY - 3), (1, 0)):
            for j in range(3):
                for half in range(2):
                    start = (v * PX + 3 + 8 * half) * PY + Y0 + first + j
                    sy[step, side, v, pl.ds(j * CX + 8 * half, 8)] = flat[pl.ds(start, 8, PY)]

    def interior(step):
        g = (g0, g1)[step]

        def body(v, carry):
            mid = g[v, 3 : 3 + CX, Y0 : Y0 + CY]
            total = mid * CENTER
            for j in OFFSETS:
                total = total + g[v, 3 + j : 3 + j + CX, Y0 : Y0 + CY] * tap(0, j)
            for j in OFFSETS:
                total = total + g[v, 3 : 3 + CX, Y0 + j : Y0 + CY + j] * tap(1, j)
            z_part = three_term(mid.reshape(CX * CY, CZ), band_z[...])
            res[pl.ds(v * CX, CX)] = total + z_part.reshape(CX, CY, CZ)
            return carry

        lax.fori_loop(0, NV, body, 0)

    def rows_to(src, source, count, dst, target, phase, peer):
        pltpu.make_async_remote_copy(
            src_ref=src.at[pl.ds(source, count)], dst_ref=dst.at[pl.ds(target, count)],
            send_sem=row_send.at[phase], recv_sem=row_recv.at[phase],
            device_id=peer, device_id_type=MESH,
        ).start()

    def rows_wait(buf, count, sem):
        part = buf.at[pl.ds(0, count)]
        pltpu.make_async_copy(part, part, sem).wait()

    x_rows = pl.ds(pl.multiple_of(gx * GY, GY), GY)
    b1[x_rows] = a1[x_rows]
    pl.semaphore_wait(barrier, greeted)
    for peer in along_y:
        pl.semaphore_signal(vouched, inc=1, device_id=peer, device_id_type=MESH)
    for peer in along_x:
        rows_to(a1, pl.multiple_of(peer[0] * GY, GY), GY, b1, pl.multiple_of(gx * GY, GY), 0, peer)

    def first_faces(v, carry):
        flow_in(v).wait()
        pack_faces(0, v)
        return carry

    lax.fori_loop(0, NV, first_faces, 0)
    for side in range(4):
        @pl.when(sends[side])
        def _():
            face(0, side).start()

    for side in range(4):
        @pl.when(jnp.logical_not(takes[side]))
        def _():
            halo = (hx, hx, hy, hy)[side]
            for step in range(STEPS):
                halo[step, side % 2] = jnp.zeros(halo.shape[2:], F32)
            tables[side] = jnp.zeros((32, SLOTS), F32)

    def clear(v, carry):
        for g in (g0, g1):
            g[v, 0:3, Y0 : Y0 + CY] = jnp.zeros((3, CY, CZ), F32)
            g[v, PX - 3 : PX, Y0 : Y0 + CY] = jnp.zeros((3, CY, CZ), F32)
            g[v, 3 : PX - 3, 0:Y0] = jnp.zeros((CX, Y0, CZ), F32)
            g[v, 3 : PX - 3, Y0 + CY : PY] = jnp.zeros((CX, PY - Y0 - CY, CZ), F32)
        return carry

    lax.fori_loop(0, NV, clear, 0)
    for pad in (pad_x, pad_y, pad_z):
        size = pad.shape[0]
        pad[0:8] = jnp.zeros((8, SLOTS), F32)
        pad[size - 8 : size] = jnp.zeros((8, SLOTS), F32)

    z_from = lax.broadcasted_iota(jnp.int32, (CZ, CZ), 0)
    z_to = lax.broadcasted_iota(jnp.int32, (CZ, CZ), 1)
    band = jnp.zeros((CZ, CZ), F32)
    for j in OFFSETS:
        band = jnp.where(z_from - z_to == j, tap(2, j), band)
    band_high, band_low = split(band)
    band_z[0:CZ] = band_high
    band_z[CZ : 2 * CZ] = band_high
    band_z[2 * CZ :] = band_low

    interior(0)
    rows_wait(b1, DEVICES - GY, row_recv.at[0])
    for h in range(GY):
        bt[h * GX : (h + 1) * GX] = b1[pl.ds(h, GX, GY)]
    y_rows = pl.ds(pl.multiple_of(gy * GX, GX), GX)
    c1[y_rows] = bt[y_rows]
    pl.semaphore_wait(vouched, 3)
    for peer in plane_yz:
        rows_to(bt, pl.multiple_of(peer[1] * GX, GX), GX, c1, pl.multiple_of(gy * GX, GX), 1, peer)

    flat_res = res.reshape(NV * CX * CY, CZ)

    def add_halo(step, v):
        for r in range(3):
            low = res[v * CX + r]
            high = res[v * CX + CX - 1 - r]
            for j in range(-3, -r):
                low = low + hx[step, 0, v, r + j + 3] * tap(0, j)
                high = high + hx[step, 1, v, -r - 1 - j] * tap(0, -j)
            res[v * CX + r] = low
            res[v * CX + CX - 1 - r] = high
        for r in range(3):
            for half in range(2):
                start = (v * CX + 8 * half) * CY
                at_low = pl.ds(start + r, 8, CY)
                at_high = pl.ds(start + CY - 1 - r, 8, CY)
                low = flat_res[at_low]
                high = flat_res[at_high]
                for j in range(-3, -r):
                    low = low + hy[step, 0, v, pl.ds((r + j + 3) * CX + 8 * half, 8)] * tap(1, j)
                    high = high + hy[step, 1, v, pl.ds((-r - 1 - j) * CX + 8 * half, 8)] * tap(1, -j)
                flat_res[at_low] = low
                flat_res[at_high] = high

    def variable(v):
        start = v * CX * CY
        return pl.ds(start if isinstance(v, int) else pl.multiple_of(start, CX * CY), CX * CY)

    for side in range(4):
        @pl.when(takes[side])
        def _():
            face(0, side).wait_recv()

    def first_lhs(v, carry):
        add_halo(0, v)
        high, low = split(flat_res[variable(v)])
        lhs[variable(v), 0:CZ] = high
        lhs[variable(v), CZ : 2 * CZ] = low
        lhs[variable(v), 2 * CZ :] = high
        return carry

    lax.fori_loop(0, NV, first_lhs, 0)

    rows_wait(c1, DEVICES - GX, row_recv.at[1])
    turned = jnp.transpose(c1[...])
    table[:, 0:DEVICES] = turned[0:32]
    table[:, DEVICES:] = turned[32:64]

    def table_copy(side):
        return pltpu.make_async_remote_copy(
            src_ref=table, dst_ref=tables.at[side],
            send_sem=table_send.at[side], recv_sem=table_recv.at[side],
            device_id=targets[side], device_id_type=MESH,
        )

    for side in (2, 3, 0, 1):
        @pl.when(sends[side])
        def _():
            table_copy(side).start()

    row8 = lax.broadcasted_iota(jnp.int32, (8, SLOTS), 0)

    def weights_of(asked):
        block = asked[29:30].astype(jnp.int32)
        places = (block // 64, (block // 16) % 4, block % 16)
        spread = [
            jnp.concatenate(
                [jnp.where(place == b, asked[8 * d : 8 * d + 8], 0.0) for b in range(size // 8)],
                axis=0,
            )
            for d, (place, size) in enumerate(zip(places, (CX, CY, CZ)))
        ]
        return places, spread

    def put_three(ref, at, values):
        high, low = split(values)
        ref[0:CZ, at] = high
        ref[CZ : 2 * CZ, at] = high
        ref[2 * CZ :, at] = low

    asked = table[...]
    (kx, ky, kz), (weights_x, weights_y, weights_z) = weights_of(asked)
    last = asked[24:32]
    offset = last[6:7].astype(jnp.int32)
    live = last[7:8]
    near = jnp.where(row8 < NV, last, 0.0)
    put_three(wz_rhs, slice(0, SLOTS), weights_z)
    for x in range(CX):
        plane[x * CY : (x + 1) * CY] = weights_x[x : x + 1] * weights_y
    cell = (8 * kx + offset // 64) * CY + 8 * ky + (offset // 8) % 8
    cell = jnp.where(live > 0.5, cell, -1)
    cell_z = 8 * kz + offset % 8
    places = lax.broadcasted_iota(jnp.int32, (CX * CY, SLOTS), 0)
    picked = jnp.where(places == cell, 1.0, 0.0).astype(F32).astype(BF16)
    pick[:, 0:SLOTS] = picked
    pick[:, SLOTS:] = picked
    places_z = lax.broadcasted_iota(jnp.int32, (CZ, SLOTS), 0)
    hot_z = jnp.where(places_z == cell_z, 1.0, 0.0).astype(F32).astype(BF16)
    counts = lax.dot_general(
        picked, hot_z, contract_last, preferred_element_type=F32
    )
    recip[...] = 1.0 / (1.0 + counts)

    def moved(pad, values, dim):
        size = values.shape[0]
        pad[8 : 8 + size] = values
        total = jnp.zeros_like(values)
        for j in OFFSETS:
            total = total + pad[8 - j : 8 - j + size] * tap(dim, j)
        return total

    moved_x = weights_x * CENTER + moved(pad_x, weights_x, 0)
    moved_y = moved(pad_y, weights_y, 1)
    put_three(wz_rhs, slice(SLOTS, 2 * SLOTS), moved(pad_z, weights_z, 2))
    for x in range(CX):
        plane_z[x * CY : (x + 1) * CY] = (
            moved_x[x : x + 1] * weights_y + weights_x[x : x + 1] * moved_y
        )

    def relaxed(step, near):
        def body(v, interp):
            if step == 0:
                t = jnp.dot(lhs[variable(v)], wz_rhs[:, 0:SLOTS], preferred_element_type=F32)
            else:
                add_halo(1, v)
                t = three_term(flat_res[variable(v)], wz_rhs[:, 0:SLOTS])
            here = jnp.sum(t * plane[...], axis=0, keepdims=True)
            return jnp.where(row8 == v, here, interp)

        if step == 1:
            for side in range(4):
                @pl.when(takes[side])
                def _():
                    face(1, side).wait_recv()
        interp = lax.fori_loop(0, NV, body, jnp.zeros((8, SLOTS), F32), unroll=True)
        return near + relaxation * (interp - near)

    def injected(near):
        right = []
        for v in range(NV):
            high, low = split(jnp.broadcast_to(near[v : v + 1], (16, SLOTS)))
            hot = hot_z.reshape(CZ // 16, 16, SLOTS)
            right.append(
                jnp.concatenate(
                    [
                        (hot * high[None]).reshape(CZ, SLOTS),
                        (hot * low[None]).reshape(CZ, SLOTS),
                    ],
                    axis=1,
                )
            )
        gained = lax.dot_general(
            pick[...], jnp.concatenate(right, axis=0), contract_last, preferred_element_type=F32
        )
        for v in range(NV):
            part = gained[:, v * CZ : (v + 1) * CZ]
            yield v, ((flat_res[variable(v)] + part) * recip[...]).reshape(CX, CY, CZ)

    near = relaxed(0, near)

    for v, values in injected(near):
        g1[v, 3 : 3 + CX, Y0 : Y0 + CY] = values
        pack_faces(1, v)
        high, low = split(values.reshape(CX * CY, CZ))
        lhs[variable(v), 0:CZ] = high
        lhs[variable(v), CZ : 2 * CZ] = low
        lhs[variable(v), 2 * CZ :] = high
    for side in range(4):
        @pl.when(sends[side])
        def _():
            face(1, side).start()

    def own_part(v, own):
        t = jnp.dot(lhs[variable(v)], wz_rhs[...], preferred_element_type=F32)
        both = t[:, 0:SLOTS] * plane_z[...] + t[:, SLOTS:] * plane[...]
        return jnp.where(row8 == v, jnp.sum(both, axis=0, keepdims=True), own)

    own = lax.fori_loop(0, NV, own_part, jnp.zeros((8, SLOTS), F32), unroll=True)
    parts = [near + relaxation * (own - near)]
    for side in range(4):
        if side % 2 == 0:
            for other in (side, side + 1):
                @pl.when(takes[other])
                def _():
                    table_copy(other).wait_recv()
        _, spread = weights_of(tables[side])
        put_three(near_rhs.at[side], slice(0, SLOTS), spread[2])
        dim = side // 2
        across, beside = spread[dim], spread[1 - dim]
        size = across.shape[0]
        reach = []
        for i in range(3):
            total = jnp.zeros((1, SLOTS), F32)
            for j in range(1, 4):
                if side % 2 == 0 and j > i:
                    total = total + across[size + i - j : size + i - j + 1] * tap(dim, j)
                if side % 2 == 1 and j >= 3 - i:
                    total = total + across[i - 3 + j : i - 2 + j] * tap(dim, -j)
            reach.append(total * beside)
        reach = jnp.concatenate(reach, axis=0)
        if dim == 0:
            first = 0 if side == 0 else (CX - 3) * CY
            left = jnp.concatenate(
                [lhs[v * CX * CY + first : v * CX * CY + first + 3 * CY] for v in range(NV)], axis=0
            )
            t = jnp.dot(left, near_rhs[side], preferred_element_type=F32)
        else:
            t = three_term(sy[1, 3 - side].reshape(NV * 3 * CX, CZ), near_rhs[side])
        rows = reach.shape[0]
        added = jnp.zeros((8, SLOTS), F32)
        for v in range(NV):
            here = jnp.sum(t[v * rows : (v + 1) * rows] * reach, axis=0, keepdims=True)
            added = jnp.where(row8 == v, here, added)
        parts.append(relaxation * added)

    back = jnp.concatenate(
        [part[:, half : half + DEVICES] for part in parts for half in (0, DEVICES)]
        + [jnp.zeros((DEVICES - 80, DEVICES), F32)],
        axis=0,
    )
    d1[...] = jnp.transpose(back)
    for _, (px, py) in placed:
        rows_to(d1, py * GX + px, 1, fin, me, 2, (px, py))
    fin[pl.ds(me, 1)] = d1[pl.ds(gy * GX + gx, 1)]

    interior(1)
    near = relaxed(1, near)

    for v, values in injected(near):
        flow_out[v] = values

    rows_wait(a1, DEVICES - GY, row_send.at[0])
    rows_wait(bt, DEVICES - GX, row_send.at[1])
    for side in range(4):
        @pl.when(sends[side])
        def _():
            face(0, side).wait_send()
            face(1, side).wait_send()
            table_copy(side).wait_send()

    rows_wait(d1, DEVICES - 1, row_send.at[2])
    rows_wait(fin, DEVICES - 1, row_recv.at[2])
    returned = jnp.transpose(fin[...])
    total = returned[0:16]
    for side, shift in enumerate((DEVICES - GY, GY, DEVICES - 1, 1)):
        total = total + pltpu.roll(returned[16 + 16 * side : 32 + 16 * side], shift, axis=1)
    total = jnp.concatenate([total[0:8], total[8:16]], axis=1)
    high, low = split(total)
    rest = total - high.astype(F32) - low.astype(F32)
    served = jnp.dot(
        jnp.concatenate([high.astype(F32), low.astype(F32), rest], axis=0).astype(BF16),
        ohot_low[...], preferred_element_type=F32,
    )
    near_out[...] = (served[0:8] + served[8:16] + served[16:24])[0:NV]


def hand_over(flow_vmem, near_vmem, flow_out, near_out, sems):
    copies = [
        pltpu.make_async_copy(flow_vmem, flow_out, sems.at[0]),
        pltpu.make_async_copy(near_vmem, near_out, sems.at[1]),
    ]
    for copy in copies:
        copy.start()
    for copy in copies:
        copy.wait()


def shards(flow, near, donor_owner, donor_block, recv_offset, weights):
    hbm = pl.BlockSpec(memory_space=pltpu.HBM)
    whole = pl.BlockSpec(memory_space=pltpu.VMEM)
    vmem = pltpu.VMEM
    dma = pltpu.SemaphoreType.DMA
    operands = (
        flow,
        near,
        donor_owner.reshape(1, FR),
        donor_block.reshape(1, FR),
        recv_offset.reshape(1, FR),
        weights.reshape(24, FR),
    )
    flow, near = pl.pallas_call(
        kernel,
        out_shape=(vmem((NV, CX, CY, CZ), F32), vmem((NV, FR), F32)),
        in_specs=[hbm] * 6,
        out_specs=(whole, whole),
        scratch_shapes=[
            vmem((NV, PX, PY, CZ), F32),
            vmem((NV, PX, PY, CZ), F32),
            vmem((NV * CX, CY, CZ), F32),
            vmem((STEPS, 2, NV, 3, CY, CZ), F32),
            vmem((STEPS, 2, NV, 3 * CX, CZ), F32),
            vmem((STEPS, 2, NV, 3 * CX, CZ), F32),
            vmem((NV, FR), F32),
            vmem((1, FR), jnp.int32),
            vmem((1, FR), jnp.int32),
            vmem((1, FR), jnp.int32),
            vmem((24, FR), F32),
            vmem((DEVICES, 128), F32),
            vmem((DEVICES, 128), F32),
            vmem((DEVICES, 128), F32),
            vmem((DEVICES, 128), F32),
            vmem((DEVICES, 128), F32),
            vmem((DEVICES, 128), F32),
            vmem((32, SLOTS), F32),
            vmem((4, 32, SLOTS), F32),
            vmem((2, DEVICES, FR), F32),
            vmem((2 * DEVICES, FR), BF16),
            vmem((3 * CZ, CZ), BF16),
            vmem((NV * CX * CY, 3 * CZ), BF16),
            vmem((3 * CZ, 2 * SLOTS), BF16),
            vmem((4, 3 * CZ, SLOTS), BF16),
            vmem((CX * CY, SLOTS), F32),
            vmem((CX * CY, SLOTS), F32),
            vmem((CX + 16, SLOTS), F32),
            vmem((CY + 16, SLOTS), F32),
            vmem((CZ + 16, SLOTS), F32),
            vmem((CX * CY, 2 * SLOTS), BF16),
            vmem((CX * CY, CZ), F32),
            dma((NV,)),
            dma((5,)),
            dma((STEPS, 4)),
            dma((STEPS, 4)),
            dma((3,)),
            dma((3,)),
            pltpu.SemaphoreType.REGULAR,
            dma((4,)),
            dma((4,)),
        ],
        compiler_params=pltpu.CompilerParams(
            collective_id=0, has_side_effects=True, vmem_limit_bytes=40 * 1024 * 1024
        ),
        cost_estimate=pl.CostEstimate(
            flops=2 * STEPS * 20 * NV * CX * CY * CZ,
            bytes_accessed=2 * 4 * NV * CX * CY * CZ,
            transcendentals=0,
        ),
        name="rotor_wake_steps",
    )(*[pltpu.with_memory_space_constraint(operand, pltpu.HBM) for operand in operands])
    return pl.pallas_call(
        hand_over,
        out_shape=(
            jax.ShapeDtypeStruct((NV, CX, CY, CZ), F32),
            jax.ShapeDtypeStruct((NV, FR), F32),
        ),
        in_specs=[whole, whole],
        out_specs=(hbm, hbm),
        scratch_shapes=[dma((2,))],
        name="hand_over",
    )(
        pltpu.with_memory_space_constraint(flow, pltpu.VMEM),
        pltpu.with_memory_space_constraint(near, pltpu.VMEM),
    )


def solution(mesh):
    in_specs = (
        P(None, "gx", "gy", None),
        P(None, ("gx", "gy")),
        P(("gx", "gy"), None),
        P(("gx", "gy")),
        P(("gx", "gy")),
        P(None, None, ("gx", "gy")),
    )
    out_specs = (P(None, "gx", "gy", None), P(None, ("gx", "gy")))
    return jax.shard_map(shards, mesh=mesh, in_specs=in_specs, out_specs=out_specs, check_vma=False)
```

```python
import itertools

import jax
import jax.numpy as jnp
from jax import lax
from jax.experimental import pallas as pl
from jax.experimental.pallas import tpu as pltpu
from jax.sharding import PartitionSpec as P

STEPS = 2
NV = 5
CX = 16
CY = 32
CZ = 128
FR = 128
GX = 8
GY = 16
DEVICES = GX * GY
SLOTS = 2 * DEVICES
PX = CX + 6
PY = CY + 16
Y0 = 8

second_taps = (1.0 / 90, -3.0 / 20, 3.0 / 2, -49.0 / 18, 3.0 / 2, -3.0 / 20, 1.0 / 90)
first_taps = (-1.0 / 60, 3.0 / 20, -3.0 / 4, 0.0, 3.0 / 4, -3.0 / 20, 1.0 / 60)
diffusion = 0.05
velocity = (0.6, -0.5, 0.4)
relaxation = 0.6

TAPS = [
    [diffusion * second_taps[o] - velocity[d] * first_taps[o] for o in range(7)] for d in range(3)
]
CENTER = 1.0 + sum(TAPS[d][3] for d in range(3))
OFFSETS = (-3, -2, -1, 1, 2, 3)
HIGHEST = lax.Precision.HIGHEST
MESH = pl.DeviceIdType.MESH
BF16 = jnp.bfloat16
F32 = jnp.float32


OTHERS = sorted(
    itertools.product(range(4), range(2), range(4), range(4)),
    key=lambda o: -10 * sum(min(o[i], 4 - o[i]) for i in (0, 2, 3)) - o[1],
)[:-1]


def tap(dim, j):
    return TAPS[dim][j + 3]


def split(value):
    high = value.astype(BF16)
    low = (value - high.astype(F32)).astype(BF16)
    return high, low


def three_term(values, right):
    high, low = split(values)
    return jnp.dot(
        jnp.concatenate([high, low, high], axis=1), right, preferred_element_type=F32
    )


def kernel(
    flow_hbm, near_hbm, owner_hbm, block_hbm, offset_hbm, weights_hbm,
    flow_out, near_out,
    g0, g1, res, hx, hy, sy,
    near_in, owner_in, block_in, offset_in, weights_in,
    a1, b1, bt, c1, d1, fin, table, tables,
    ohot, ohot_low, band_z, lhs, wz_rhs, near_rhs, plane, plane_z, pad_x, pad_y, pad_z, pick, recip,
    in_sem, small_sem, halo_send, halo_recv, row_send, row_recv, vouched,
    table_send, table_recv,
):
    gx = lax.axis_index("gx")
    gy = lax.axis_index("gy")
    me = gx * GY + gy
    chip_x, core = gx // 2, lax.rem(gx, 2)
    chip_z, chip_y = gy // 4, lax.rem(gy, 4)

    placed = [
        (
            (dx, dc, dz, dy),
            (
                lax.rem(chip_x + dx, 4) * 2 + lax.rem(core + dc, 2),
                lax.rem(chip_z + dz, 4) * 4 + lax.rem(chip_y + dy, 4),
            ),
        )
        for dx, dc, dz, dy in OTHERS
    ]

    along_x = [(px, py) for o, (px, py) in placed if o[2] == o[3] == 0]
    along_y = [(gx, py) for o, (px, py) in placed if o[0] == o[1] == o[2] == 0]
    along_z = [(gx, py) for o, (px, py) in placed if o[0] == o[1] == o[3] == 0]
    plane_yz = [(gx, py) for o, (px, py) in placed if o[0] == o[1] == 0]
    barrier = pltpu.get_barrier_semaphore()
    for peer in along_z + along_y + along_x:
        pl.semaphore_signal(barrier, inc=1, device_id=peer, device_id_type=MESH)
    after = (chip_y == 3) & (gy < GY - 1)
    before = (chip_y == 0) & (gy > 0)

    @pl.when(after)
    def _():
        pl.semaphore_signal(barrier, inc=1, device_id=(gx, gy + 1), device_id_type=MESH)

    @pl.when(before)
    def _():
        pl.semaphore_signal(barrier, inc=1, device_id=(gx, gy - 1), device_id_type=MESH)

    greeted = GX + 5 + after.astype(jnp.int32) + before.astype(jnp.int32)

    small = [
        pltpu.make_async_copy(src, dst, small_sem.at[i])
        for i, (src, dst) in enumerate(
            (
                (owner_hbm, owner_in),
                (block_hbm, block_in),
                (offset_hbm, offset_in),
                (near_hbm, near_in),
                (weights_hbm, weights_in),
            )
        )
    ]
    for copy in small:
        copy.start()

    def flow_in(v):
        return pltpu.make_async_copy(
            flow_hbm.at[v], g0.at[v, pl.ds(3, CX), pl.ds(Y0, CY)], in_sem.at[v]
        )

    for v in range(NV):
        flow_in(v).start()

    for copy in small:
        copy.wait()
    row = lax.broadcasted_iota(jnp.int32, (FR, FR), 0)
    col = lax.broadcasted_iota(jnp.int32, (FR, FR), 1)
    owner_wide = jnp.broadcast_to(owner_in[...], (FR, FR))
    owner_tall = jnp.transpose(owner_wide)
    earlier = jnp.where((owner_wide == owner_tall) & (row < col), 1.0, 0.0).astype(F32)
    rank = jnp.sum(earlier, axis=0, keepdims=True)
    mine = owner_wide == row
    ohot[0] = jnp.where(mine & (rank < 0.5), 1.0, 0.0).astype(F32)
    ohot[1] = jnp.where(mine & (rank > 0.5), 1.0, 0.0).astype(F32)
    ohot_low[...] = ohot[...].reshape(2 * DEVICES, FR).astype(BF16)
    payload = jnp.concatenate(
        [
            weights_in[...],
            near_in[...],
            block_in[...].astype(F32),
            offset_in[...].astype(F32),
            jnp.ones((1, FR), F32),
        ],
        axis=0,
    )
    nothing = jnp.zeros((32, FR), F32)
    blank = jnp.zeros((64, FR), F32)
    contract_last = (((1,), (1,)), ((), ()))
    a1[...] = lax.dot_general(
        ohot[0], jnp.concatenate([payload, nothing, blank], axis=0), contract_last,
        precision=HIGHEST, preferred_element_type=F32,
    ) + lax.dot_general(
        ohot[1], jnp.concatenate([nothing, payload, blank], axis=0), contract_last,
        precision=HIGHEST, preferred_element_type=F32,
    )

    targets = ((gx + 1, gy), (gx - 1, gy), (gx, gy + 1), (gx, gy - 1))
    sends = (gx < GX - 1, gx > 0, gy < GY - 1, gy > 0)
    takes = (gx > 0, gx < GX - 1, gy > 0, gy < GY - 1)

    def face(step, side):
        if side < 2:
            layers = pl.ds(CX if side == 0 else 3, 3)
            src, dst = (g0, g1)[step].at[:, layers, pl.ds(Y0, CY)], hx.at[step, side]
        else:
            src, dst = sy.at[step, side - 2], hy.at[step, side - 2]
        return pltpu.make_async_remote_copy(
            src_ref=src, dst_ref=dst,
            send_sem=halo_send.at[step, side], recv_sem=halo_recv.at[step, side],
            device_id=targets[side], device_id_type=MESH,
        )

    def pack_faces(step, v):
        flat = (g0, g1)[step].reshape(NV * PX * PY, CZ)
        for side, first in ((0, CY - 3), (1, 0)):
            for j in range(3):
                for half in range(2):
                    start = (v * PX + 3 + 8 * half) * PY + Y0 + first + j
                    sy[step, side, v, pl.ds(j * CX + 8 * half, 8)] = flat[pl.ds(start, 8, PY)]

    def interior(step):
        g = (g0, g1)[step]

        def body(v, carry):
            mid = g[v, 3 : 3 + CX, Y0 : Y0 + CY]
            total = mid * CENTER
            for j in OFFSETS:
                total = total + g[v, 3 + j : 3 + j + CX, Y0 : Y0 + CY] * tap(0, j)
            for j in OFFSETS:
                total = total + g[v, 3 : 3 + CX, Y0 + j : Y0 + CY + j] * tap(1, j)
            z_part = three_term(mid.reshape(CX * CY, CZ), band_z[...])
            res[pl.ds(v * CX, CX)] = total + z_part.reshape(CX, CY, CZ)
            return carry

        lax.fori_loop(0, NV, body, 0)

    def rows_to(src, source, count, dst, target, phase, peer):
        pltpu.make_async_remote_copy(
            src_ref=src.at[pl.ds(source, count)], dst_ref=dst.at[pl.ds(target, count)],
            send_sem=row_send.at[phase], recv_sem=row_recv.at[phase],
            device_id=peer, device_id_type=MESH,
        ).start()

    def rows_wait(buf, count, sem):
        part = buf.at[pl.ds(0, count)]
        pltpu.make_async_copy(part, part, sem).wait()

    x_rows = pl.ds(pl.multiple_of(gx * GY, GY), GY)
    b1[x_rows] = a1[x_rows]
    pl.semaphore_wait(barrier, greeted)
    for peer in along_y:
        pl.semaphore_signal(vouched, inc=1, device_id=peer, device_id_type=MESH)
    for peer in along_x:
        rows_to(a1, pl.multiple_of(peer[0] * GY, GY), GY, b1, pl.multiple_of(gx * GY, GY), 0, peer)

    def first_faces(v, carry):
        flow_in(v).wait()
        pack_faces(0, v)
        return carry

    lax.fori_loop(0, NV, first_faces, 0)
    for side in range(4):
        @pl.when(sends[side])
        def _():
            face(0, side).start()

    for side in range(4):
        @pl.when(jnp.logical_not(takes[side]))
        def _():
            halo = (hx, hx, hy, hy)[side]
            for step in range(STEPS):
                halo[step, side % 2] = jnp.zeros(halo.shape[2:], F32)
            tables[side] = jnp.zeros((32, SLOTS), F32)

    def clear(v, carry):
        for g in (g0, g1):
            g[v, 0:3, Y0 : Y0 + CY] = jnp.zeros((3, CY, CZ), F32)
            g[v, PX - 3 : PX, Y0 : Y0 + CY] = jnp.zeros((3, CY, CZ), F32)
            g[v, 3 : PX - 3, 0:Y0] = jnp.zeros((CX, Y0, CZ), F32)
            g[v, 3 : PX - 3, Y0 + CY : PY] = jnp.zeros((CX, PY - Y0 - CY, CZ), F32)
        return carry

    lax.fori_loop(0, NV, clear, 0)
    for pad in (pad_x, pad_y, pad_z):
        size = pad.shape[0]
        pad[0:8] = jnp.zeros((8, SLOTS), F32)
        pad[size - 8 : size] = jnp.zeros((8, SLOTS), F32)

    z_from = lax.broadcasted_iota(jnp.int32, (CZ, CZ), 0)
    z_to = lax.broadcasted_iota(jnp.int32, (CZ, CZ), 1)
    band = jnp.zeros((CZ, CZ), F32)
    for j in OFFSETS:
        band = jnp.where(z_from - z_to == j, tap(2, j), band)
    band_high, band_low = split(band)
    band_z[0:CZ] = band_high
    band_z[CZ : 2 * CZ] = band_high
    band_z[2 * CZ :] = band_low

    interior(0)
    rows_wait(b1, DEVICES - GY, row_recv.at[0])
    for h in range(GY):
        bt[h * GX : (h + 1) * GX] = b1[pl.ds(h, GX, GY)]
    y_rows = pl.ds(pl.multiple_of(gy * GX, GX), GX)
    c1[y_rows] = bt[y_rows]
    pl.semaphore_wait(vouched, 3)
    for peer in plane_yz:
        rows_to(bt, pl.multiple_of(peer[1] * GX, GX), GX, c1, pl.multiple_of(gy * GX, GX), 1, peer)

    flat_res = res.reshape(NV * CX * CY, CZ)

    def add_halo(step, v):
        for r in range(3):
            low = res[v * CX + r]
            high = res[v * CX + CX - 1 - r]
            for j in range(-3, -r):
                low = low + hx[step, 0, v, r + j + 3] * tap(0, j)
                high = high + hx[step, 1, v, -r - 1 - j] * tap(0, -j)
            res[v * CX + r] = low
            res[v * CX + CX - 1 - r] = high
        for r in range(3):
            for half in range(2):
                start = (v * CX + 8 * half) * CY
                at_low = pl.ds(start + r, 8, CY)
                at_high = pl.ds(start + CY - 1 - r, 8, CY)
                low = flat_res[at_low]
                high = flat_res[at_high]
                for j in range(-3, -r):
                    low = low + hy[step, 0, v, pl.ds((r + j + 3) * CX + 8 * half, 8)] * tap(1, j)
                    high = high + hy[step, 1, v, pl.ds((-r - 1 - j) * CX + 8 * half, 8)] * tap(1, -j)
                flat_res[at_low] = low
                flat_res[at_high] = high

    def variable(v):
        start = v * CX * CY
        return pl.ds(start if isinstance(v, int) else pl.multiple_of(start, CX * CY), CX * CY)

    for side in range(4):
        @pl.when(takes[side])
        def _():
            face(0, side).wait_recv()

    def first_lhs(v, carry):
        add_halo(0, v)
        high, low = split(flat_res[variable(v)])
        lhs[variable(v), 0:CZ] = high
        lhs[variable(v), CZ : 2 * CZ] = low
        lhs[variable(v), 2 * CZ :] = high
        return carry

    lax.fori_loop(0, NV, first_lhs, 0)

    rows_wait(c1, DEVICES - GX, row_recv.at[1])
    turned = jnp.transpose(c1[...])
    table[:, 0:DEVICES] = turned[0:32]
    table[:, DEVICES:] = turned[32:64]

    def table_copy(side):
        return pltpu.make_async_remote_copy(
            src_ref=table, dst_ref=tables.at[side],
            send_sem=table_send.at[side], recv_sem=table_recv.at[side],
            device_id=targets[side], device_id_type=MESH,
        )

    for side in (2, 3, 0, 1):
        @pl.when(sends[side])
        def _():
            table_copy(side).start()

    row8 = lax.broadcasted_iota(jnp.int32, (8, SLOTS), 0)

    def weights_of(asked):
        block = asked[29:30].astype(jnp.int32)
        places = (block // 64, (block // 16) % 4, block % 16)
        spread = [
            jnp.concatenate(
                [jnp.where(place == b, asked[8 * d : 8 * d + 8], 0.0) for b in range(size // 8)],
                axis=0,
            )
            for d, (place, size) in enumerate(zip(places, (CX, CY, CZ)))
        ]
        return places, spread

    def put_three(ref, at, values):
        high, low = split(values)
        ref[0:CZ, at] = high
        ref[CZ : 2 * CZ, at] = high
        ref[2 * CZ :, at] = low

    asked = table[...]
    (kx, ky, kz), (weights_x, weights_y, weights_z) = weights_of(asked)
    last = asked[24:32]
    offset = last[6:7].astype(jnp.int32)
    live = last[7:8]
    near = jnp.where(row8 < NV, last, 0.0)
    put_three(wz_rhs, slice(0, SLOTS), weights_z)
    for x in range(CX):
        plane[x * CY : (x + 1) * CY] = weights_x[x : x + 1] * weights_y
    cell = (8 * kx + offset // 64) * CY + 8 * ky + (offset // 8) % 8
    cell = jnp.where(live > 0.5, cell, -1)
    cell_z = 8 * kz + offset % 8
    places = lax.broadcasted_iota(jnp.int32, (CX * CY, SLOTS), 0)
    picked = jnp.where(places == cell, 1.0, 0.0).astype(F32).astype(BF16)
    pick[:, 0:SLOTS] = picked
    pick[:, SLOTS:] = picked
    places_z = lax.broadcasted_iota(jnp.int32, (CZ, SLOTS), 0)
    hot_z = jnp.where(places_z == cell_z, 1.0, 0.0).astype(F32).astype(BF16)
    counts = lax.dot_general(
        picked, hot_z, contract_last, preferred_element_type=F32
    )
    recip[...] = 1.0 / (1.0 + counts)

    def moved(pad, values, dim):
        size = values.shape[0]
        pad[8 : 8 + size] = values
        total = jnp.zeros_like(values)
        for j in OFFSETS:
            total = total + pad[8 - j : 8 - j + size] * tap(dim, j)
        return total

    moved_x = weights_x * CENTER + moved(pad_x, weights_x, 0)
    moved_y = moved(pad_y, weights_y, 1)
    put_three(wz_rhs, slice(SLOTS, 2 * SLOTS), moved(pad_z, weights_z, 2))
    for x in range(CX):
        plane_z[x * CY : (x + 1) * CY] = (
            moved_x[x : x + 1] * weights_y + weights_x[x : x + 1] * moved_y
        )

    def relaxed(step, near):
        def body(v, interp):
            if step == 0:
                t = jnp.dot(lhs[variable(v)], wz_rhs[:, 0:SLOTS], preferred_element_type=F32)
            else:
                add_halo(1, v)
                t = three_term(flat_res[variable(v)], wz_rhs[:, 0:SLOTS])
            here = jnp.sum(t * plane[...], axis=0, keepdims=True)
            return jnp.where(row8 == v, here, interp)

        if step == 1:
            for side in range(4):
                @pl.when(takes[side])
                def _():
                    face(1, side).wait_recv()
        interp = lax.fori_loop(0, NV, body, jnp.zeros((8, SLOTS), F32), unroll=True)
        return near + relaxation * (interp - near)

    def injected(near):
        right = []
        for v in range(NV):
            high, low = split(jnp.broadcast_to(near[v : v + 1], (16, SLOTS)))
            hot = hot_z.reshape(CZ // 16, 16, SLOTS)
            right.append(
                jnp.concatenate(
                    [
                        (hot * high[None]).reshape(CZ, SLOTS),
                        (hot * low[None]).reshape(CZ, SLOTS),
                    ],
                    axis=1,
                )
            )
        gained = lax.dot_general(
            pick[...], jnp.concatenate(right, axis=0), contract_last, preferred_element_type=F32
        )
        for v in range(NV):
            part = gained[:, v * CZ : (v + 1) * CZ]
            yield v, ((flat_res[variable(v)] + part) * recip[...]).reshape(CX, CY, CZ)

    near = relaxed(0, near)

    for v, values in injected(near):
        g1[v, 3 : 3 + CX, Y0 : Y0 + CY] = values
        pack_faces(1, v)
        high, low = split(values.reshape(CX * CY, CZ))
        lhs[variable(v), 0:CZ] = high
        lhs[variable(v), CZ : 2 * CZ] = low
        lhs[variable(v), 2 * CZ :] = high
    for side in range(4):
        @pl.when(sends[side])
        def _():
            face(1, side).start()

    def own_part(v, own):
        t = jnp.dot(lhs[variable(v)], wz_rhs[...], preferred_element_type=F32)
        both = t[:, 0:SLOTS] * plane_z[...] + t[:, SLOTS:] * plane[...]
        return jnp.where(row8 == v, jnp.sum(both, axis=0, keepdims=True), own)

    own = lax.fori_loop(0, NV, own_part, jnp.zeros((8, SLOTS), F32), unroll=True)
    parts = [near + relaxation * (own - near)]
    for side in range(4):
        if side % 2 == 0:
            for other in (side, side + 1):
                @pl.when(takes[other])
                def _():
                    table_copy(other).wait_recv()
        _, spread = weights_of(tables[side])
        put_three(near_rhs.at[side], slice(0, SLOTS), spread[2])
        dim = side // 2
        across, beside = spread[dim], spread[1 - dim]
        size = across.shape[0]
        reach = []
        for i in range(3):
            total = jnp.zeros((1, SLOTS), F32)
            for j in range(1, 4):
                if side % 2 == 0 and j > i:
                    total = total + across[size + i - j : size + i - j + 1] * tap(dim, j)
                if side % 2 == 1 and j >= 3 - i:
                    total = total + across[i - 3 + j : i - 2 + j] * tap(dim, -j)
            reach.append(total * beside)
        reach = jnp.concatenate(reach, axis=0)
        if dim == 0:
            first = 0 if side == 0 else (CX - 3) * CY
            left = jnp.concatenate(
                [lhs[v * CX * CY + first : v * CX * CY + first + 3 * CY] for v in range(NV)], axis=0
            )
            t = jnp.dot(left, near_rhs[side], preferred_element_type=F32)
        else:
            t = three_term(sy[1, 3 - side].reshape(NV * 3 * CX, CZ), near_rhs[side])
        rows = reach.shape[0]
        added = jnp.zeros((8, SLOTS), F32)
        for v in range(NV):
            here = jnp.sum(t[v * rows : (v + 1) * rows] * reach, axis=0, keepdims=True)
            added = jnp.where(row8 == v, here, added)
        parts.append(relaxation * added)

    back = jnp.concatenate(
        [part[:, half : half + DEVICES] for part in parts for half in (0, DEVICES)]
        + [jnp.zeros((DEVICES - 80, DEVICES), F32)],
        axis=0,
    )
    d1[...] = jnp.transpose(back)
    for _, (px, py) in placed:
        rows_to(d1, py * GX + px, 1, fin, me, 2, (px, py))
    fin[pl.ds(me, 1)] = d1[pl.ds(gy * GX + gx, 1)]

    interior(1)
    near = relaxed(1, near)

    for v, values in injected(near):
        flow_out[v] = values

    rows_wait(a1, DEVICES - GY, row_send.at[0])
    rows_wait(bt, DEVICES - GX, row_send.at[1])
    for side in range(4):
        @pl.when(sends[side])
        def _():
            face(0, side).wait_send()
            face(1, side).wait_send()
            table_copy(side).wait_send()

    rows_wait(d1, DEVICES - 1, row_send.at[2])
    rows_wait(fin, DEVICES - 1, row_recv.at[2])
    returned = jnp.transpose(fin[...])
    total = returned[0:16]
    for side, shift in enumerate((DEVICES - GY, GY, DEVICES - 1, 1)):
        total = total + pltpu.roll(returned[16 + 16 * side : 32 + 16 * side], shift, axis=1)
    total = jnp.concatenate([total[0:8], total[8:16]], axis=1)
    high, low = split(total)
    rest = total - high.astype(F32) - low.astype(F32)
    served = jnp.dot(
        jnp.concatenate([high.astype(F32), low.astype(F32), rest], axis=0).astype(BF16),
        ohot_low[...], preferred_element_type=F32,
    )
    near_out[...] = (served[0:8] + served[8:16] + served[16:24])[0:NV]


def hand_over(flow_vmem, near_vmem, flow_out, near_out, sems):
    copies = [
        pltpu.make_async_copy(flow_vmem, flow_out, sems.at[0]),
        pltpu.make_async_copy(near_vmem, near_out, sems.at[1]),
    ]
    for copy in copies:
        copy.start()
    for copy in copies:
        copy.wait()


def shards(flow, near, donor_owner, donor_block, recv_offset, weights):
    hbm = pl.BlockSpec(memory_space=pltpu.HBM)
    whole = pl.BlockSpec(memory_space=pltpu.VMEM)
    vmem = pltpu.VMEM
    dma = pltpu.SemaphoreType.DMA
    operands = (
        flow,
        near,
        donor_owner.reshape(1, FR),
        donor_block.reshape(1, FR),
        recv_offset.reshape(1, FR),
        weights.reshape(24, FR),
    )
    flow, near = pl.pallas_call(
        kernel,
        out_shape=(vmem((NV, CX, CY, CZ), F32), vmem((NV, FR), F32)),
        in_specs=[hbm] * 6,
        out_specs=(whole, whole),
        scratch_shapes=[
            vmem((NV, PX, PY, CZ), F32),
            vmem((NV, PX, PY, CZ), F32),
            vmem((NV * CX, CY, CZ), F32),
            vmem((STEPS, 2, NV, 3, CY, CZ), F32),
            vmem((STEPS, 2, NV, 3 * CX, CZ), F32),
            vmem((STEPS, 2, NV, 3 * CX, CZ), F32),
            vmem((NV, FR), F32),
            vmem((1, FR), jnp.int32),
            vmem((1, FR), jnp.int32),
            vmem((1, FR), jnp.int32),
            vmem((24, FR), F32),
            vmem((DEVICES, 128), F32),
            vmem((DEVICES, 128), F32),
            vmem((DEVICES, 128), F32),
            vmem((DEVICES, 128), F32),
            vmem((DEVICES, 128), F32),
            vmem((DEVICES, 128), F32),
            vmem((32, SLOTS), F32),
            vmem((4, 32, SLOTS), F32),
            vmem((2, DEVICES, FR), F32),
            vmem((2 * DEVICES, FR), BF16),
            vmem((3 * CZ, CZ), BF16),
            vmem((NV * CX * CY, 3 * CZ), BF16),
            vmem((3 * CZ, 2 * SLOTS), BF16),
            vmem((4, 3 * CZ, SLOTS), BF16),
            vmem((CX * CY, SLOTS), F32),
            vmem((CX * CY, SLOTS), F32),
            vmem((CX + 16, SLOTS), F32),
            vmem((CY + 16, SLOTS), F32),
            vmem((CZ + 16, SLOTS), F32),
            vmem((CX * CY, 2 * SLOTS), BF16),
            vmem((CX * CY, CZ), F32),
            dma((NV,)),
            dma((5,)),
            dma((STEPS, 4)),
            dma((STEPS, 4)),
            dma((3,)),
            dma((3,)),
            pltpu.SemaphoreType.REGULAR,
            dma((4,)),
            dma((4,)),
        ],
        compiler_params=pltpu.CompilerParams(
            collective_id=0, has_side_effects=True, vmem_limit_bytes=40 * 1024 * 1024
        ),
        cost_estimate=pl.CostEstimate(
            flops=2 * STEPS * 20 * NV * CX * CY * CZ,
            bytes_accessed=2 * 4 * NV * CX * CY * CZ,
            transcendentals=0,
        ),
        name="rotor_wake_steps",
    )(*[pltpu.with_memory_space_constraint(operand, pltpu.HBM) for operand in operands])
    return pl.pallas_call(
        hand_over,
        out_shape=(
            jax.ShapeDtypeStruct((NV, CX, CY, CZ), F32),
            jax.ShapeDtypeStruct((NV, FR), F32),
        ),
        in_specs=[whole, whole],
        out_specs=(hbm, hbm),
        scratch_shapes=[dma((2,))],
        name="hand_over",
    )(
        pltpu.with_memory_space_constraint(flow, pltpu.VMEM),
        pltpu.with_memory_space_constraint(near, pltpu.VMEM),
    )


def solution(mesh):
    in_specs = (
        P(None, "gx", "gy", None),
        P(None, ("gx", "gy")),
        P(("gx", "gy"), None),
        P(("gx", "gy")),
        P(("gx", "gy")),
        P(None, None, ("gx", "gy")),
    )
    out_specs = (P(None, "gx", "gy", None), P(None, ("gx", "gy")))
    return jax.shard_map(shards, mesh=mesh, in_specs=in_specs, out_specs=out_specs, check_vma=False)
```
